32 devices in a mesh: sec: 2 (over x), gx: 4 (over y, core), gy: 4 (over z).
Axes of the slice: x: 2, y: 2, z: 4, core: 2. Of those that a mesh axis runs over, the one named last changes fastest.
Arguments:
- fields: float32 [2, 5, 128, 1024], P('sec', None, 'gx', 'gy'), may hold values from -1.5 to 6, as said below
- stored_rates: bfloat16 [2, 3, 5, 128, 1024], P('sec', None, None, 'gx', 'gy'), may hold values from -6 to 6
Outputs:
- advanced: float32 [2, 5, 128, 1024], P('sec', None, 'gx', 'gy')
The draws below stay inside these ranges and needn't reach their ends.
Inputs may be any that keep to these rules, and one draw needn't show every extreme that they name: `fields`: for every level and cell: density in [0.6, 1.4], every velocity component within 0.9 in magnitude, pressure in [0.6, 1.4]; momenta are density times velocity and energy is pressure / 0.4 plus density times kinetic energy.
All inputs are finite; a program needn't handle non-finite values.
Results may differ from the reference program's by a relative error of at most 0.0005.
Values may be sent and summed in bfloat16 or wider, within the bound.
No kernel may reach another device: no remote copies, remote signals or barrier semaphores. Data moves between devices by JAX's collectives and lax.ppermute only.
A program may use at most 64 MiB of HBM per device.

```python
import jax
import jax.numpy as jnp

NZ = 32
TICKS = 3
LEVELS = 2
MEMBERS = 1
NX = 128
NY = 32


def draw_fields(key, part):
    keys = jax.random.split(jax.random.fold_in(key, 17), 3)
    shape = (MEMBERS * LEVELS, NX, NY * NZ)
    matter_per_volume = jax.random.uniform(keys[0], shape, jnp.float32, 0.7, 1.3)
    velocity = jnp.clip(0.45 * jax.random.normal(keys[1], (3,) + shape, jnp.float32), -0.9, 0.9)
    normal_stress_scalar = jax.random.uniform(keys[2], shape, jnp.float32, 0.6, 1.4)
    motion_half_square = 0.5 * (velocity[0] * velocity[0] + velocity[1] * velocity[1] + velocity[2] * velocity[2])
    energy = normal_stress_scalar / 0.4 + matter_per_volume * motion_half_square
    return jnp.stack([matter_per_volume, matter_per_volume * velocity[0], matter_per_volume * velocity[1], matter_per_volume * velocity[2], energy], axis=1)


def shard_levels(key, shape, shards, smallest, top_value):
    gain, own = 1.0, jax.random.fold_in(key, 6)
    for position, parts in shards:
        heights = jnp.exp(jax.random.uniform(jax.random.fold_in(own, position), (parts,), jnp.float32, smallest / len(shards), top_value / len(shards)))
        gain = gain * jnp.repeat(heights, shape[position] // parts).reshape([-1 if axis == position else 1 for axis in range(len(shape))])
    return gain


def scatter_about(own_key, shape, spread, reach, pieces=(), dtype=jnp.bfloat16):
    level = shard_levels(own_key, shape, pieces, -0.22, 0.18) if pieces else 1.0
    drawn = jax.random.normal(own_key, shape, jnp.float32) * spread * level
    return jnp.minimum(jnp.maximum(drawn, -reach), reach).astype(dtype)


def setup_inputs(seed: int = 0) -> dict:
    arg_keys = jax.random.split(jax.random.key(seed), 3)
    return {
        "fields": draw_fields(jax.random.fold_in(arg_keys[2], 71), 0),
        "stored_rates": scatter_about(arg_keys[1], (MEMBERS * LEVELS, 3, 5, NX, NY * NZ), 1.0, 6.0, ((0, 2), (3, 4), (4, 4))),
    }


TIME_STEP = 0.04
DYNAMIC_FRICTION = 0.4
CONDUCTIVITY = 0.5
GAMMA_LESS = 0.4
QUAD_WEIGHTS = (1.0 / 24.0, -5.0 / 24.0, 19.0 / 24.0, 9.0 / 24.0)


def shift_z(values, step, depth):
    column = jax.lax.broadcasted_iota(jnp.int32, values.shape, values.ndim - 1) % depth
    unwrapped = jnp.roll(values, -step, axis=-1)
    if step > 0:
        wrapped = jnp.roll(values, depth - step, axis=-1)
        inside = column + step < depth
    else:
        wrapped = jnp.roll(values, -step - depth, axis=-1)
        inside = column + step >= 0
    return jnp.where(inside, unwrapped, wrapped)


def rates(matter_per_volume, mom_x, mom_y, mom_z, energy, window, depth):
    vel_x = mom_x / matter_per_volume
    vel_y = mom_y / matter_per_volume
    vel_z = mom_z / matter_per_volume
    motion_half_square = 0.5 * (vel_x * vel_x + vel_y * vel_y + vel_z * vel_z)
    normal_stress_scalar = GAMMA_LESS * (energy - matter_per_volume * motion_half_square)
    gas_warmth_field = normal_stress_scalar / matter_per_volume
    enthalpy = energy + normal_stress_scalar

    def diff_x(values):
        return (window(values, 1, 0) - window(values, -1, 0)) * 0.5

    def diff_y(values):
        return (window(values, 0, 1) - window(values, 0, -1)) * 0.5

    def diff_z(values):
        center = window(values, 0, 0)
        return (shift_z(center, 1, depth) - shift_z(center, -1, depth)) * 0.5

    def middle_sweep_tier(values):
        center = window(values, 0, 0)
        along_x = window(values, 2, 0) - 2.0 * center + window(values, -2, 0)
        along_y = window(values, 0, 2) - 2.0 * center + window(values, 0, -2)
        along_z = shift_z(center, 2, depth) - 2.0 * center + shift_z(center, -2, depth)
        return (along_x + along_y + along_z) * 0.25

    mass = -(diff_x(mom_x) + diff_y(mom_y) + diff_z(mom_z))
    flow_x = -(diff_x(mom_x * vel_x + normal_stress_scalar) + diff_y(mom_x * vel_y) + diff_z(mom_x * vel_z)) + DYNAMIC_FRICTION * middle_sweep_tier(vel_x)
    flow_y = -(diff_x(mom_y * vel_x) + diff_y(mom_y * vel_y + normal_stress_scalar) + diff_z(mom_y * vel_z)) + DYNAMIC_FRICTION * middle_sweep_tier(vel_y)
    flow_z = -(diff_x(mom_z * vel_x) + diff_y(mom_z * vel_y) + diff_z(mom_z * vel_z + normal_stress_scalar)) + DYNAMIC_FRICTION * middle_sweep_tier(vel_z)
    conducted_warmth_current = -(diff_x(enthalpy * vel_x) + diff_y(enthalpy * vel_y) + diff_z(enthalpy * vel_z))
    conducted_warmth_current = conducted_warmth_current + DYNAMIC_FRICTION * middle_sweep_tier(motion_half_square) + CONDUCTIVITY * middle_sweep_tier(gas_warmth_field)
    return jnp.stack([mass, flow_x, flow_y, flow_z, conducted_warmth_current])


def level_rates(level_state):
    def window(values, across, along):
        return jnp.roll(values, (-across, -along * NZ), (0, 1))

    return rates(level_state[0], level_state[1], level_state[2], level_state[3], level_state[4], window, NZ)


def advance_member(member_fields, member_stored):
    levels = member_fields.shape[0]
    current = member_fields
    stored = member_stored
    first_level = (jnp.arange(levels) == 0)[:, None, None, None]
    for tick_count in range(TICKS):
        own_rates = jnp.stack([level_rates(current[level]) for level in range(levels)])
        lower = own_rates[:-1].astype(jnp.bfloat16)
        fresh_rates = jnp.concatenate([jnp.zeros_like(lower[:1]), lower], axis=0)
        quadrature = (QUAD_WEIGHTS[0] * stored[:, 0].astype(jnp.float32)
                      + QUAD_WEIGHTS[1] * stored[:, 1].astype(jnp.float32)
                      + QUAD_WEIGHTS[2] * stored[:, 2].astype(jnp.float32)
                      + QUAD_WEIGHTS[3] * fresh_rates.astype(jnp.float32))
        correction = quadrature - stored[:, 2].astype(jnp.float32)
        current = current + TIME_STEP * (own_rates + jnp.where(first_level, jnp.float32(0.0), correction))
        stored = jnp.concatenate([stored[:, 1:], fresh_rates[:, None]], axis=1)
    return current


def reference(fields, stored_rates):
    results = []
    for member in range(MEMBERS):
        start = member * LEVELS
        results.append(advance_member(fields[start:start + LEVELS], stored_rates[start:start + LEVELS]))
    return jnp.concatenate(results, axis=0)
```

```python
import functools

import jax
import jax.numpy as jnp
import numpy as np
from jax import lax
from jax.experimental import pallas as pl
from jax.experimental.pallas import tpu as pltpu
from jax.sharding import PartitionSpec as P

NZ = 32
TICKS = 3


TIME_STEP = 0.04
DYNAMIC_FRICTION = 0.4
CONDUCTIVITY = 0.5
GAMMA_LESS = 0.4
QUAD_WEIGHTS = (1.0 / 24.0, -5.0 / 24.0, 19.0 / 24.0, 9.0 / 24.0)

LANES = 128
EDGE = 8
FIELDS = 5


def neighbours(axis, even, low_edge, high_edge):
    count = lax.axis_size(axis)
    if count % 2:
        from_next = lax.ppermute(low_edge, axis, [(i, (i - 1) % count) for i in range(count)])
        from_last = lax.ppermute(high_edge, axis, [(i, (i + 1) % count) for i in range(count)])
        return from_next, from_last
    if low_edge is high_edge:
        outward = inward = low_edge
    else:
        outward = jnp.where(even, high_edge, low_edge)
        inward = jnp.where(even, low_edge, high_edge)
    far = [(i, (i + 1) % count if i % 2 else (i - 1) % count) for i in range(count)]
    near = [(i, i + 1 if i % 2 == 0 else i - 1) for i in range(count)]
    second = lax.ppermute(inward, axis, far)
    first = lax.ppermute(outward, axis, near)
    return first, second


def from_lower(block, levels, distance):
    count = lax.axis_size("sec")
    route = []
    for start in range(0, count, levels):
        route += [(start + i, start + (i + distance) % levels) for i in range(levels)]
    return lax.ppermute(block, "sec", route)


def stencil_matrix():
    per_tile = LANES // NZ
    out = 2 * LANES
    d_y = np.zeros((4 * LANES, out), np.float32)
    d_z = np.zeros((out, out), np.float32)
    sweep = np.zeros((4 * LANES, out), np.float32)
    for y in range(2 * per_tile):
        for z in range(NZ):
            column = y * NZ + z
            here = (y + per_tile) * NZ + z
            d_y[here + NZ, column] += 0.5
            d_y[here - NZ, column] -= 0.5
            d_z[y * NZ + (z + 1) % NZ, column] += 0.5
            d_z[y * NZ + (z - 1) % NZ, column] -= 0.5
            sweep[here, column] -= 1.0
            sweep[here + 2 * NZ, column] += 0.25
            sweep[here - 2 * NZ, column] += 0.25
            base = (y + per_tile) * NZ
            sweep[base + (z + 2) % NZ, column] += 0.25
            sweep[base + (z - 2) % NZ, column] += 0.25
    return np.concatenate([d_y, d_z, sweep], axis=0)


def advance_kernel(chain, corrected, rows, *refs):
    flags = refs[0]
    matrix = refs[1]
    refs = list(refs[2:])
    even_x = flags[0] == 1
    even_y = flags[1] == 1
    position = flags[2]
    inputs = []
    for link in range(chain):
        state = refs[:5]
        refs = refs[5:]
        extra = None
        if corrected[link]:
            extra = refs[:5]
            refs = refs[5:]
        inputs.append((state, extra))
    out, state_s, term_s, fresh_s, flow_x, slow, flow_y, flow_z, slow_yz = refs
    high = rows + 2 * EDGE

    def lanes(tile):
        return pl.ds(tile * LANES, LANES)

    for link in range(chain):
        (center, y_first, y_second, x_first, x_second), extra = inputs[link]
        for field in range(FIELDS):
            for tile in range(6):
                if tile in (2, 3):
                    middle = center[field, :, lanes(tile - 2)].astype(jnp.float32)
                else:
                    one = y_first[field, :, lanes(tile % 2)].astype(jnp.float32)
                    two = y_second[field, :, lanes(tile % 2)].astype(jnp.float32)
                    middle = jnp.where(even_y, two, one) if tile < 2 else jnp.where(even_y, one, two)
                one = x_first[field, :, lanes(tile)]
                two = x_second[field, :, lanes(tile)]
                state_s[link, field, tile, pl.ds(EDGE, rows), :] = middle
                state_s[link, field, tile, pl.ds(0, EDGE), :] = jnp.where(even_x, two, one)
                state_s[link, field, tile, pl.ds(EDGE + rows, EDGE), :] = jnp.where(even_x, one, two)
        if extra is not None:
            stored, y_first, y_second, x_first, x_second = extra
            for field in range(FIELDS):
                for tile in (2, 3):
                    old = [stored[age, field, :, lanes(tile - 2)].astype(jnp.float32) for age in range(3)]
                    terms = kept_terms(old)
                    for tick in range(TICKS):
                        term_s[link, tick, field, tile - 1, pl.ds(EDGE, rows), :] = terms[tick]
                for tick in range(2):
                    plane = tick * FIELDS + field
                    one = y_first[plane].astype(jnp.float32)
                    two = y_second[plane].astype(jnp.float32)
                    term_s[link, tick, field, 0, pl.ds(EDGE, rows), :] = jnp.where(even_y, two, one)
                    term_s[link, tick, field, 3, pl.ds(EDGE, rows), :] = jnp.where(even_y, one, two)
                    for tile in range(4):
                        one = x_first[plane, :, lanes(tile)]
                        two = x_second[plane, :, lanes(tile)]
                        term_s[link, tick, field, tile, pl.ds(0, EDGE), :] = jnp.where(even_x, two, one)
                        term_s[link, tick, field, tile, pl.ds(EDGE + rows, EDGE), :] = jnp.where(
                            even_x, one, two
                        )

    def pointwise(link, tile):
        density, mom_x, mom_y, mom_z, energy = [state_s[link, field, tile] for field in range(FIELDS)]
        inverse = 1.0 / density
        vel_x = mom_x * inverse
        vel_y = mom_y * inverse
        vel_z = mom_z * inverse
        kinetic = 0.5 * (vel_x * vel_x + vel_y * vel_y + vel_z * vel_z)
        pressure = GAMMA_LESS * (energy - density * kinetic)
        enthalpy = energy + pressure
        heat = DYNAMIC_FRICTION * kinetic + CONDUCTIVITY * (pressure * inverse)
        xy = mom_x * vel_y
        xz = mom_x * vel_z
        yz = mom_y * vel_z
        along_x = (mom_x, mom_x * vel_x + pressure, xy, xz, enthalpy * vel_x)
        along_y = (mom_y, xy, mom_y * vel_y + pressure, yz, enthalpy * vel_y)
        along_z = (mom_z, xz, yz, mom_z * vel_z + pressure, enthalpy * vel_z)
        spread = (
            DYNAMIC_FRICTION * vel_x,
            DYNAMIC_FRICTION * vel_y,
            DYNAMIC_FRICTION * vel_z,
            heat,
        )
        for field in range(FIELDS):
            flow_y[pl.ds(field * high, high), lanes(tile)] = (-along_y[field]).astype(jnp.bfloat16)
            if 1 <= tile <= 4:
                flow_z[pl.ds(field * high, high), lanes(tile - 1)] = (-along_z[field]).astype(jnp.bfloat16)
                flow_x[field, tile - 1, pl.ds(EDGE, high), :] = along_x[field]
            if field:
                slow_yz[pl.ds(field * high, high), lanes(tile)] = spread[field - 1].astype(jnp.bfloat16)
                if 1 <= tile <= 4:
                    slow[field - 1, tile - 1, pl.ds(EDGE, high), :] = spread[field - 1]

    slow_yz[pl.ds(0, high), :] = jnp.zeros((high, 6 * LANES), jnp.bfloat16)

    def rates(link, tick):
        for tile in range(6) if tick == 0 else range(1, 5):
            pointwise(link, tile)
        groups = ((1, 2), (3, 4)) if tick < TICKS - 1 else ((2, 3),)
        found = [{} for _ in range(FIELDS)]
        for group in groups:
            around = pl.ds((group[0] - 1) * LANES, 4 * LANES)
            inner = pl.ds((group[0] - 1) * LANES, 2 * LANES)
            left = jnp.concatenate([flow_y[:, around], flow_z[:, inner], slow_yz[:, around]], axis=1)
            product = jnp.dot(left, matrix[...], preferred_element_type=jnp.float32)
            for field in range(FIELDS):
                for place, tile in enumerate(group):
                    total = product[field * high : (field + 1) * high, place * LANES : (place + 1) * LANES]

                    def shifted(ref, index, step):
                        return ref[index, tile - 1, pl.ds(EDGE + step, high), :]

                    total = total - 0.5 * (shifted(flow_x, field, 1) - shifted(flow_x, field, -1))
                    if field:
                        total = total + (
                            0.25 * (shifted(slow, field - 1, 2) + shifted(slow, field - 1, -2))
                            - 0.5 * shifted(slow, field - 1, 0)
                        )
                    found[field][tile] = total
        return found

    for tick in range(TICKS):
        for link in reversed(range(chain)):
            if link > TICKS - tick:
                continue
            found = rates(link, tick)
            last = tick == TICKS - 1
            for field in range(FIELDS):
                for tile, rate in found[field].items():
                    if link:
                        fresh_s[link - 1, tick, field, tile - 1] = rate.astype(jnp.bfloat16).astype(jnp.float32)
                    if link + tick >= TICKS:
                        continue
                    step = rate
                    if corrected[link]:
                        extra = term_s[link, tick, field, tile - 1] + QUAD_WEIGHTS[3] * fresh_s[
                            link, tick, field, tile - 1
                        ]
                        for age in range(tick):
                            weight = QUAD_WEIGHTS[3 - tick + age] - (1.0 if age == tick - 1 else 0.0)
                            extra = extra + weight * fresh_s[link, age, field, tile - 1]
                        step = rate + jnp.where(position > link, extra, 0.0)
                    state = state_s[link, field, tile] + TIME_STEP * step
                    if last:
                        out[field, :, lanes(tile - 2)] = state[EDGE : EDGE + rows]
                    else:
                        state_s[link, field, tile] = state


def kept_terms(old):
    first, second, third, _ = QUAD_WEIGHTS
    return (
        first * old[0] + second * old[1] + (third - 1.0) * old[2],
        first * old[1] + second * old[2],
        first * old[2],
    )


def per_device(fields, stored_rates):
    levels = min(4, lax.axis_size("sec"))
    position = lax.axis_index("sec") % levels
    even_x = lax.axis_index("gx") % 2 == 0 if lax.axis_size("gx") % 2 == 0 else jnp.bool_(True)
    even_y = lax.axis_index("gy") % 2 == 0 if lax.axis_size("gy") % 2 == 0 else jnp.bool_(True)
    block = fields[0]
    stored = stored_rates[0]
    rows, columns = block.shape[1:]
    chain = min(levels, TICKS + 1)
    corrected = [link < levels - 1 and link < TICKS for link in range(chain)]
    sent = block.astype(jnp.bfloat16)

    def ordered_y(pair):
        first, second = pair
        return jnp.where(even_y, second, first), jnp.where(even_y, first, second)

    def edges_x(padded):
        return padded[:, :EDGE], padded[:, -EDGE:]

    own_y = neighbours("gy", even_y, sent, sent)
    centers = [sent] + [from_lower(sent, levels, link) for link in range(1, chain)]
    old = stored.astype(jnp.float32)
    kept = jnp.concatenate(kept_terms(old)[:2], axis=0).astype(jnp.bfloat16)
    kept_y = neighbours("gy", even_y, kept[:, :, :LANES], kept[:, :, -LANES:])
    low, top = ordered_y(own_y)
    padded = jnp.concatenate([low, sent, top], axis=2)
    own_x = neighbours("gx", even_x, *edges_x(padded))
    both = jnp.concatenate(own_y, axis=0)
    low, top = ordered_y(kept_y)
    kept_padded = jnp.concatenate([low, kept, top], axis=2)

    states = [(block, *own_y, *own_x)]
    extras = [None] * chain
    late = []
    for link in range(chain):
        if link:
            arrived = from_lower(both, levels, link)
            link_y = (arrived[:FIELDS], arrived[FIELDS:])
            low, top = ordered_y(link_y)
            late.append(jnp.concatenate([low, centers[link], top], axis=2))
            states.append((centers[link], *link_y))
        if corrected[link]:
            if link:
                link_stored = from_lower(stored, levels, link)
                link_y = tuple(from_lower(half, levels, link) for half in kept_y)
                link_padded = from_lower(kept_padded, levels, link)
            else:
                link_stored, link_y, link_padded = stored, kept_y, kept_padded
            extras[link] = (link_stored, *link_y)
            late += [link_padded[:FIELDS], link_padded[FIELDS:]]
    late_x = neighbours("gx", even_x, *edges_x(jnp.concatenate(late, axis=2)))

    operands = []
    start = 0
    for link in range(chain):
        if link:
            width = columns + 4 * LANES
            operands += [*states[link], *(half[:, :, start : start + width] for half in late_x)]
            start += width
        else:
            operands += states[0]
        if corrected[link]:
            width = columns + 2 * LANES
            operands += extras[link]
            operands += [
                jnp.concatenate(
                    [half[:, :, start : start + width], half[:, :, start + width : start + 2 * width]], axis=0
                )
                for half in late_x
            ]
            start += 2 * width
    operands = [
        part.astype(jnp.float32) if part.ndim == 3 and part.shape[1] == EDGE else part for part in operands
    ]
    flags = jnp.stack([even_x.astype(jnp.int32), even_y.astype(jnp.int32), position])
    matrix = jnp.asarray(stencil_matrix(), jnp.bfloat16)
    high = rows + 2 * EDGE
    tall = high + 2 * EDGE
    vmem = pl.BlockSpec(memory_space=pltpu.VMEM)
    result = pl.pallas_call(
        functools.partial(advance_kernel, chain, corrected, rows),
        out_shape=jax.ShapeDtypeStruct((FIELDS, rows, columns), jnp.float32),
        in_specs=[pl.BlockSpec(memory_space=pltpu.SMEM)] + [vmem] * (len(operands) + 1),
        out_specs=vmem,
        scratch_shapes=[
            pltpu.VMEM((chain, FIELDS, 6, high, LANES), jnp.float32),
            pltpu.VMEM((chain, TICKS, FIELDS, 4, high, LANES), jnp.float32),
            pltpu.VMEM((chain, TICKS, FIELDS, 4, high, LANES), jnp.float32),
            pltpu.VMEM((FIELDS, 4, tall, LANES), jnp.float32),
            pltpu.VMEM((FIELDS - 1, 4, tall, LANES), jnp.float32),
            pltpu.VMEM((FIELDS * high, 6 * LANES), jnp.bfloat16),
            pltpu.VMEM((FIELDS * high, 4 * LANES), jnp.bfloat16),
            pltpu.VMEM((FIELDS * high, 6 * LANES), jnp.bfloat16),
        ],
        compiler_params=pltpu.CompilerParams(vmem_limit_bytes=48 * 1024 * 1024),
    )(flags, matrix, *operands)
    return result[None]


def solution(mesh):
    return jax.shard_map(
        per_device,
        mesh=mesh,
        in_specs=(P("sec", None, "gx", "gy"), P("sec", None, None, "gx", "gy")),
        out_specs=P("sec", None, "gx", "gy"),
        check_vma=False,
    )
```

```python
import functools

import jax
import jax.numpy as jnp
import numpy as np
from jax import lax
from jax.experimental import pallas as pl
from jax.experimental.pallas import tpu as pltpu
from jax.sharding import PartitionSpec as P

NZ = 32
TICKS = 3


TIME_STEP = 0.04
DYNAMIC_FRICTION = 0.4
CONDUCTIVITY = 0.5
GAMMA_LESS = 0.4
QUAD_WEIGHTS = (1.0 / 24.0, -5.0 / 24.0, 19.0 / 24.0, 9.0 / 24.0)

LANES = 128
EDGE = 8
FIELDS = 5


def neighbours(axis, even, low_edge, high_edge):
    count = lax.axis_size(axis)
    if count % 2:
        from_next = lax.ppermute(low_edge, axis, [(i, (i - 1) % count) for i in range(count)])
        from_last = lax.ppermute(high_edge, axis, [(i, (i + 1) % count) for i in range(count)])
        return from_next, from_last
    if low_edge is high_edge:
        outward = inward = low_edge
    else:
        outward = jnp.where(even, high_edge, low_edge)
        inward = jnp.where(even, low_edge, high_edge)
    far = [(i, (i + 1) % count if i % 2 else (i - 1) % count) for i in range(count)]
    near = [(i, i + 1 if i % 2 == 0 else i - 1) for i in range(count)]
    second = lax.ppermute(inward, axis, far)
    first = lax.ppermute(outward, axis, near)
    return first, second


def from_lower(block, levels, distance):
    count = lax.axis_size("sec")
    route = []
    for start in range(0, count, levels):
        route += [(start + i, start + (i + distance) % levels) for i in range(levels)]
    return lax.ppermute(block, "sec", route)


def stencil_matrix():
    per_tile = LANES // NZ
    out = 2 * LANES
    d_y = np.zeros((4 * LANES, out), np.float32)
    d_z = np.zeros((out, out), np.float32)
    sweep = np.zeros((4 * LANES, out), np.float32)
    for y in range(2 * per_tile):
        for z in range(NZ):
            column = y * NZ + z
            here = (y + per_tile) * NZ + z
            d_y[here + NZ, column] -= 0.5
            d_y[here - NZ, column] += 0.5
            d_z[y * NZ + (z + 1) % NZ, column] -= 0.5
            d_z[y * NZ + (z - 1) % NZ, column] += 0.5
            sweep[here, column] -= 1.0
            sweep[here + 2 * NZ, column] += 0.25
            sweep[here - 2 * NZ, column] += 0.25
            base = (y + per_tile) * NZ
            sweep[base + (z + 2) % NZ, column] += 0.25
            sweep[base + (z - 2) % NZ, column] += 0.25
    return np.concatenate([d_y, d_z, sweep], axis=0)


def advance_kernel(chain, corrected, rows, *refs):
    flags, matrix, x_first, x_second = refs[:4]
    refs = list(refs[4:])
    even_x = flags[0] == 1
    even_y = flags[1] == 1
    position = flags[2]
    inputs = []
    for link in range(chain):
        state, refs = refs[:3], refs[3:]
        extra = None
        if corrected[link]:
            extra, refs = refs[:3], refs[3:]
        inputs.append((state, extra))
    out, own, state_s, term_s, fresh_s, flow_x, slow, flow_y, flow_z, slow_yz, edges, arrival = refs
    high = rows + 2 * EDGE
    block = FIELDS * high
    load_own = pltpu.make_async_copy(inputs[0][0][0], own, arrival)
    load_own.start()

    def lanes(tile):
        return pl.ds(tile * LANES, LANES)

    taken = x_first.shape[1]
    for field in range(FIELDS):
        for tile in range(4):
            one = x_first[field, :, lanes(tile)]
            two = x_second[field, :, lanes(tile)]
            edges[0, field, tile, pl.ds(0, taken), :] = jnp.where(even_x, two, one)
            edges[1, field, tile, pl.ds(0, taken), :] = jnp.where(even_x, one, two)
    sources, _ = edge_layout(chain, corrected)

    def place(target, index, kind):
        for distance, count, tiles, row, first_tile in sources[kind]:
            for tile in range(tiles):
                start = (4 - tiles) // 2 + tile
                low = edges[0, index[-1], first_tile + tile, pl.ds(row, count), :]
                top = edges[1, index[-1], first_tile + tile, pl.ds(row, count), :]
                target(start)[pl.ds(EDGE - distance - count, count), :] = low
                target(start)[pl.ds(EDGE + rows + distance, count), :] = top

    for link in reversed(range(chain)):
        (center, y_first, y_second), extra = inputs[link]
        if link == 0:
            load_own.wait()
            center = own
        for field in range(FIELDS):
            rest = jnp.full((EDGE, LANES), (1.0, 0.0, 0.0, 0.0, 2.5)[field], jnp.float32)
            for tile in range(6):
                if tile in (2, 3):
                    middle = center[field, :, lanes(tile - 2)].astype(jnp.float32)
                else:
                    one = y_first[field, :, lanes(tile % 2)].astype(jnp.float32)
                    two = y_second[field, :, lanes(tile % 2)].astype(jnp.float32)
                    middle = jnp.where(even_y, two, one) if tile < 2 else jnp.where(even_y, one, two)
                state_s[link, field, tile, pl.ds(EDGE, rows), :] = middle
                state_s[link, field, tile, pl.ds(0, EDGE), :] = rest
                state_s[link, field, tile, pl.ds(EDGE + rows, EDGE), :] = rest
            place(lambda tile: state_s.at[link, field, tile + 1], (field,), ("state", link))
        if extra is not None:
            stored, y_first, y_second = extra
            none = jnp.zeros((EDGE, LANES), jnp.float32)
            for field in range(FIELDS):
                for tile in (2, 3):
                    old = [stored[age, field, :, lanes(tile - 2)].astype(jnp.float32) for age in range(3)]
                    terms = kept_terms(old)
                    for tick in range(TICKS):
                        term_s[link, tick, field, tile - 1, pl.ds(EDGE, rows), :] = terms[tick]
                for tick in range(2):
                    plane = tick * FIELDS + field
                    one = y_first[plane].astype(jnp.float32)
                    two = y_second[plane].astype(jnp.float32)
                    term_s[link, tick, field, 0, pl.ds(EDGE, rows), :] = jnp.where(even_y, two, one)
                    term_s[link, tick, field, 3, pl.ds(EDGE, rows), :] = jnp.where(even_y, one, two)
                    for tile in range(4):
                        term_s[link, tick, field, tile, pl.ds(0, EDGE), :] = none
                        term_s[link, tick, field, tile, pl.ds(EDGE + rows, EDGE), :] = none
                    place(lambda tile: term_s.at[link, tick, field, tile], (field,), ("kept", link, tick))

    def pointwise(link, tile):
        density, mom_x, mom_y, mom_z, energy = [state_s[link, field, tile] for field in range(FIELDS)]
        inverse = 1.0 / density
        vel_x = mom_x * inverse
        vel_y = mom_y * inverse
        vel_z = mom_z * inverse
        kinetic = 0.5 * (vel_x * vel_x + vel_y * vel_y + vel_z * vel_z)
        pressure = GAMMA_LESS * (energy - density * kinetic)
        enthalpy = energy + pressure
        heat = DYNAMIC_FRICTION * kinetic + CONDUCTIVITY * (pressure * inverse)
        xy = mom_x * vel_y
        xz = mom_x * vel_z
        yz = mom_y * vel_z
        along_x = (mom_x, mom_x * vel_x + pressure, xy, xz, enthalpy * vel_x)
        along_y = (mom_y, xy, mom_y * vel_y + pressure, yz, enthalpy * vel_y)
        along_z = (mom_z, xz, yz, mom_z * vel_z + pressure, enthalpy * vel_z)
        spread = (
            DYNAMIC_FRICTION * vel_x,
            DYNAMIC_FRICTION * vel_y,
            DYNAMIC_FRICTION * vel_z,
            heat,
        )
        for field in range(FIELDS):
            place = pl.ds(link * block + field * high, high)
            flow_y[place, lanes(tile)] = along_y[field].astype(jnp.bfloat16)
            if 1 <= tile <= 4:
                flow_z[place, lanes(tile - 1)] = along_z[field].astype(jnp.bfloat16)
                flow_x[link, field, tile - 1, pl.ds(EDGE, high), :] = along_x[field]
            if field:
                slow_yz[place, lanes(tile)] = spread[field - 1].astype(jnp.bfloat16)
                if 1 <= tile <= 4:
                    slow[link, field - 1, tile - 1, pl.ds(EDGE, high), :] = spread[field - 1]

    for link in range(chain):
        slow_yz[pl.ds(link * block, high), :] = jnp.zeros((high, 6 * LANES), jnp.bfloat16)

    def along_x(link, field, tile):
        def shifted(ref, index, step):
            return ref[link, index, tile - 1, pl.ds(EDGE + step, high), :]

        total = 0.5 * (shifted(flow_x, field, -1) - shifted(flow_x, field, 1))
        if field:
            total = total + (
                0.25 * (shifted(slow, field - 1, 2) + shifted(slow, field - 1, -2))
                - 0.5 * shifted(slow, field - 1, 0)
            )
        return total

    for tick in range(TICKS):
        last = tick == TICKS - 1
        active = min(chain, TICKS - tick + 1)
        for link in reversed(range(active)):
            for tile in range(6) if tick == 0 else range(1, 5):
                pointwise(link, tile)
        tall = pl.ds(0, active * block)
        for group in ((2, 3),) if last else ((1, 2), (3, 4)):
            around = pl.ds((group[0] - 1) * LANES, 4 * LANES)
            inner = pl.ds((group[0] - 1) * LANES, 2 * LANES)
            left = jnp.concatenate([flow_y[tall, around], flow_z[tall, inner], slow_yz[tall, around]], axis=1)
            product = jnp.dot(left, matrix[...], preferred_element_type=jnp.float32)
            for link in reversed(range(active)):
                for field in range(FIELDS):
                    for side, tile in enumerate(group):
                        start = link * block + field * high
                        rate = product[start : start + high, side * LANES : (side + 1) * LANES]
                        rate = rate + along_x(link, field, tile)
                        if link:
                            fresh_s[link - 1, tick, field, tile - 1] = rate.astype(jnp.bfloat16).astype(
                                jnp.float32
                            )
                        if link + tick >= TICKS:
                            continue
                        step = rate
                        if corrected[link]:
                            extra = term_s[link, tick, field, tile - 1] + QUAD_WEIGHTS[3] * fresh_s[
                                link, tick, field, tile - 1
                            ]
                            for age in range(tick):
                                weight = QUAD_WEIGHTS[3 - tick + age] - (1.0 if age == tick - 1 else 0.0)
                                extra = extra + weight * fresh_s[link, age, field, tile - 1]
                            step = rate + jnp.where(position > link, extra, 0.0)
                        state = state_s[link, field, tile] + TIME_STEP * step
                        if not last:
                            state_s[link, field, tile] = state
                        elif link == 0:
                            out[field, :, lanes(tile - 2)] = state[EDGE : EDGE + rows]


def edge_layout(chain, corrected):
    sources = {}
    wide = []
    narrow = []
    for link in range(chain):
        wide.append((("state", link), 0, 4))
        narrow.append((("state", link), 4))
        if corrected[link]:
            wide.append((("kept", link, 0), 0, 2))
            narrow.append((("kept", link, 0), 2))
            narrow.append((("kept", link, 1), 0))
    row = 0
    for kind, distance, count in wide:
        sources.setdefault(kind, []).append((distance, count, 4, row, 0))
        row += count
    for place, (kind, distance) in enumerate(narrow):
        sources.setdefault(kind, []).append((distance, 2, 2, row + 2 * (place // 2), 2 * (place % 2)))
    return sources, row + 2 * ((len(narrow) + 1) // 2)


def kept_terms(old):
    first, second, third, _ = QUAD_WEIGHTS
    return (
        first * old[0] + second * old[1] + (third - 1.0) * old[2],
        first * old[1] + second * old[2],
        first * old[2],
    )


def per_device(fields, stored_rates):
    levels = min(4, lax.axis_size("sec"))
    position = lax.axis_index("sec") % levels
    even_x = lax.axis_index("gx") % 2 == 0 if lax.axis_size("gx") % 2 == 0 else jnp.bool_(True)
    even_y = lax.axis_index("gy") % 2 == 0 if lax.axis_size("gy") % 2 == 0 else jnp.bool_(True)
    block = fields[0]
    stored = stored_rates[0]
    rows, columns = block.shape[1:]
    chain = min(levels, TICKS + 1)
    corrected = [link < levels - 1 and link < TICKS for link in range(chain)]
    sent = block.astype(jnp.bfloat16)

    def padded_y(pair, center):
        first, second = pair
        low, top = jnp.where(even_y, second, first), jnp.where(even_y, first, second)
        return jnp.concatenate([low[:, :, -LANES:], center, top[:, :, :LANES]], axis=2)

    own_y = neighbours("gy", even_y, sent, sent)
    centers = [sent] + [from_lower(sent, levels, link) for link in range(1, chain)]
    kept = jnp.concatenate(kept_terms(stored.astype(jnp.float32))[:2], axis=0).astype(jnp.bfloat16)
    kept_y = neighbours("gy", even_y, kept[:, :, :LANES], kept[:, :, -LANES:])
    both = jnp.concatenate(own_y, axis=0)
    forwarded = [from_lower(both, levels, link) for link in range(1, chain)]
    kept_y, forwarded = lax.optimization_barrier((kept_y, forwarded))

    padded = {}
    operands = []
    for link in range(chain):
        if link:
            link_y = (forwarded[link - 1][:FIELDS], forwarded[link - 1][FIELDS:])
            operands += [centers[link], *link_y]
        else:
            link_y = own_y
            operands += [block, *own_y]
        padded["state", link] = padded_y(link_y, centers[link])
        if corrected[link]:
            if link:
                link_kept = from_lower(kept, levels, link)
                link_y = tuple(from_lower(half, levels, link) for half in kept_y)
                operands += [from_lower(stored, levels, link), *link_y]
            else:
                link_kept, link_y = kept, kept_y
                operands += [stored, *link_y]
            link_padded = padded_y(link_y, link_kept)
            padded["kept", link, 0] = link_padded[:FIELDS]
            padded["kept", link, 1] = link_padded[FIELDS:]

    sources, taken = edge_layout(chain, corrected)
    width = columns + 2 * LANES

    def edge(from_top):
        grid = {}
        for kind, pieces in sources.items():
            for distance, count, tiles, row, first_tile in pieces:
                start = rows - distance - count if from_top else distance
                skip = (4 - tiles) // 2 * LANES
                grid[row, first_tile] = padded[kind][:, start : start + count, skip : width - skip]
        parts = []
        for row, first_tile in sorted(grid):
            if first_tile:
                continue
            part = grid[row, 0]
            if part.shape[2] < width:
                part = jnp.concatenate([part, grid.get((row, 2), part)], axis=2)
            parts.append(part)
        return jnp.concatenate(parts, axis=1)

    over_x = neighbours("gx", even_x, edge(False), edge(True))
    operands = [half.astype(jnp.float32) for half in over_x] + operands
    flags = jnp.stack([even_x.astype(jnp.int32), even_y.astype(jnp.int32), position])
    matrix = jnp.asarray(stencil_matrix(), jnp.bfloat16)
    high = rows + 2 * EDGE
    tall = high + 2 * EDGE
    vmem = pl.BlockSpec(memory_space=pltpu.VMEM)
    specs = [vmem] * (len(operands) + 1)
    specs[3] = pl.BlockSpec(memory_space=pl.ANY)
    result = pl.pallas_call(
        functools.partial(advance_kernel, chain, corrected, rows),
        out_shape=jax.ShapeDtypeStruct((FIELDS, rows, columns), jnp.float32),
        in_specs=[pl.BlockSpec(memory_space=pltpu.SMEM)] + specs,
        out_specs=vmem,
        scratch_shapes=[
            pltpu.VMEM((FIELDS, rows, columns), jnp.float32),
            pltpu.VMEM((chain, FIELDS, 6, high, LANES), jnp.float32),
            pltpu.VMEM((chain, TICKS, FIELDS, 4, high, LANES), jnp.float32),
            pltpu.VMEM((chain, TICKS, FIELDS, 4, high, LANES), jnp.float32),
            pltpu.VMEM((chain, FIELDS, 4, tall, LANES), jnp.float32),
            pltpu.VMEM((chain, FIELDS - 1, 4, tall, LANES), jnp.float32),
            pltpu.VMEM((chain * FIELDS * high, 6 * LANES), jnp.bfloat16),
            pltpu.VMEM((chain * FIELDS * high, 4 * LANES), jnp.bfloat16),
            pltpu.VMEM((chain * FIELDS * high, 6 * LANES), jnp.bfloat16),
            pltpu.VMEM((2, FIELDS, 4, -(-taken // 8) * 8, LANES), jnp.float32),
            pltpu.SemaphoreType.DMA(()),
        ],
        compiler_params=pltpu.CompilerParams(vmem_limit_bytes=48 * 1024 * 1024),
    )(flags, matrix, *operands)
    return result[None]


def solution(mesh):
    return jax.shard_map(
        per_device,
        mesh=mesh,
        in_specs=(P("sec", None, "gx", "gy"), P("sec", None, None, "gx", "gy")),
        out_specs=P("sec", None, "gx", "gy"),
        check_vma=False,
    )
```

```python
import functools

import jax
import jax.numpy as jnp
import numpy as np
from jax import lax
from jax.experimental import pallas as pl
from jax.experimental.pallas import tpu as pltpu
from jax.sharding import PartitionSpec as P

NZ = 32
TICKS = 3


TIME_STEP = 0.04
DYNAMIC_FRICTION = 0.4
CONDUCTIVITY = 0.5
GAMMA_LESS = 0.4
QUAD_WEIGHTS = (1.0 / 24.0, -5.0 / 24.0, 19.0 / 24.0, 9.0 / 24.0)

LANES = 128
FIRST = 12
START = 8
WINDOW = 2 * (FIRST - START)
FIELDS = 5


def neighbours(axis, even, low_edge, high_edge):
    count = lax.axis_size(axis)
    if count % 2:
        from_next = lax.ppermute(low_edge, axis, [(i, (i - 1) % count) for i in range(count)])
        from_last = lax.ppermute(high_edge, axis, [(i, (i + 1) % count) for i in range(count)])
        return from_next, from_last
    if low_edge is high_edge:
        outward = inward = low_edge
    else:
        outward = jnp.where(even, high_edge, low_edge)
        inward = jnp.where(even, low_edge, high_edge)
    far = [(i, (i + 1) % count if i % 2 else (i - 1) % count) for i in range(count)]
    near = [(i, i + 1 if i % 2 == 0 else i - 1) for i in range(count)]
    second = lax.ppermute(inward, axis, far)
    first = lax.ppermute(outward, axis, near)
    return first, second


def from_lower(block, levels, distance):
    count = lax.axis_size("sec")
    route = []
    for start in range(0, count, levels):
        route += [(start + i, start + (i + distance) % levels) for i in range(levels)]
    return lax.ppermute(block, "sec", route)


def stencil_matrix():
    per_tile = LANES // NZ
    wide = 2 * LANES
    half = LANES // 2
    d_y = np.zeros((4 * LANES, wide), np.float32)
    d_z = np.zeros((wide, wide), np.float32)
    sweep = np.zeros((4 * LANES, wide), np.float32)
    for y in range(2 * per_tile):
        for z in range(NZ):
            column = y * NZ + z
            here = (y + per_tile) * NZ + z
            d_y[here + NZ, column] -= 0.5
            d_y[here - NZ, column] += 0.5
            d_z[y * NZ + (z + 1) % NZ, column] -= 0.5
            d_z[y * NZ + (z - 1) % NZ, column] += 0.5
            sweep[here, column] -= 1.0
            sweep[here + 2 * NZ, column] += 0.25
            sweep[here - 2 * NZ, column] += 0.25
            base = (y + per_tile) * NZ
            sweep[base + (z + 2) % NZ, column] += 0.25
            sweep[base + (z - 2) % NZ, column] += 0.25

    def inner(matrix):
        return matrix[LANES : 3 * LANES]

    def outer(matrix):
        return np.concatenate([matrix[3 * LANES : 3 * LANES + half], matrix[half:LANES]])

    return np.concatenate([inner(d_y), d_z, inner(sweep), outer(d_y), outer(sweep)], axis=0)


def advance_kernel(chain, corrected, rows, *refs):
    flags, matrix, x_first, x_second = refs[:4]
    refs = list(refs[4:])
    even_x = flags[0] == 1
    even_y = flags[1] == 1
    position = flags[2]
    inputs = []
    for link in range(chain):
        state, refs = refs[:3], refs[3:]
        extra = None
        if corrected[link]:
            extra, refs = refs[:3], refs[3:]
        inputs.append((state, extra))
    out, own, state_s, term_s, fresh_s, flow_x, slow, flow_y, flow_z, edges, arrival = refs
    high = rows + WINDOW
    above = START + high
    window = pl.ds(START, high)
    load_own = pltpu.make_async_copy(inputs[0][0][0], own, arrival)
    load_own.start()

    def lanes(tile):
        return pl.ds(tile * LANES, LANES)

    taken = x_first.shape[1]
    for field in range(FIELDS):
        for tile in range(4):
            one = x_first[field, :, lanes(tile)]
            two = x_second[field, :, lanes(tile)]
            edges[0, field, tile, pl.ds(0, taken), :] = jnp.where(even_x, two, one)
            edges[1, field, tile, pl.ds(0, taken), :] = jnp.where(even_x, one, two)
    sources, _ = edge_layout(chain, corrected)

    def place(target, index, kind):
        for distance, count, tiles, row, first_tile in sources[kind]:
            for tile in range(tiles):
                start = (4 - tiles) // 2 + tile
                low = edges[0, index[-1], first_tile + tile, pl.ds(row, count), :]
                top = edges[1, index[-1], first_tile + tile, pl.ds(row, count), :]
                target(start)[pl.ds(FIRST - distance - count, count), :] = low
                target(start)[pl.ds(FIRST + rows + distance, count), :] = top

    def assemble(link):
        (center, y_first, y_second), extra = inputs[link]
        if link == 0:
            load_own.wait()
            center = own
        for field in range(FIELDS):
            rest = jnp.full((FIRST, LANES), (1.0, 0.0, 0.0, 0.0, 2.5)[field], jnp.float32)
            for tile in range(6):
                if tile in (2, 3):
                    middle = center[field, :, lanes(tile - 2)].astype(jnp.float32)
                else:
                    one = y_first[field, :, lanes(tile % 2)].astype(jnp.float32)
                    two = y_second[field, :, lanes(tile % 2)].astype(jnp.float32)
                    middle = jnp.where(even_y, two, one) if tile < 2 else jnp.where(even_y, one, two)
                state_s[link, field, tile, pl.ds(FIRST, rows), :] = middle
                state_s[link, field, tile, pl.ds(0, FIRST), :] = rest
                state_s[link, field, tile, pl.ds(FIRST + rows, FIRST), :] = rest
            place(lambda tile: state_s.at[link, field, tile + 1], (field,), ("state", link))

    def assemble_terms(link):
        extra = inputs[link][1]
        if extra is not None:
            stored, y_first, y_second = extra
            none = jnp.zeros((FIRST, LANES), jnp.float32)
            for field in range(FIELDS):
                for tile in (2, 3):
                    old = [stored[age, field, :, lanes(tile - 2)].astype(jnp.float32) for age in range(3)]
                    terms = kept_terms(old)
                    for tick in range(TICKS):
                        term_s[link, tick, field, tile - 1, pl.ds(FIRST, rows), :] = terms[tick]
                for tick in range(2):
                    plane = tick * FIELDS + field
                    one = y_first[plane].astype(jnp.float32)
                    two = y_second[plane].astype(jnp.float32)
                    term_s[link, tick, field, 0, pl.ds(FIRST, rows), :] = jnp.where(even_y, two, one)
                    term_s[link, tick, field, 3, pl.ds(FIRST, rows), :] = jnp.where(even_y, one, two)
                    for tile in range(4):
                        term_s[link, tick, field, tile, pl.ds(0, FIRST), :] = none
                        term_s[link, tick, field, tile, pl.ds(FIRST + rows, FIRST), :] = none
                    place(lambda tile: term_s.at[link, tick, field, tile], (field,), ("kept", link, tick))

    def pointwise(link, tile, start, count, only_x):
        place = pl.ds(start, count)
        density, mom_x, mom_y, mom_z, energy = [state_s[link, field, tile, place, :] for field in range(FIELDS)]
        inverse = 1.0 / density
        vel_x = mom_x * inverse
        vel_y = mom_y * inverse
        vel_z = mom_z * inverse
        kinetic = 0.5 * (vel_x * vel_x + vel_y * vel_y + vel_z * vel_z)
        pressure = GAMMA_LESS * (energy - density * kinetic)
        enthalpy = energy + pressure
        heat = DYNAMIC_FRICTION * kinetic + CONDUCTIVITY * (pressure * inverse)
        xy = mom_x * vel_y
        xz = mom_x * vel_z
        yz = mom_y * vel_z
        along_x = (mom_x, mom_x * vel_x + pressure, xy, xz, enthalpy * vel_x)
        along_y = (mom_y, xy, mom_y * vel_y + pressure, yz, enthalpy * vel_y)
        along_z = (mom_z, xz, yz, mom_z * vel_z + pressure, enthalpy * vel_z)
        spread = (
            DYNAMIC_FRICTION * vel_x,
            DYNAMIC_FRICTION * vel_y,
            DYNAMIC_FRICTION * vel_z,
            heat,
        )
        for field in range(FIELDS):
            if 1 <= tile <= 4:
                flow_x[link, field, tile - 1, place, :] = along_x[field]
            if field:
                slow[link, field - 1, tile, place, :] = spread[field - 1]
            if not only_x:
                flow_y[link, tile, pl.ds(field * high, high), :] = along_y[field]
                if 1 <= tile <= 4:
                    flow_z[link, tile - 1, pl.ds(field * high, high), :] = along_z[field]

    def along_x(link, field, tile):
        def shifted(ref, *index, step):
            return ref[(link, *index, pl.ds(START + step, high))]

        total = 0.5 * (shifted(flow_x, field, tile - 1, step=-1) - shifted(flow_x, field, tile - 1, step=1))
        if field:
            around = shifted(slow, field - 1, tile, step=2) + shifted(slow, field - 1, tile, step=-2)
            total = total + (0.25 * around - 0.5 * shifted(slow, field - 1, tile, step=0))
        return total

    from_above = lax.broadcasted_iota(jnp.int32, (FIELDS * high, LANES), 1) < LANES // 2

    def products(link, tick):
        for tile in range(6) if tick == 0 else range(1, 5):
            pointwise(link, tile, START, high, False)
            if tick == 0 and 1 <= tile <= 4:
                pointwise(link, tile, 0, START, True)
                pointwise(link, tile, above, START, True)

        def spreading(tile):
            none = jnp.zeros((high, LANES), jnp.float32)
            return jnp.concatenate([none] + [slow[link, field, tile, window, :] for field in range(FIELDS - 1)])

        found = {}
        for low, top in ((2, 3),) if tick == TICKS - 1 else ((1, 2), (3, 4)):
            parts = [
                flow_y[link, low],
                flow_y[link, top],
                flow_z[link, low - 1],
                flow_z[link, top - 1],
                spreading(low),
                spreading(top),
                jnp.where(from_above, flow_y[link, top + 1], flow_y[link, low - 1]),
                jnp.where(from_above, spreading(top + 1), spreading(low - 1)),
            ]
            left = jnp.concatenate([part.astype(jnp.bfloat16) for part in parts], axis=1)
            found[low, top] = jnp.dot(left, matrix[...], preferred_element_type=jnp.float32)
        return found

    def update(link, tick, found):
        last = tick == TICKS - 1
        for group, product in found.items():
            for field in range(FIELDS):
                for side, tile in enumerate(group):
                    start = field * high
                    rate = product[start : start + high, side * LANES : (side + 1) * LANES]
                    rate = rate + along_x(link, field, tile)
                    if link:
                        fresh_s[link - 1, tick, field, tile - 1] = rate.astype(jnp.bfloat16).astype(jnp.float32)
                    if link + tick >= TICKS:
                        continue
                    step = rate
                    if corrected[link]:
                        extra = term_s[link, tick, field, tile - 1, window, :] + QUAD_WEIGHTS[3] * fresh_s[
                            link, tick, field, tile - 1
                        ]
                        for age in range(tick):
                            weight = QUAD_WEIGHTS[3 - tick + age] - (1.0 if age == tick - 1 else 0.0)
                            extra = extra + weight * fresh_s[link, age, field, tile - 1]
                        step = rate + jnp.where(position > link, extra, 0.0)
                    state = state_s[link, field, tile, window, :] + TIME_STEP * step
                    state_s[link, field, tile, window, :] = state
                    if last and link == 0:
                        out[field, :, lanes(tile - 2)] = state_s[link, field, tile, pl.ds(FIRST, rows), :]

    waiting = {}

    def finish(link, tick):
        if (link, tick) in waiting:
            finish(link + 1, tick)
            update(link, tick, waiting.pop((link, tick)))

    for tick in range(TICKS):
        for link in reversed(range(min(chain, TICKS - tick + 1))):
            if tick == 0:
                assemble(link)
            finish(link, tick - 1)
            waiting[link, tick] = products(link, tick)
            if tick == 0:
                assemble_terms(link)
    for link, tick in sorted(waiting, reverse=True):
        finish(link, tick)


def edge_layout(chain, corrected):
    sources = {}
    wide = []
    narrow = []
    for link in range(chain):
        wide.append((("state", link), 0, 4))
        narrow.append((("state", link), 4))
        if corrected[link]:
            wide.append((("kept", link, 0), 0, 2))
            narrow.append((("kept", link, 0), 2))
            narrow.append((("kept", link, 1), 0))
    row = 0
    for kind, distance, count in wide:
        sources.setdefault(kind, []).append((distance, count, 4, row, 0))
        row += count
    for place, (kind, distance) in enumerate(narrow):
        sources.setdefault(kind, []).append((distance, 2, 2, row + 2 * (place // 2), 2 * (place % 2)))
    return sources, row + 2 * ((len(narrow) + 1) // 2)


def kept_terms(old):
    first, second, third, _ = QUAD_WEIGHTS
    return (
        first * old[0] + second * old[1] + (third - 1.0) * old[2],
        first * old[1] + second * old[2],
        first * old[2],
    )


def per_device(fields, stored_rates):
    levels = min(4, lax.axis_size("sec"))
    position = lax.axis_index("sec") % levels
    even_x = lax.axis_index("gx") % 2 == 0 if lax.axis_size("gx") % 2 == 0 else jnp.bool_(True)
    even_y = lax.axis_index("gy") % 2 == 0 if lax.axis_size("gy") % 2 == 0 else jnp.bool_(True)
    block = fields[0]
    stored = stored_rates[0]
    rows, columns = block.shape[1:]
    chain = min(levels, TICKS + 1)
    corrected = [link < levels - 1 and link < TICKS for link in range(chain)]
    sent = block.astype(jnp.bfloat16)

    def padded_y(pair, center):
        first, second = pair
        low, top = jnp.where(even_y, second, first), jnp.where(even_y, first, second)
        return jnp.concatenate([low[:, :, -LANES:], center, top[:, :, :LANES]], axis=2)

    own_y = neighbours("gy", even_y, sent, sent)
    centers = [sent] + [from_lower(sent, levels, link) for link in range(1, chain)]
    kept = jnp.concatenate(kept_terms(stored.astype(jnp.float32))[:2], axis=0).astype(jnp.bfloat16)
    kept_y = neighbours("gy", even_y, kept[:, :, :LANES], kept[:, :, -LANES:])
    if chain > 1:
        first, centers = lax.optimization_barrier((own_y[0], centers))
        own_y = first, own_y[1]
    forwarded = [tuple(from_lower(half, levels, link) for half in own_y) for link in range(1, chain)]
    kept_y, forwarded = lax.optimization_barrier((kept_y, forwarded))

    padded = {}
    operands = []
    for link in range(chain):
        if link:
            link_y = forwarded[link - 1]
            operands += [centers[link], *link_y]
        else:
            link_y = own_y
            operands += [block, *own_y]
        padded["state", link] = padded_y(link_y, centers[link])
        if corrected[link]:
            if link:
                link_kept = from_lower(kept, levels, link)
                link_y = tuple(from_lower(half, levels, link) for half in kept_y)
                operands += [from_lower(stored, levels, link), *link_y]
            else:
                link_kept, link_y = kept, kept_y
                operands += [stored, *link_y]
            link_padded = padded_y(link_y, link_kept)
            padded["kept", link, 0] = link_padded[:FIELDS]
            padded["kept", link, 1] = link_padded[FIELDS:]

    sources, taken = edge_layout(chain, corrected)
    width = columns + 2 * LANES

    def edge(from_top):
        grid = {}
        for kind, pieces in sources.items():
            for distance, count, tiles, row, first_tile in pieces:
                start = rows - distance - count if from_top else distance
                skip = (4 - tiles) // 2 * LANES
                grid[row, first_tile] = padded[kind][:, start : start + count, skip : width - skip]
        parts = []
        for row, first_tile in sorted(grid):
            if first_tile:
                continue
            part = grid[row, 0]
            if part.shape[2] < width:
                part = jnp.concatenate([part, grid.get((row, 2), part)], axis=2)
            parts.append(part)
        return jnp.concatenate(parts, axis=1)

    over_x = neighbours("gx", even_x, edge(False), edge(True))
    operands = [half.astype(jnp.float32) for half in over_x] + operands
    flags = jnp.stack([even_x.astype(jnp.int32), even_y.astype(jnp.int32), position])
    matrix = jnp.asarray(stencil_matrix(), jnp.bfloat16)
    high = rows + WINDOW
    tall = rows + 2 * FIRST
    vmem = pl.BlockSpec(memory_space=pltpu.VMEM)
    specs = [vmem] * (len(operands) + 1)
    specs[3] = pl.BlockSpec(memory_space=pl.ANY)
    result = pl.pallas_call(
        functools.partial(advance_kernel, chain, corrected, rows),
        out_shape=jax.ShapeDtypeStruct((FIELDS, rows, columns), jnp.float32),
        in_specs=[pl.BlockSpec(memory_space=pltpu.SMEM)] + specs,
        out_specs=vmem,
        scratch_shapes=[
            pltpu.VMEM((FIELDS, rows, columns), jnp.float32),
            pltpu.VMEM((chain, FIELDS, 6, tall, LANES), jnp.float32),
            pltpu.VMEM((chain, TICKS, FIELDS, 4, tall, LANES), jnp.float32),
            pltpu.VMEM((chain, TICKS, FIELDS, 4, high, LANES), jnp.float32),
            pltpu.VMEM((chain, FIELDS, 4, tall, LANES), jnp.float32),
            pltpu.VMEM((chain, FIELDS - 1, 6, tall, LANES), jnp.float32),
            pltpu.VMEM((chain, 6, FIELDS * high, LANES), jnp.float32),
            pltpu.VMEM((chain, 4, FIELDS * high, LANES), jnp.float32),
            pltpu.VMEM((2, FIELDS, 4, -(-taken // 8) * 8, LANES), jnp.float32),
            pltpu.SemaphoreType.DMA(()),
        ],
        compiler_params=pltpu.CompilerParams(vmem_limit_bytes=48 * 1024 * 1024),
    )(flags, matrix, *operands)
    return result[None]


def solution(mesh):
    return jax.shard_map(
        per_device,
        mesh=mesh,
        in_specs=(P("sec", None, "gx", "gy"), P("sec", None, None, "gx", "gy")),
        out_specs=P("sec", None, "gx", "gy"),
        check_vma=False,
    )
```

```python
import functools

import jax
import jax.numpy as jnp
import numpy as np
from jax import lax
from jax.experimental import pallas as pl
from jax.experimental.pallas import tpu as pltpu
from jax.sharding import PartitionSpec as P

NZ = 32
TICKS = 3


TIME_STEP = 0.04
DYNAMIC_FRICTION = 0.4
CONDUCTIVITY = 0.5
GAMMA_LESS = 0.4
QUAD_WEIGHTS = (1.0 / 24.0, -5.0 / 24.0, 19.0 / 24.0, 9.0 / 24.0)

LANES = 128
FIRST = 12
START = 8
WINDOW = 2 * (FIRST - START)
FIELDS = 5


def neighbours(axis, even, low_edge, high_edge):
    count = lax.axis_size(axis)
    if count % 2:
        from_next = lax.ppermute(low_edge, axis, [(i, (i - 1) % count) for i in range(count)])
        from_last = lax.ppermute(high_edge, axis, [(i, (i + 1) % count) for i in range(count)])
        return from_next, from_last
    if low_edge is high_edge:
        outward = inward = low_edge
    else:
        outward = jnp.where(even, high_edge, low_edge)
        inward = jnp.where(even, low_edge, high_edge)
    far = [(i, (i + 1) % count if i % 2 else (i - 1) % count) for i in range(count)]
    near = [(i, i + 1 if i % 2 == 0 else i - 1) for i in range(count)]
    second = lax.ppermute(inward, axis, far)
    first = lax.ppermute(outward, axis, near)
    return first, second


def from_lower(block, levels, distance):
    count = lax.axis_size("sec")
    route = []
    for start in range(0, count, levels):
        route += [(start + i, start + (i + distance) % levels) for i in range(levels)]
    return lax.ppermute(block, "sec", route)


def stencil_matrix():
    per_tile = LANES // NZ
    wide = 2 * LANES
    half = LANES // 2
    d_y = np.zeros((4 * LANES, wide), np.float32)
    d_z = np.zeros((wide, wide), np.float32)
    sweep = np.zeros((4 * LANES, wide), np.float32)
    for y in range(2 * per_tile):
        for z in range(NZ):
            column = y * NZ + z
            here = (y + per_tile) * NZ + z
            d_y[here + NZ, column] -= 0.5
            d_y[here - NZ, column] += 0.5
            d_z[y * NZ + (z + 1) % NZ, column] -= 0.5
            d_z[y * NZ + (z - 1) % NZ, column] += 0.5
            sweep[here, column] -= 1.0
            sweep[here + 2 * NZ, column] += 0.25
            sweep[here - 2 * NZ, column] += 0.25
            base = (y + per_tile) * NZ
            sweep[base + (z + 2) % NZ, column] += 0.25
            sweep[base + (z - 2) % NZ, column] += 0.25

    def inner(matrix):
        return matrix[LANES : 3 * LANES]

    def outer(matrix):
        return np.concatenate([matrix[3 * LANES : 3 * LANES + half], matrix[half:LANES]])

    return np.concatenate([inner(d_y), d_z, inner(sweep), outer(d_y), outer(sweep)], axis=0)


def advance_kernel(chain, corrected, rows, *refs):
    flags, matrix, x_first, x_second = refs[:4]
    refs = list(refs[4:])
    even_x = flags[0] == 1
    even_y = flags[1] == 1
    position = flags[2]
    inputs = []
    for link in range(chain):
        state, refs = refs[:3], refs[3:]
        extra = None
        if corrected[link]:
            extra, refs = refs[:3], refs[3:]
        inputs.append((state, extra))
    out, state_s, term_s, fresh_s, flow_x, slow, flow_y, flow_z, edges = refs
    high = rows + WINDOW
    above = START + high
    window = pl.ds(START, high)

    def lanes(tile):
        return pl.ds(tile * LANES, LANES)

    taken = x_first.shape[1]
    for field in range(FIELDS):
        for tile in range(4):
            one = x_first[field, :, lanes(tile)]
            two = x_second[field, :, lanes(tile)]
            edges[0, field, tile, pl.ds(0, taken), :] = jnp.where(even_x, two, one)
            edges[1, field, tile, pl.ds(0, taken), :] = jnp.where(even_x, one, two)
    sources, _ = edge_layout(chain, corrected)

    def place(target, index, kind):
        for distance, count, tiles, row, first_tile in sources[kind]:
            for tile in range(tiles):
                start = (4 - tiles) // 2 + tile
                low = edges[0, index[-1], first_tile + tile, pl.ds(row, count), :]
                top = edges[1, index[-1], first_tile + tile, pl.ds(row, count), :]
                target(start)[pl.ds(FIRST - distance - count, count), :] = low
                target(start)[pl.ds(FIRST + rows + distance, count), :] = top

    def assemble(link):
        (center, y_first, y_second), extra = inputs[link]
        for field in range(FIELDS):
            rest = jnp.full((FIRST, LANES), (1.0, 0.0, 0.0, 0.0, 2.5)[field], jnp.float32)
            for tile in range(6):
                if tile in (2, 3):
                    middle = center[field, :, lanes(tile - 2)].astype(jnp.float32)
                else:
                    one = y_first[field, :, lanes(tile % 2)].astype(jnp.float32)
                    two = y_second[field, :, lanes(tile % 2)].astype(jnp.float32)
                    middle = jnp.where(even_y, two, one) if tile < 2 else jnp.where(even_y, one, two)
                state_s[link, field, tile, pl.ds(FIRST, rows), :] = middle
                state_s[link, field, tile, pl.ds(0, FIRST), :] = rest
                state_s[link, field, tile, pl.ds(FIRST + rows, FIRST), :] = rest
            place(lambda tile: state_s.at[link, field, tile + 1], (field,), ("state", link))

    def assemble_terms(link):
        extra = inputs[link][1]
        if extra is not None:
            stored, y_first, y_second = extra
            none = jnp.zeros((FIRST, LANES), jnp.float32)
            for field in range(FIELDS):
                for tile in (2, 3):
                    old = [stored[age, field, :, lanes(tile - 2)].astype(jnp.float32) for age in range(3)]
                    terms = kept_terms(old)
                    for tick in range(TICKS):
                        term_s[link, tick, field, tile - 1, pl.ds(FIRST, rows), :] = terms[tick]
                for tick in range(2):
                    plane = tick * FIELDS + field
                    one = y_first[plane].astype(jnp.float32)
                    two = y_second[plane].astype(jnp.float32)
                    term_s[link, tick, field, 0, pl.ds(FIRST, rows), :] = jnp.where(even_y, two, one)
                    term_s[link, tick, field, 3, pl.ds(FIRST, rows), :] = jnp.where(even_y, one, two)
                    for tile in range(4):
                        term_s[link, tick, field, tile, pl.ds(0, FIRST), :] = none
                        term_s[link, tick, field, tile, pl.ds(FIRST + rows, FIRST), :] = none
                    place(lambda tile: term_s.at[link, tick, field, tile], (field,), ("kept", link, tick))

    def pointwise(link, tile, start, count, only_x):
        place = pl.ds(start, count)
        density, mom_x, mom_y, mom_z, energy = [state_s[link, field, tile, place, :] for field in range(FIELDS)]
        inverse = 1.0 / density
        vel_x = mom_x * inverse
        vel_y = mom_y * inverse
        vel_z = mom_z * inverse
        kinetic = 0.5 * (vel_x * vel_x + vel_y * vel_y + vel_z * vel_z)
        pressure = GAMMA_LESS * (energy - density * kinetic)
        enthalpy = energy + pressure
        heat = DYNAMIC_FRICTION * kinetic + CONDUCTIVITY * (pressure * inverse)
        xy = mom_x * vel_y
        xz = mom_x * vel_z
        yz = mom_y * vel_z
        along_x = (mom_x, mom_x * vel_x + pressure, xy, xz, enthalpy * vel_x)
        along_y = (mom_y, xy, mom_y * vel_y + pressure, yz, enthalpy * vel_y)
        along_z = (mom_z, xz, yz, mom_z * vel_z + pressure, enthalpy * vel_z)
        spread = (
            DYNAMIC_FRICTION * vel_x,
            DYNAMIC_FRICTION * vel_y,
            DYNAMIC_FRICTION * vel_z,
            heat,
        )
        for field in range(FIELDS):
            if 1 <= tile <= 4:
                flow_x[link, field, tile - 1, place, :] = along_x[field]
            if field:
                slow[link, field - 1, tile, place, :] = spread[field - 1]
            if not only_x:
                flow_y[link, tile, pl.ds(field * high, high), :] = along_y[field]
                if 1 <= tile <= 4:
                    flow_z[link, tile - 1, pl.ds(field * high, high), :] = along_z[field]

    def along_x(link, field, tile):
        def shifted(ref, *index, step):
            return ref[(link, *index, pl.ds(START + step, high))]

        total = 0.5 * (shifted(flow_x, field, tile - 1, step=-1) - shifted(flow_x, field, tile - 1, step=1))
        if field:
            around = shifted(slow, field - 1, tile, step=2) + shifted(slow, field - 1, tile, step=-2)
            total = total + (0.25 * around - 0.5 * shifted(slow, field - 1, tile, step=0))
        return total

    from_above = lax.broadcasted_iota(jnp.int32, (FIELDS * high, LANES), 1) < LANES // 2

    def products(link, tick):
        for tile in range(6) if tick == 0 else range(1, 5):
            pointwise(link, tile, START, high, False)
            if tick == 0 and 1 <= tile <= 4:
                pointwise(link, tile, 0, START, True)
                pointwise(link, tile, above, START, True)

        def spreading(tile):
            none = jnp.zeros((high, LANES), jnp.float32)
            return jnp.concatenate([none] + [slow[link, field, tile, window, :] for field in range(FIELDS - 1)])

        found = {}
        for low, top in ((2, 3),) if tick == TICKS - 1 else ((1, 2), (3, 4)):
            parts = [
                flow_y[link, low],
                flow_y[link, top],
                flow_z[link, low - 1],
                flow_z[link, top - 1],
                spreading(low),
                spreading(top),
                jnp.where(from_above, flow_y[link, top + 1], flow_y[link, low - 1]),
                jnp.where(from_above, spreading(top + 1), spreading(low - 1)),
            ]
            left = jnp.concatenate([part.astype(jnp.bfloat16) for part in parts], axis=1)
            found[low, top] = jnp.dot(left, matrix[...], preferred_element_type=jnp.float32)
        return found

    def update(link, tick, found, lowest):
        last = tick == TICKS - 1
        for group, product in found.items():
            for field in range(FIELDS):
                for side, tile in enumerate(group):
                    start = field * high
                    rate = product[start : start + high, side * LANES : (side + 1) * LANES]
                    rate = rate + along_x(link, field, tile)
                    if link:
                        fresh_s[link - 1, tick, field, tile - 1] = rate.astype(jnp.bfloat16).astype(jnp.float32)
                    if link + tick >= TICKS:
                        continue
                    step = rate
                    if corrected[link] and not lowest:
                        extra = term_s[link, tick, field, tile - 1, window, :] + QUAD_WEIGHTS[3] * fresh_s[
                            link, tick, field, tile - 1
                        ]
                        for age in range(tick):
                            weight = QUAD_WEIGHTS[3 - tick + age] - (1.0 if age == tick - 1 else 0.0)
                            extra = extra + weight * fresh_s[link, age, field, tile - 1]
                        step = rate + (jnp.where(position > link, extra, 0.0) if link else extra)
                    state = state_s[link, field, tile, window, :] + TIME_STEP * step
                    state_s[link, field, tile, window, :] = state
                    if last and link == 0:
                        out[field, :, lanes(tile - 2)] = state_s[link, field, tile, pl.ds(FIRST, rows), :]

    def advance(links):
        waiting = {}

        def finish(link, tick):
            if (link, tick) in waiting:
                finish(link + 1, tick)
                update(link, tick, waiting.pop((link, tick)), links == 1)

        for tick in range(TICKS):
            for link in reversed(range(min(links, TICKS - tick + 1))):
                if tick == 0:
                    assemble(link)
                finish(link, tick - 1)
                waiting[link, tick] = products(link, tick)
                if tick == 0 and links > 1:
                    assemble_terms(link)
        for link, tick in sorted(waiting, reverse=True):
            finish(link, tick)

    if chain == 1:
        advance(1)
    else:
        pl.when(position == 0)(lambda: advance(1))
        pl.when(position > 0)(lambda: advance(chain))


def edge_layout(chain, corrected):
    sources = {}
    wide = []
    narrow = []
    for link in range(chain):
        wide.append((("state", link), 0, 4))
        narrow.append((("state", link), 4))
        if corrected[link]:
            wide.append((("kept", link, 0), 0, 2))
            narrow.append((("kept", link, 0), 2))
            narrow.append((("kept", link, 1), 0))
    row = 0
    for kind, distance, count in wide:
        sources.setdefault(kind, []).append((distance, count, 4, row, 0))
        row += count
    for place, (kind, distance) in enumerate(narrow):
        sources.setdefault(kind, []).append((distance, 2, 2, row + 2 * (place // 2), 2 * (place % 2)))
    return sources, row + 2 * ((len(narrow) + 1) // 2)


def kept_terms(old):
    first, second, third, _ = QUAD_WEIGHTS
    return (
        first * old[0] + second * old[1] + (third - 1.0) * old[2],
        first * old[1] + second * old[2],
        first * old[2],
    )


def per_device(fields, stored_rates):
    levels = min(4, lax.axis_size("sec"))
    position = lax.axis_index("sec") % levels
    even_x = lax.axis_index("gx") % 2 == 0 if lax.axis_size("gx") % 2 == 0 else jnp.bool_(True)
    even_y = lax.axis_index("gy") % 2 == 0 if lax.axis_size("gy") % 2 == 0 else jnp.bool_(True)
    block = fields[0]
    stored = stored_rates[0]
    rows, columns = block.shape[1:]
    chain = min(levels, TICKS + 1)
    corrected = [link < levels - 1 and link < TICKS for link in range(chain)]
    whole = lax.reduce_precision(block, 8, 22)
    sent = block.astype(jnp.bfloat16)
    whole, sent = lax.optimization_barrier((whole, sent))

    def padded_y(pair, center):
        first, second = pair
        low, top = jnp.where(even_y, second, first), jnp.where(even_y, first, second)
        return jnp.concatenate([low[:, :, -LANES:], center, top[:, :, :LANES]], axis=2)

    own_y = neighbours("gy", even_y, sent, sent)
    centers = [sent] + [from_lower(sent, levels, link) for link in range(1, chain)]
    kept = jnp.concatenate(kept_terms(stored.astype(jnp.float32))[:2], axis=0).astype(jnp.bfloat16)
    kept_y = neighbours("gy", even_y, kept[:, :, :LANES], kept[:, :, -LANES:])
    if chain > 1:
        first, centers = lax.optimization_barrier((own_y[0], centers))
        own_y = first, own_y[1]
    forwarded = [tuple(from_lower(half, levels, link) for half in own_y) for link in range(1, chain)]
    kept_y, forwarded = lax.optimization_barrier((kept_y, forwarded))

    padded = {}
    operands = []
    for link in range(chain):
        if link:
            link_y = forwarded[link - 1]
            operands += [centers[link], *link_y]
        else:
            link_y = own_y
            operands += [whole, *own_y]
        padded["state", link] = padded_y(link_y, centers[link])
        if corrected[link]:
            if link:
                link_kept = from_lower(kept, levels, link)
                link_y = tuple(from_lower(half, levels, link) for half in kept_y)
                operands += [from_lower(stored, levels, link), *link_y]
            else:
                link_kept, link_y = kept, kept_y
                operands += [stored, *link_y]
            link_padded = padded_y(link_y, link_kept)
            padded["kept", link, 0] = link_padded[:FIELDS]
            padded["kept", link, 1] = link_padded[FIELDS:]

    sources, taken = edge_layout(chain, corrected)
    width = columns + 2 * LANES

    def edge(from_top):
        grid = {}
        for kind, pieces in sources.items():
            for distance, count, tiles, row, first_tile in pieces:
                start = rows - distance - count if from_top else distance
                skip = (4 - tiles) // 2 * LANES
                grid[row, first_tile] = padded[kind][:, start : start + count, skip : width - skip]
        parts = []
        for row, first_tile in sorted(grid):
            if first_tile:
                continue
            part = grid[row, 0]
            if part.shape[2] < width:
                part = jnp.concatenate([part, grid.get((row, 2), part)], axis=2)
            parts.append(part)
        return jnp.concatenate(parts, axis=1)

    over_x = neighbours("gx", even_x, edge(False), edge(True))
    operands = [half.astype(jnp.float32) for half in over_x] + operands
    flags = jnp.stack([even_x.astype(jnp.int32), even_y.astype(jnp.int32), position])
    matrix = jnp.asarray(stencil_matrix(), jnp.bfloat16)
    high = rows + WINDOW
    tall = rows + 2 * FIRST
    vmem = pl.BlockSpec(memory_space=pltpu.VMEM)
    specs = [vmem] * (len(operands) + 1)
    result = pl.pallas_call(
        functools.partial(advance_kernel, chain, corrected, rows),
        out_shape=jax.ShapeDtypeStruct((FIELDS, rows, columns), jnp.float32),
        in_specs=[pl.BlockSpec(memory_space=pltpu.SMEM)] + specs,
        out_specs=vmem,
        scratch_shapes=[
            pltpu.VMEM((chain, FIELDS, 6, tall, LANES), jnp.float32),
            pltpu.VMEM((chain, TICKS, FIELDS, 4, tall, LANES), jnp.float32),
            pltpu.VMEM((chain, TICKS, FIELDS, 4, high, LANES), jnp.float32),
            pltpu.VMEM((chain, FIELDS, 4, tall, LANES), jnp.float32),
            pltpu.VMEM((chain, FIELDS - 1, 6, tall, LANES), jnp.float32),
            pltpu.VMEM((chain, 6, FIELDS * high, LANES), jnp.float32),
            pltpu.VMEM((chain, 4, FIELDS * high, LANES), jnp.float32),
            pltpu.VMEM((2, FIELDS, 4, -(-taken // 8) * 8, LANES), jnp.float32),
        ],
        compiler_params=pltpu.CompilerParams(vmem_limit_bytes=48 * 1024 * 1024),
    )(flags, matrix, *operands)
    return result[None]


def solution(mesh):
    return jax.shard_map(
        per_device,
        mesh=mesh,
        in_specs=(P("sec", None, "gx", "gy"), P("sec", None, None, "gx", "gy")),
        out_specs=P("sec", None, "gx", "gy"),
        check_vma=False,
    )
```

```python
import functools

import jax
import jax.numpy as jnp
import numpy as np
from jax import lax
from jax.experimental import pallas as pl
from jax.experimental.pallas import tpu as pltpu
from jax.sharding import PartitionSpec as P

NZ = 32
TICKS = 3


TIME_STEP = 0.04
DYNAMIC_FRICTION = 0.4
CONDUCTIVITY = 0.5
GAMMA_LESS = 0.4
QUAD_WEIGHTS = (1.0 / 24.0, -5.0 / 24.0, 19.0 / 24.0, 9.0 / 24.0)

LANES = 128
FIRST = 12
START = 8
WINDOW = 2 * (FIRST - START)
FIELDS = 5


def neighbours(axis, even, low_edge, high_edge):
    count = lax.axis_size(axis)
    if count % 2:
        from_next = lax.ppermute(low_edge, axis, [(i, (i - 1) % count) for i in range(count)])
        from_last = lax.ppermute(high_edge, axis, [(i, (i + 1) % count) for i in range(count)])
        return from_next, from_last
    if low_edge is high_edge:
        outward = inward = low_edge
    else:
        outward = jnp.where(even, high_edge, low_edge)
        inward = jnp.where(even, low_edge, high_edge)
    far = [(i, (i + 1) % count if i % 2 else (i - 1) % count) for i in range(count)]
    near = [(i, i + 1 if i % 2 == 0 else i - 1) for i in range(count)]
    second = lax.ppermute(inward, axis, far)
    first = lax.ppermute(outward, axis, near)
    return first, second


def from_lower(block, levels, distance):
    count = lax.axis_size("sec")
    route = []
    for start in range(0, count, levels):
        route += [(start + i, start + (i + distance) % levels) for i in range(levels)]
    return lax.ppermute(block, "sec", route)


def stencil_matrix():
    per_tile = LANES // NZ
    wide = 2 * LANES
    half = LANES // 2
    d_y = np.zeros((4 * LANES, wide), np.float32)
    d_z = np.zeros((wide, wide), np.float32)
    sweep = np.zeros((4 * LANES, wide), np.float32)
    for y in range(2 * per_tile):
        for z in range(NZ):
            column = y * NZ + z
            here = (y + per_tile) * NZ + z
            d_y[here + NZ, column] -= 0.5
            d_y[here - NZ, column] += 0.5
            d_z[y * NZ + (z + 1) % NZ, column] -= 0.5
            d_z[y * NZ + (z - 1) % NZ, column] += 0.5
            sweep[here, column] -= 1.0
            sweep[here + 2 * NZ, column] += 0.25
            sweep[here - 2 * NZ, column] += 0.25
            base = (y + per_tile) * NZ
            sweep[base + (z + 2) % NZ, column] += 0.25
            sweep[base + (z - 2) % NZ, column] += 0.25

    def inner(matrix):
        return matrix[LANES : 3 * LANES]

    def outer(matrix):
        return np.concatenate([matrix[3 * LANES : 3 * LANES + half], matrix[half:LANES]])

    return np.concatenate([inner(d_y), d_z, inner(sweep), outer(d_y), outer(sweep)], axis=0)


def advance_kernel(chain, corrected, rows, *refs):
    flags, matrix, *came = refs[:6]
    refs = list(refs[6:])
    even_x = flags[0] == 1
    even_y = flags[1] == 1
    position = flags[2]
    inputs = []
    for link in range(chain):
        state, refs = refs[:3], refs[3:]
        extra = None
        if corrected[link]:
            extra, refs = refs[:3], refs[3:]
        inputs.append((state, extra))
    out, state_s, term_s, fresh_s, flow_x, slow, flow_y, flow_z, edges = refs
    high = rows + WINDOW
    above = START + high
    window = pl.ds(START, high)

    def lanes(tile):
        return pl.ds(tile * LANES, LANES)

    sources = {}
    for turn, kinds in enumerate(edge_turns(chain, corrected)):
        pieces, taken = edge_layout(kinds)
        sources.update((kind, (turn, parts)) for kind, parts in pieces.items())
        first, second = came[2 * turn : 2 * turn + 2]
        for field in range(FIELDS):
            for tile in range(4):
                one = first[field, :, lanes(tile)]
                two = second[field, :, lanes(tile)]
                edges[turn, 0, field, tile, pl.ds(0, taken), :] = jnp.where(even_x, two, one)
                edges[turn, 1, field, tile, pl.ds(0, taken), :] = jnp.where(even_x, one, two)

    def place(target, index, kind):
        turn, pieces = sources[kind]
        for distance, count, tiles, row, first_tile in pieces:
            for tile in range(tiles):
                start = (4 - tiles) // 2 + tile
                low = edges[turn, 0, index[-1], first_tile + tile, pl.ds(row, count), :]
                top = edges[turn, 1, index[-1], first_tile + tile, pl.ds(row, count), :]
                target(start)[pl.ds(FIRST - distance - count, count), :] = low
                target(start)[pl.ds(FIRST + rows + distance, count), :] = top

    def assemble(link):
        (center, y_first, y_second), extra = inputs[link]
        for field in range(FIELDS):
            rest = jnp.full((FIRST, LANES), (1.0, 0.0, 0.0, 0.0, 2.5)[field], jnp.float32)
            for tile in range(6):
                if tile in (2, 3):
                    middle = center[field, :, lanes(tile - 2)].astype(jnp.float32)
                else:
                    one = y_first[field, :, lanes(tile % 2)].astype(jnp.float32)
                    two = y_second[field, :, lanes(tile % 2)].astype(jnp.float32)
                    middle = jnp.where(even_y, two, one) if tile < 2 else jnp.where(even_y, one, two)
                state_s[link, field, tile, pl.ds(FIRST, rows), :] = middle
                state_s[link, field, tile, pl.ds(0, FIRST), :] = rest
                state_s[link, field, tile, pl.ds(FIRST + rows, FIRST), :] = rest
            place(lambda tile: state_s.at[link, field, tile + 1], (field,), ("state", link))

    def assemble_terms(link):
        extra = inputs[link][1]
        if extra is not None:
            stored, y_first, y_second = extra
            none = jnp.zeros((FIRST, LANES), jnp.float32)
            for field in range(FIELDS):
                for tile in (2, 3):
                    old = [stored[age, field, :, lanes(tile - 2)].astype(jnp.float32) for age in range(3)]
                    terms = kept_terms(old)
                    for tick in range(TICKS):
                        term_s[link, tick, field, tile - 1, pl.ds(FIRST, rows), :] = terms[tick]
                for tick in range(2):
                    plane = tick * FIELDS + field
                    one = y_first[plane].astype(jnp.float32)
                    two = y_second[plane].astype(jnp.float32)
                    term_s[link, tick, field, 0, pl.ds(FIRST, rows), :] = jnp.where(even_y, two, one)
                    term_s[link, tick, field, 3, pl.ds(FIRST, rows), :] = jnp.where(even_y, one, two)
                    for tile in range(4):
                        term_s[link, tick, field, tile, pl.ds(0, FIRST), :] = none
                        term_s[link, tick, field, tile, pl.ds(FIRST + rows, FIRST), :] = none
                    place(lambda tile: term_s.at[link, tick, field, tile], (field,), ("kept", link, tick))

    def pointwise(link, tile, start, count, only_x):
        place = pl.ds(start, count)
        density, mom_x, mom_y, mom_z, energy = [state_s[link, field, tile, place, :] for field in range(FIELDS)]
        inverse = 1.0 / density
        vel_x = mom_x * inverse
        vel_y = mom_y * inverse
        vel_z = mom_z * inverse
        kinetic = 0.5 * (vel_x * vel_x + vel_y * vel_y + vel_z * vel_z)
        pressure = GAMMA_LESS * (energy - density * kinetic)
        enthalpy = energy + pressure
        heat = DYNAMIC_FRICTION * kinetic + CONDUCTIVITY * (pressure * inverse)
        xy = mom_x * vel_y
        xz = mom_x * vel_z
        yz = mom_y * vel_z
        along_x = (mom_x, mom_x * vel_x + pressure, xy, xz, enthalpy * vel_x)
        along_y = (mom_y, xy, mom_y * vel_y + pressure, yz, enthalpy * vel_y)
        along_z = (mom_z, xz, yz, mom_z * vel_z + pressure, enthalpy * vel_z)
        spread = (
            DYNAMIC_FRICTION * vel_x,
            DYNAMIC_FRICTION * vel_y,
            DYNAMIC_FRICTION * vel_z,
            heat,
        )
        for field in range(FIELDS):
            if 1 <= tile <= 4:
                flow_x[link, field, tile - 1, place, :] = along_x[field]
            if field:
                slow[link, field - 1, tile, place, :] = spread[field - 1]
            if not only_x:
                flow_y[link, tile, pl.ds(field * high, high), :] = along_y[field]
                if 1 <= tile <= 4:
                    flow_z[link, tile - 1, pl.ds(field * high, high), :] = along_z[field]

    def along_x(link, field, tile):
        def shifted(ref, *index, step):
            return ref[(link, *index, pl.ds(START + step, high))]

        total = 0.5 * (shifted(flow_x, field, tile - 1, step=-1) - shifted(flow_x, field, tile - 1, step=1))
        if field:
            around = shifted(slow, field - 1, tile, step=2) + shifted(slow, field - 1, tile, step=-2)
            total = total + (0.25 * around - 0.5 * shifted(slow, field - 1, tile, step=0))
        return total

    from_above = lax.broadcasted_iota(jnp.int32, (FIELDS * high, LANES), 1) < LANES // 2

    def products(link, tick):
        for tile in range(6) if tick == 0 else range(1, 5):
            pointwise(link, tile, START, high, False)
            if tick == 0 and 1 <= tile <= 4:
                pointwise(link, tile, 0, START, True)
                pointwise(link, tile, above, START, True)

        def spreading(tile):
            none = jnp.zeros((high, LANES), jnp.float32)
            return jnp.concatenate([none] + [slow[link, field, tile, window, :] for field in range(FIELDS - 1)])

        found = {}
        for low, top in ((2, 3),) if tick == TICKS - 1 else ((1, 2), (3, 4)):
            parts = [
                flow_y[link, low],
                flow_y[link, top],
                flow_z[link, low - 1],
                flow_z[link, top - 1],
                spreading(low),
                spreading(top),
                jnp.where(from_above, flow_y[link, top + 1], flow_y[link, low - 1]),
                jnp.where(from_above, spreading(top + 1), spreading(low - 1)),
            ]
            left = jnp.concatenate([part.astype(jnp.bfloat16) for part in parts], axis=1)
            found[low, top] = jnp.dot(left, matrix[...], preferred_element_type=jnp.float32)
        return found

    def update(link, tick, found, lowest):
        last = tick == TICKS - 1
        for group, product in found.items():
            for field in range(FIELDS):
                for side, tile in enumerate(group):
                    start = field * high
                    rate = product[start : start + high, side * LANES : (side + 1) * LANES]
                    rate = rate + along_x(link, field, tile)
                    if link:
                        fresh_s[link - 1, tick, field, tile - 1] = rate.astype(jnp.bfloat16).astype(jnp.float32)
                    if link + tick >= TICKS:
                        continue
                    step = rate
                    if corrected[link] and not lowest:
                        extra = term_s[link, tick, field, tile - 1, window, :] + QUAD_WEIGHTS[3] * fresh_s[
                            link, tick, field, tile - 1
                        ]
                        for age in range(tick):
                            weight = QUAD_WEIGHTS[3 - tick + age] - (1.0 if age == tick - 1 else 0.0)
                            extra = extra + weight * fresh_s[link, age, field, tile - 1]
                        step = rate + (jnp.where(position > link, extra, 0.0) if link else extra)
                    state = state_s[link, field, tile, window, :] + TIME_STEP * step
                    state_s[link, field, tile, window, :] = state
                    if last and link == 0:
                        out[field, :, lanes(tile - 2)] = state_s[link, field, tile, pl.ds(FIRST, rows), :]

    def advance(links):
        waiting = {}

        def finish(link, tick):
            if (link, tick) in waiting:
                finish(link + 1, tick)
                update(link, tick, waiting.pop((link, tick)), links == 1)

        for tick in range(TICKS):
            for link in reversed(range(min(links, TICKS - tick + 1))):
                if tick == 0:
                    assemble(link)
                finish(link, tick - 1)
                waiting[link, tick] = products(link, tick)
                if tick == 0 and links > 1:
                    assemble_terms(link)
        for link, tick in sorted(waiting, reverse=True):
            finish(link, tick)

    if chain == 1:
        advance(1)
    else:
        pl.when(position == 0)(lambda: advance(1))
        pl.when(position > 0)(lambda: advance(chain))


def edge_turns(chain, corrected):
    state = ((0, 4, True), (4, 2, False))
    terms = (((0, 2, True), (2, 2, False)), ((0, 2, False),))
    early = [(("state", 0), state)]
    late = []
    for link in range(chain):
        if link:
            late.append((("state", link), state))
        if corrected[link]:
            late.append((("kept", link, 0), terms[0]))
            (late if link else early).append((("kept", link, 1), terms[1]))
    return early, late


def edge_layout(kinds):
    sources = {}
    narrow = []
    row = 0
    for kind, pieces in kinds:
        for distance, count, wide in pieces:
            if wide:
                sources.setdefault(kind, []).append((distance, count, 4, row, 0))
                row += count
            else:
                narrow.append((kind, distance, count))
    for place, (kind, distance, count) in enumerate(narrow):
        sources.setdefault(kind, []).append((distance, count, 2, row + 2 * (place // 2), 2 * (place % 2)))
    return sources, row + 2 * ((len(narrow) + 1) // 2)


def kept_terms(old):
    first, second, third, _ = QUAD_WEIGHTS
    return (
        first * old[0] + second * old[1] + (third - 1.0) * old[2],
        first * old[1] + second * old[2],
        first * old[2],
    )


def per_device(fields, stored_rates):
    levels = min(4, lax.axis_size("sec"))
    position = lax.axis_index("sec") % levels
    even_x = lax.axis_index("gx") % 2 == 0 if lax.axis_size("gx") % 2 == 0 else jnp.bool_(True)
    even_y = lax.axis_index("gy") % 2 == 0 if lax.axis_size("gy") % 2 == 0 else jnp.bool_(True)
    block = fields[0]
    stored = stored_rates[0]
    rows, columns = block.shape[1:]
    chain = min(levels, TICKS + 1)
    corrected = [link < levels - 1 and link < TICKS for link in range(chain)]
    whole = lax.reduce_precision(block, 8, 22)
    sent = block.astype(jnp.bfloat16)
    whole, sent = lax.optimization_barrier((whole, sent))

    def padded_y(pair, center):
        first, second = pair
        low, top = jnp.where(even_y, second, first), jnp.where(even_y, first, second)
        return jnp.concatenate([low[:, :, -LANES:], center, top[:, :, :LANES]], axis=2)

    own_y = neighbours("gy", even_y, sent, sent)
    centers = [sent] + [from_lower(sent, levels, link) for link in range(1, chain)]
    kept = jnp.concatenate(kept_terms(stored.astype(jnp.float32))[:2], axis=0).astype(jnp.bfloat16)
    kept_y = neighbours("gy", even_y, kept[:, :, :LANES], kept[:, :, -LANES:])
    if chain > 1:
        first, centers = lax.optimization_barrier((own_y[0], centers))
        own_y = first, own_y[1]
    forwarded = [tuple(from_lower(half, levels, link) for half in own_y) for link in range(1, chain)]
    kept_y, forwarded = lax.optimization_barrier((kept_y, forwarded))

    padded = {("state", 0): padded_y(own_y, sent)}
    if corrected[0]:
        padded["kept", 0, 1] = jnp.pad(kept[FIELDS:], ((0, 0), (0, 0), (LANES, LANES)))

    width = columns + 2 * LANES

    def over_x(kinds):
        pieces, _ = edge_layout(kinds)

        def edge(from_top):
            grid = {}
            for kind, parts in pieces.items():
                for distance, count, tiles, row, first_tile in parts:
                    start = rows - distance - count if from_top else distance
                    skip = (4 - tiles) // 2 * LANES
                    grid[row, first_tile] = padded[kind][:, start : start + count, skip : width - skip]
            parts = []
            for row, first_tile in sorted(grid):
                if first_tile:
                    continue
                part = grid[row, 0]
                if part.shape[2] < width:
                    part = jnp.concatenate([part, grid.get((row, 2), part)], axis=2)
                parts.append(part)
            return jnp.concatenate(parts, axis=1)

        return [half.astype(jnp.float32) for half in neighbours("gx", even_x, edge(False), edge(True))]

    early, late = edge_turns(chain, corrected)
    came = over_x(early)
    kept_y, forwarded = lax.optimization_barrier((kept_y, forwarded))
    operands = [whole, *own_y]
    for link in range(chain):
        if link:
            operands += [centers[link], *forwarded[link - 1]]
            padded["state", link] = padded_y(forwarded[link - 1], centers[link])
        if corrected[link]:
            if link:
                link_kept = from_lower(kept, levels, link)
                link_y = tuple(from_lower(half, levels, link) for half in kept_y)
                operands += [from_lower(stored, levels, link), *link_y]
            else:
                link_kept, link_y = kept, kept_y
                operands += [stored, *link_y]
            link_padded = padded_y(link_y, link_kept)
            padded["kept", link, 0] = link_padded[:FIELDS]
            if link:
                padded["kept", link, 1] = link_padded[FIELDS:]
    came += over_x(late)
    operands = came + operands
    flags = jnp.stack([even_x.astype(jnp.int32), even_y.astype(jnp.int32), position])
    matrix = jnp.asarray(stencil_matrix(), jnp.bfloat16)
    high = rows + WINDOW
    tall = rows + 2 * FIRST
    vmem = pl.BlockSpec(memory_space=pltpu.VMEM)
    taken = max(edge_layout(kinds)[1] for kinds in (early, late))
    specs = [vmem] * (len(operands) + 1)
    result = pl.pallas_call(
        functools.partial(advance_kernel, chain, corrected, rows),
        out_shape=jax.ShapeDtypeStruct((FIELDS, rows, columns), jnp.float32),
        in_specs=[pl.BlockSpec(memory_space=pltpu.SMEM)] + specs,
        out_specs=vmem,
        scratch_shapes=[
            pltpu.VMEM((chain, FIELDS, 6, tall, LANES), jnp.float32),
            pltpu.VMEM((chain, TICKS, FIELDS, 4, tall, LANES), jnp.float32),
            pltpu.VMEM((chain, TICKS, FIELDS, 4, high, LANES), jnp.float32),
            pltpu.VMEM((chain, FIELDS, 4, tall, LANES), jnp.float32),
            pltpu.VMEM((chain, FIELDS - 1, 6, tall, LANES), jnp.float32),
            pltpu.VMEM((chain, 6, FIELDS * high, LANES), jnp.float32),
            pltpu.VMEM((chain, 4, FIELDS * high, LANES), jnp.float32),
            pltpu.VMEM((2, 2, FIELDS, 4, -(-taken // 8) * 8, LANES), jnp.float32),
        ],
        compiler_params=pltpu.CompilerParams(vmem_limit_bytes=48 * 1024 * 1024),
    )(flags, matrix, *operands)
    return result[None]


def solution(mesh):
    return jax.shard_map(
        per_device,
        mesh=mesh,
        in_specs=(P("sec", None, "gx", "gy"), P("sec", None, None, "gx", "gy")),
        out_specs=P("sec", None, "gx", "gy"),
        check_vma=False,
    )
```

```python
import functools

import jax
import jax.numpy as jnp
import numpy as np
from jax import lax
from jax.experimental import pallas as pl
from jax.experimental.pallas import tpu as pltpu
from jax.sharding import PartitionSpec as P

NZ = 32
TICKS = 3


TIME_STEP = 0.04
DYNAMIC_FRICTION = 0.4
CONDUCTIVITY = 0.5
GAMMA_LESS = 0.4
QUAD_WEIGHTS = (1.0 / 24.0, -5.0 / 24.0, 19.0 / 24.0, 9.0 / 24.0)

LANES = 128
FIRST = 12
START = 8
WINDOW = 2 * (FIRST - START)
FIELDS = 5


def neighbours(axis, even, low_edge, high_edge):
    count = lax.axis_size(axis)
    if count % 2:
        from_next = lax.ppermute(low_edge, axis, [(i, (i - 1) % count) for i in range(count)])
        from_last = lax.ppermute(high_edge, axis, [(i, (i + 1) % count) for i in range(count)])
        return from_next, from_last
    if low_edge is high_edge:
        outward = inward = low_edge
    else:
        outward = jnp.where(even, high_edge, low_edge)
        inward = jnp.where(even, low_edge, high_edge)
    far = [(i, (i + 1) % count if i % 2 else (i - 1) % count) for i in range(count)]
    near = [(i, i + 1 if i % 2 == 0 else i - 1) for i in range(count)]
    second = lax.ppermute(inward, axis, far)
    first = lax.ppermute(outward, axis, near)
    return first, second


def from_lower(block, levels, distance):
    count = lax.axis_size("sec")
    route = []
    for start in range(0, count, levels):
        route += [(start + i, start + (i + distance) % levels) for i in range(levels)]
    return lax.ppermute(block, "sec", route)


def stencil_matrix():
    per_tile = LANES // NZ
    wide = 2 * LANES
    half = LANES // 2
    d_y = np.zeros((4 * LANES, wide), np.float32)
    d_z = np.zeros((wide, wide), np.float32)
    sweep = np.zeros((4 * LANES, wide), np.float32)
    for y in range(2 * per_tile):
        for z in range(NZ):
            column = y * NZ + z
            here = (y + per_tile) * NZ + z
            d_y[here + NZ, column] -= 0.5
            d_y[here - NZ, column] += 0.5
            d_z[y * NZ + (z + 1) % NZ, column] -= 0.5
            d_z[y * NZ + (z - 1) % NZ, column] += 0.5
            sweep[here, column] -= 1.0
            sweep[here + 2 * NZ, column] += 0.25
            sweep[here - 2 * NZ, column] += 0.25
            base = (y + per_tile) * NZ
            sweep[base + (z + 2) % NZ, column] += 0.25
            sweep[base + (z - 2) % NZ, column] += 0.25

    def inner(matrix):
        return matrix[LANES : 3 * LANES]

    def outer(matrix):
        return np.concatenate([matrix[3 * LANES : 3 * LANES + half], matrix[half:LANES]])

    return np.concatenate([inner(d_y), d_z, inner(sweep), outer(d_y), outer(sweep)], axis=0)


def lanes(tile):
    return pl.ds(tile * LANES, LANES)


def scratch_of_level(rows):
    high, tall = rows + WINDOW, rows + 2 * FIRST
    return [
        pltpu.VMEM((FIELDS, 6, tall, LANES), jnp.float32),
        pltpu.VMEM((FIELDS, 4, tall, LANES), jnp.float32),
        pltpu.VMEM((FIELDS - 1, 6, tall, LANES), jnp.float32),
        pltpu.VMEM((6, FIELDS * high, LANES), jnp.float32),
        pltpu.VMEM((4, FIELDS * high, LANES), jnp.float32),
    ]


def unpack_edges(edges, first, second, even_x):
    count = first.shape[1]
    for field in range(FIELDS):
        for tile in range(4):
            one = first[field, :, lanes(tile)]
            two = second[field, :, lanes(tile)]
            edges[0, field, tile, pl.ds(0, count), :] = jnp.where(even_x, two, one)
            edges[1, field, tile, pl.ds(0, count), :] = jnp.where(even_x, one, two)


def place_edges(target, edges, pieces, field, rows):
    for distance, count, tiles, row, first_tile in pieces:
        for tile in range(tiles):
            start = (4 - tiles) // 2 + tile
            came = field, first_tile + tile, pl.ds(row, count)
            target(start)[pl.ds(FIRST - distance - count, count), :] = edges[(0, *came)]
            target(start)[pl.ds(FIRST + rows + distance, count), :] = edges[(1, *came)]


class Level:
    def __init__(self, rows, even_x, even_y, matrix, scratch):
        self.rows, self.even_x, self.even_y, self.matrix = rows, even_x, even_y, matrix
        self.state, self.flow_x, self.slow, self.flow_y, self.flow_z = scratch
        self.high = rows + WINDOW
        self.window = pl.ds(START, self.high)

    def ordered(self, even, first, second):
        return jnp.where(even, second, first), jnp.where(even, first, second)

    def assemble(self, center, y_first, y_second, edges, pieces):
        rows = self.rows
        for field in range(FIELDS):
            rest = jnp.full((FIRST, LANES), (1.0, 0.0, 0.0, 0.0, 2.5)[field], jnp.float32)
            for tile in range(6):
                target = self.state.at[field, tile]
                if tile in (2, 3):
                    middle = center[field, :, lanes(tile - 2)].astype(jnp.float32)
                else:
                    one = y_first[field, :, lanes(tile % 2)].astype(jnp.float32)
                    two = y_second[field, :, lanes(tile % 2)].astype(jnp.float32)
                    middle = self.ordered(self.even_y, one, two)[tile // 4]
                target[pl.ds(FIRST, rows), :] = middle
                target[pl.ds(0, FIRST), :] = rest
                target[pl.ds(FIRST + rows, FIRST), :] = rest
            place_edges(lambda tile: self.state.at[field, tile + 1], edges, pieces, field, rows)

    def assemble_terms(self, terms, stored, y_first, y_second, edges, pieces):
        rows = self.rows
        none = jnp.zeros((FIRST, LANES), jnp.float32)
        for field in range(FIELDS):
            for tile in (1, 2):
                old = [stored[age, field, :, lanes(tile - 1)].astype(jnp.float32) for age in range(3)]
                for tick, term in enumerate(kept_terms(old)):
                    terms[tick, field, tile, pl.ds(FIRST, rows), :] = term
            for tick in range(2):
                one = y_first[tick * FIELDS + field].astype(jnp.float32)
                two = y_second[tick * FIELDS + field].astype(jnp.float32)
                low, top = self.ordered(self.even_y, one, two)
                terms[tick, field, 0, pl.ds(FIRST, rows), :] = low
                terms[tick, field, 3, pl.ds(FIRST, rows), :] = top
                for tile in range(4):
                    terms[tick, field, tile, pl.ds(0, FIRST), :] = none
                    terms[tick, field, tile, pl.ds(FIRST + rows, FIRST), :] = none
                place_edges(lambda tile: terms.at[tick, field, tile], edges[tick], pieces[tick], field, rows)

    def pointwise(self, tile, start, count, only_x):
        place = pl.ds(start, count)
        density, mom_x, mom_y, mom_z, energy = [self.state[field, tile, place, :] for field in range(FIELDS)]
        inverse = 1.0 / density
        vel_x = mom_x * inverse
        vel_y = mom_y * inverse
        vel_z = mom_z * inverse
        kinetic = 0.5 * (vel_x * vel_x + vel_y * vel_y + vel_z * vel_z)
        pressure = GAMMA_LESS * (energy - density * kinetic)
        enthalpy = energy + pressure
        heat = DYNAMIC_FRICTION * kinetic + CONDUCTIVITY * (pressure * inverse)
        xy = mom_x * vel_y
        xz = mom_x * vel_z
        yz = mom_y * vel_z
        along_x = (mom_x, mom_x * vel_x + pressure, xy, xz, enthalpy * vel_x)
        along_y = (mom_y, xy, mom_y * vel_y + pressure, yz, enthalpy * vel_y)
        along_z = (mom_z, xz, yz, mom_z * vel_z + pressure, enthalpy * vel_z)
        spread = (
            DYNAMIC_FRICTION * vel_x,
            DYNAMIC_FRICTION * vel_y,
            DYNAMIC_FRICTION * vel_z,
            heat,
        )
        for field in range(FIELDS):
            if 1 <= tile <= 4:
                self.flow_x[field, tile - 1, place, :] = along_x[field]
            if field:
                self.slow[field - 1, tile, place, :] = spread[field - 1]
            if not only_x:
                self.flow_y[tile, pl.ds(field * self.high, self.high), :] = along_y[field]
                if 1 <= tile <= 4:
                    self.flow_z[tile - 1, pl.ds(field * self.high, self.high), :] = along_z[field]

    def spreading(self, tile):
        none = jnp.zeros((self.high, LANES), jnp.float32)
        return jnp.concatenate([none] + [self.slow[kind, tile, self.window, :] for kind in range(FIELDS - 1)])

    def products(self, tick):
        for tile in range(6) if tick == 0 else range(1, 5):
            self.pointwise(tile, START, self.high, False)
            if tick == 0 and 1 <= tile <= 4:
                self.pointwise(tile, 0, START, True)
                self.pointwise(tile, START + self.high, START, True)
        from_above = lax.broadcasted_iota(jnp.int32, (FIELDS * self.high, LANES), 1) < LANES // 2
        flow_y, flow_z, spreading = self.flow_y, self.flow_z, self.spreading
        found = {}
        for low, top in ((2, 3),) if tick == TICKS - 1 else ((1, 2), (3, 4)):
            parts = [
                flow_y[low],
                flow_y[top],
                flow_z[low - 1],
                flow_z[top - 1],
                spreading(low),
                spreading(top),
                jnp.where(from_above, flow_y[top + 1], flow_y[low - 1]),
                jnp.where(from_above, spreading(top + 1), spreading(low - 1)),
            ]
            left = jnp.concatenate([part.astype(jnp.bfloat16) for part in parts], axis=1)
            found[low, top] = jnp.dot(left, self.matrix[...], preferred_element_type=jnp.float32)
        return found

    def along_x(self, field, tile):
        def shifted(ref, *index, step):
            return ref[(*index, pl.ds(START + step, self.high))]

        total = 0.5 * (shifted(self.flow_x, field, tile - 1, step=-1) - shifted(self.flow_x, field, tile - 1, step=1))
        if field:
            kind = field - 1
            around = shifted(self.slow, kind, tile, step=2) + shifted(self.slow, kind, tile, step=-2)
            total = total + (0.25 * around - 0.5 * shifted(self.slow, kind, tile, step=0))
        return total

    def rates(self, found):
        for group, product in found.items():
            for field in range(FIELDS):
                for side, tile in enumerate(group):
                    start = field * self.high
                    part = product[start : start + self.high, side * LANES : (side + 1) * LANES]
                    yield field, tile, part + self.along_x(field, tile)


def edge_turns(chain, corrected):
    state = ((0, 4, True), (4, 2, False))
    terms = (((0, 2, True), (2, 2, False)), ((0, 2, False),))
    early = [(("state", 0), state)]
    late = []
    for link in range(chain):
        if link:
            late.append((("state", link), state))
        if corrected[link]:
            late.append((("kept", link, 0), terms[0]))
            (late if link else early).append((("kept", link, 1), terms[1]))
    return early, late


def edge_layout(kinds):
    sources = {}
    narrow = []
    row = 0
    for kind, pieces in kinds:
        for distance, count, wide in pieces:
            if wide:
                sources.setdefault(kind, []).append((distance, count, 4, row, 0))
                row += count
            else:
                narrow.append((kind, distance, count))
    for place, (kind, distance, count) in enumerate(narrow):
        sources.setdefault(kind, []).append((distance, count, 2, row + 2 * (place // 2), 2 * (place % 2)))
    return sources, row + 2 * ((len(narrow) + 1) // 2)


def first_kernel(chain, corrected, rows, *refs):
    flags, matrix, x_first, x_second, center, y_first, y_second, out, edges, *scratch = refs
    even_x = flags[0] == 1
    pieces, _ = edge_layout(edge_turns(chain, corrected)[0])
    unpack_edges(edges, x_first, x_second, even_x)
    level = Level(rows, even_x, flags[1] == 1, matrix, scratch)
    level.assemble(center, y_first, y_second, edges, pieces["state", 0])
    for field, tile, rate in level.rates(level.products(0)):
        out[field, tile - 1] = level.state[field, tile, level.window, :] + TIME_STEP * rate


def advance_kernel(chain, corrected, rows, *refs):
    flags, matrix, begun, *refs = refs
    came, refs = refs[:4], refs[4:]
    inputs = []
    for link in range(chain):
        state, refs = (refs[:3], refs[3:]) if link else (None, refs)
        stored, refs = (refs[:3], refs[3:]) if corrected[link] else (None, refs)
        inputs.append((state, stored))
    out, fresh, terms, edges, *refs = refs
    even_x = flags[0] == 1
    position = flags[2]
    levels = [
        Level(rows, even_x, flags[1] == 1, matrix, refs[5 * link : 5 * link + 5]) for link in range(chain)
    ]
    window = levels[0].window
    layout = {}
    for turn, kinds in enumerate(edge_turns(chain, corrected)):
        pieces, _ = edge_layout(kinds)
        layout.update((kind, (edges.at[turn], parts)) for kind, parts in pieces.items())

    def correction(link, tick, field, tile):
        total = terms[link, tick, field, tile - 1, window, :] + QUAD_WEIGHTS[3] * fresh[link, tick, field, tile - 1]
        for age in range(tick):
            weight = QUAD_WEIGHTS[3 - tick + age] - (1.0 if age == tick - 1 else 0.0)
            total = total + weight * fresh[link, age, field, tile - 1]
        return jnp.where(position > link, total, 0.0) if link else total

    def advance(links):
        def begin(link):
            state, stored = inputs[link]
            if state is not None:
                levels[link].assemble(*state, *layout["state", link])

        def begin_terms(link):
            if corrected[link]:
                places = [layout["kept", link, tick] for tick in range(2)]
                levels[link].assemble_terms(terms.at[link], *inputs[link][1], *zip(*places))

        def update(link, tick, found):
            level = levels[link]
            fix = corrected[link] and links > 1
            if link == 0 and tick == 0:
                for field in range(FIELDS):
                    for tile in range(1, 5):
                        state = begun[field, tile - 1]
                        if fix:
                            state = state + TIME_STEP * correction(0, 0, field, tile)
                        level.state[field, tile, window, :] = state
                return
            for field, tile, rate in level.rates(found):
                if link:
                    fresh[link - 1, tick, field, tile - 1] = rate.astype(jnp.bfloat16).astype(jnp.float32)
                if link + tick >= TICKS:
                    continue
                step = rate + correction(link, tick, field, tile) if fix else rate
                level.state[field, tile, window, :] = level.state[field, tile, window, :] + TIME_STEP * step
                if tick == TICKS - 1:
                    out[field, :, lanes(tile - 2)] = level.state[field, tile, pl.ds(FIRST, rows), :]

        waiting = {}

        def finish(link, tick):
            if (link, tick) in waiting:
                finish(link + 1, tick)
                update(link, tick, waiting.pop((link, tick)))

        if links > 1:
            for turn in range(2):
                unpack_edges(edges.at[turn], *came[2 * turn : 2 * turn + 2], even_x)
        for tick in range(TICKS):
            for link in reversed(range(min(links, TICKS - tick + 1))):
                if tick == 0:
                    begin(link)
                finish(link, tick - 1)
                waiting[link, tick] = levels[link].products(tick) if link or tick else None
                if tick == 0 and links > 1:
                    begin_terms(link)
        for link, tick in sorted(waiting, reverse=True):
            finish(link, tick)

    if chain == 1:
        advance(1)
    else:
        pl.when(position == 0)(lambda: advance(1))
        pl.when(position > 0)(lambda: advance(chain))


def kept_terms(old):
    first, second, third, _ = QUAD_WEIGHTS
    return (
        first * old[0] + second * old[1] + (third - 1.0) * old[2],
        first * old[1] + second * old[2],
        first * old[2],
    )


def per_device(fields, stored_rates):
    levels = min(4, lax.axis_size("sec"))
    position = lax.axis_index("sec") % levels
    even_x = lax.axis_index("gx") % 2 == 0 if lax.axis_size("gx") % 2 == 0 else jnp.bool_(True)
    even_y = lax.axis_index("gy") % 2 == 0 if lax.axis_size("gy") % 2 == 0 else jnp.bool_(True)
    block = fields[0]
    stored = stored_rates[0]
    rows, columns = block.shape[1:]
    chain = min(levels, TICKS + 1)
    corrected = [link < levels - 1 and link < TICKS for link in range(chain)]
    whole = lax.reduce_precision(block, 8, 22)
    sent = block.astype(jnp.bfloat16)
    whole, sent = lax.optimization_barrier((whole, sent))

    def padded_y(pair, center):
        first, second = pair
        low, top = jnp.where(even_y, second, first), jnp.where(even_y, first, second)
        return jnp.concatenate([low[:, :, -LANES:], center, top[:, :, :LANES]], axis=2)

    own_y = neighbours("gy", even_y, sent, sent)
    centers = [sent] + [from_lower(sent, levels, link) for link in range(1, chain)]
    kept = jnp.concatenate(kept_terms(stored.astype(jnp.float32))[:2], axis=0).astype(jnp.bfloat16)
    kept_y = neighbours("gy", even_y, kept[:, :, :LANES], kept[:, :, -LANES:])
    if chain > 1:
        first, centers = lax.optimization_barrier((own_y[0], centers))
        own_y = first, own_y[1]
    forwarded = [tuple(from_lower(half, levels, link) for half in own_y) for link in range(1, chain)]
    kept_y, forwarded = lax.optimization_barrier((kept_y, forwarded))

    padded = {("state", 0): padded_y(own_y, sent)}
    if corrected[0]:
        padded["kept", 0, 1] = jnp.pad(kept[FIELDS:], ((0, 0), (0, 0), (LANES, LANES)))

    width = columns + 2 * LANES

    def over_x(kinds):
        pieces, _ = edge_layout(kinds)

        def edge(from_top):
            grid = {}
            for kind, parts in pieces.items():
                for distance, count, tiles, row, first_tile in parts:
                    start = rows - distance - count if from_top else distance
                    skip = (4 - tiles) // 2 * LANES
                    grid[row, first_tile] = padded[kind][:, start : start + count, skip : width - skip]
            parts = []
            for row, first_tile in sorted(grid):
                if first_tile:
                    continue
                part = grid[row, 0]
                if part.shape[2] < width:
                    part = jnp.concatenate([part, grid.get((row, 2), part)], axis=2)
                parts.append(part)
            return jnp.concatenate(parts, axis=1)

        return [half.astype(jnp.float32) for half in neighbours("gx", even_x, edge(False), edge(True))]

    early, late = edge_turns(chain, corrected)
    came = over_x(early)
    kept_y, forwarded = lax.optimization_barrier((kept_y, forwarded))
    operands = []
    for link in range(chain):
        if link:
            operands += [centers[link], *forwarded[link - 1]]
            padded["state", link] = padded_y(forwarded[link - 1], centers[link])
        if corrected[link]:
            if link:
                link_kept = from_lower(kept, levels, link)
                link_y = tuple(from_lower(half, levels, link) for half in kept_y)
                operands += [from_lower(stored, levels, link), *link_y]
            else:
                link_kept, link_y = kept, kept_y
                operands += [stored, *link_y]
            link_padded = padded_y(link_y, link_kept)
            padded["kept", link, 0] = link_padded[:FIELDS]
            if link:
                padded["kept", link, 1] = link_padded[FIELDS:]
    came += over_x(late)
    flags = jnp.stack([even_x.astype(jnp.int32), even_y.astype(jnp.int32), position])
    matrix = jnp.asarray(stencil_matrix(), jnp.bfloat16)
    high, tall = rows + WINDOW, rows + 2 * FIRST
    smem = pl.BlockSpec(memory_space=pltpu.SMEM)
    vmem = pl.BlockSpec(memory_space=pltpu.VMEM)
    params = pltpu.CompilerParams(vmem_limit_bytes=48 * 1024 * 1024)
    taken = max(edge_layout(kinds)[1] for kinds in (early, late))
    edges = 2, FIELDS, 4, -(-taken // 8) * 8, LANES
    begun = pl.pallas_call(
        functools.partial(first_kernel, chain, corrected, rows),
        out_shape=jax.ShapeDtypeStruct((FIELDS, 4, high, LANES), jnp.float32),
        in_specs=[smem] + [vmem] * 6,
        out_specs=vmem,
        scratch_shapes=[pltpu.VMEM(edges, jnp.float32), *scratch_of_level(rows)],
        compiler_params=params,
        name="own_first_tick",
    )(flags, matrix, *came[:2], whole, *own_y)
    operands = [begun, *came, *operands]
    result = pl.pallas_call(
        functools.partial(advance_kernel, chain, corrected, rows),
        out_shape=jax.ShapeDtypeStruct((FIELDS, rows, columns), jnp.float32),
        in_specs=[smem] + [vmem] * (len(operands) + 1),
        out_specs=vmem,
        scratch_shapes=[
            pltpu.VMEM((chain, TICKS, FIELDS, 4, high, LANES), jnp.float32),
            pltpu.VMEM((chain, TICKS, FIELDS, 4, tall, LANES), jnp.float32),
            pltpu.VMEM((2, *edges), jnp.float32),
            *(scratch_of_level(rows) * chain),
        ],
        compiler_params=params,
        name="advance",
    )(flags, matrix, *operands)
    return result[None]


def solution(mesh):
    return jax.shard_map(
        per_device,
        mesh=mesh,
        in_specs=(P("sec", None, "gx", "gy"), P("sec", None, None, "gx", "gy")),
        out_specs=P("sec", None, "gx", "gy"),
        check_vma=False,
    )
```

```python
import functools

import jax
import jax.numpy as jnp
import numpy as np
from jax import lax
from jax.experimental import pallas as pl
from jax.experimental.pallas import tpu as pltpu
from jax.sharding import PartitionSpec as P

NZ = 32
TICKS = 3


TIME_STEP = 0.04
DYNAMIC_FRICTION = 0.4
CONDUCTIVITY = 0.5
GAMMA_LESS = 0.4
QUAD_WEIGHTS = (1.0 / 24.0, -5.0 / 24.0, 19.0 / 24.0, 9.0 / 24.0)

LANES = 128
FIRST = 12
START = 8
WINDOW = 2 * (FIRST - START)
FIELDS = 5


def neighbours(axis, even, low_edge, high_edge):
    count = lax.axis_size(axis)
    if count % 2:
        from_next = lax.ppermute(low_edge, axis, [(i, (i - 1) % count) for i in range(count)])
        from_last = lax.ppermute(high_edge, axis, [(i, (i + 1) % count) for i in range(count)])
        return from_next, from_last
    if low_edge is high_edge:
        outward = inward = low_edge
    else:
        outward = jnp.where(even, high_edge, low_edge)
        inward = jnp.where(even, low_edge, high_edge)
    far = [(i, (i + 1) % count if i % 2 else (i - 1) % count) for i in range(count)]
    near = [(i, i + 1 if i % 2 == 0 else i - 1) for i in range(count)]
    second = lax.ppermute(inward, axis, far)
    first = lax.ppermute(outward, axis, near)
    return first, second


def from_lower(block, levels, distance):
    count = lax.axis_size("sec")
    route = []
    for start in range(0, count, levels):
        route += [(start + i, start + (i + distance) % levels) for i in range(levels)]
    return lax.ppermute(block, "sec", route)


def stencil_matrix():
    per_tile = LANES // NZ
    wide = 2 * LANES
    half = LANES // 2
    d_y = np.zeros((4 * LANES, wide), np.float32)
    d_z = np.zeros((wide, wide), np.float32)
    sweep = np.zeros((4 * LANES, wide), np.float32)
    for y in range(2 * per_tile):
        for z in range(NZ):
            column = y * NZ + z
            here = (y + per_tile) * NZ + z
            d_y[here + NZ, column] -= 0.5
            d_y[here - NZ, column] += 0.5
            d_z[y * NZ + (z + 1) % NZ, column] -= 0.5
            d_z[y * NZ + (z - 1) % NZ, column] += 0.5
            sweep[here, column] -= 1.0
            sweep[here + 2 * NZ, column] += 0.25
            sweep[here - 2 * NZ, column] += 0.25
            base = (y + per_tile) * NZ
            sweep[base + (z + 2) % NZ, column] += 0.25
            sweep[base + (z - 2) % NZ, column] += 0.25

    def inner(matrix):
        return matrix[LANES : 3 * LANES]

    def outer(matrix):
        return np.concatenate([matrix[3 * LANES : 3 * LANES + half], matrix[half:LANES]])

    return np.concatenate([inner(d_y), d_z, inner(sweep), outer(d_y), outer(sweep)], axis=0)


def lanes(tile):
    return pl.ds(tile * LANES, LANES)


def scratch_of_level(rows):
    high, tall = rows + WINDOW, rows + 2 * FIRST
    return [
        pltpu.VMEM((FIELDS, 6, tall, LANES), jnp.float32),
        pltpu.VMEM((FIELDS, 4, tall, LANES), jnp.float32),
        pltpu.VMEM((FIELDS - 1, 6, tall, LANES), jnp.float32),
        pltpu.VMEM((6, FIELDS * high, LANES), jnp.float32),
        pltpu.VMEM((4, FIELDS * high, LANES), jnp.float32),
    ]


def unpack_edges(edges, first, second, even_x):
    count = first.shape[1]
    for field in range(FIELDS):
        for tile in range(4):
            one = first[field, :, lanes(tile)]
            two = second[field, :, lanes(tile)]
            edges[0, field, tile, pl.ds(0, count), :] = jnp.where(even_x, two, one)
            edges[1, field, tile, pl.ds(0, count), :] = jnp.where(even_x, one, two)


def place_edges(target, edges, pieces, field, rows):
    for distance, count, tiles, row, first_tile in pieces:
        for tile in range(tiles):
            start = (4 - tiles) // 2 + tile
            came = field, first_tile + tile, pl.ds(row, count)
            target(start)[pl.ds(FIRST - distance - count, count), :] = edges[(0, *came)]
            target(start)[pl.ds(FIRST + rows + distance, count), :] = edges[(1, *came)]


class Level:
    def __init__(self, rows, even_x, even_y, matrix, scratch):
        self.rows, self.even_x, self.even_y, self.matrix = rows, even_x, even_y, matrix
        self.state, self.flow_x, self.slow, self.flow_y, self.flow_z = scratch
        self.high = rows + WINDOW
        self.window = pl.ds(START, self.high)

    def ordered(self, even, first, second):
        return jnp.where(even, second, first), jnp.where(even, first, second)

    def assemble(self, center, y_first, y_second, edges, pieces):
        rows = self.rows
        for field in range(FIELDS):
            rest = jnp.full((FIRST, LANES), (1.0, 0.0, 0.0, 0.0, 2.5)[field], jnp.float32)
            for tile in range(6):
                target = self.state.at[field, tile]
                if tile in (2, 3):
                    middle = center[field, :, lanes(tile - 2)].astype(jnp.float32)
                else:
                    one = y_first[field, :, lanes(tile % 2)].astype(jnp.float32)
                    two = y_second[field, :, lanes(tile % 2)].astype(jnp.float32)
                    middle = self.ordered(self.even_y, one, two)[tile // 4]
                target[pl.ds(FIRST, rows), :] = middle
                target[pl.ds(0, FIRST), :] = rest
                target[pl.ds(FIRST + rows, FIRST), :] = rest
            place_edges(lambda tile: self.state.at[field, tile + 1], edges, pieces, field, rows)

    def assemble_terms(self, terms, stored, y_first, y_second, edges, pieces):
        rows = self.rows
        none = jnp.zeros((FIRST, LANES), jnp.float32)
        for field in range(FIELDS):
            for tile in (1, 2):
                old = [stored[age, field, :, lanes(tile - 1)].astype(jnp.float32) for age in range(3)]
                for tick, term in enumerate(kept_terms(old)):
                    terms[tick, field, tile, pl.ds(FIRST, rows), :] = term
            for tick in range(2):
                one = y_first[tick * FIELDS + field].astype(jnp.float32)
                two = y_second[tick * FIELDS + field].astype(jnp.float32)
                low, top = self.ordered(self.even_y, one, two)
                terms[tick, field, 0, pl.ds(FIRST, rows), :] = low
                terms[tick, field, 3, pl.ds(FIRST, rows), :] = top
                for tile in range(4):
                    terms[tick, field, tile, pl.ds(0, FIRST), :] = none
                    terms[tick, field, tile, pl.ds(FIRST + rows, FIRST), :] = none
                place_edges(lambda tile: terms.at[tick, field, tile], edges[tick], pieces[tick], field, rows)

    def pointwise(self, tile, start, count, only_x):
        place = pl.ds(start, count)
        density, mom_x, mom_y, mom_z, energy = [self.state[field, tile, place, :] for field in range(FIELDS)]
        inverse = 1.0 / density
        vel_x = mom_x * inverse
        vel_y = mom_y * inverse
        vel_z = mom_z * inverse
        kinetic = 0.5 * (vel_x * vel_x + vel_y * vel_y + vel_z * vel_z)
        pressure = GAMMA_LESS * (energy - density * kinetic)
        enthalpy = energy + pressure
        heat = DYNAMIC_FRICTION * kinetic + CONDUCTIVITY * (pressure * inverse)
        xy = mom_x * vel_y
        xz = mom_x * vel_z
        yz = mom_y * vel_z
        along_x = (mom_x, mom_x * vel_x + pressure, xy, xz, enthalpy * vel_x)
        along_y = (mom_y, xy, mom_y * vel_y + pressure, yz, enthalpy * vel_y)
        along_z = (mom_z, xz, yz, mom_z * vel_z + pressure, enthalpy * vel_z)
        spread = (
            DYNAMIC_FRICTION * vel_x,
            DYNAMIC_FRICTION * vel_y,
            DYNAMIC_FRICTION * vel_z,
            heat,
        )
        for field in range(FIELDS):
            if 1 <= tile <= 4:
                self.flow_x[field, tile - 1, place, :] = along_x[field]
            if field:
                self.slow[field - 1, tile, place, :] = spread[field - 1]
            if not only_x:
                self.flow_y[tile, pl.ds(field * self.high, self.high), :] = along_y[field]
                if 1 <= tile <= 4:
                    self.flow_z[tile - 1, pl.ds(field * self.high, self.high), :] = along_z[field]

    def products(self, tick):
        known = range(6) if tick == 0 else range(1, 5)
        for tile in known:
            self.pointwise(tile, START, self.high, False)
            if tick == 0 and 1 <= tile <= 4:
                self.pointwise(tile, 0, START, True)
                self.pointwise(tile, START + self.high, START, True)
        from_above = lax.broadcasted_iota(jnp.int32, (FIELDS * self.high, LANES), 1) < LANES // 2
        flow_z = self.flow_z

        def flow_y(tile):
            return self.flow_y[tile] if tile in known else jnp.zeros((FIELDS * self.high, LANES), jnp.float32)

        def spreading(tile):
            none = jnp.zeros((self.high, LANES), jnp.float32)
            kinds = [self.slow[kind, tile, self.window, :] if tile in known else none for kind in range(FIELDS - 1)]
            return jnp.concatenate([none, *kinds])

        found = {}
        for low, top in ((2, 3),) if tick == TICKS - 1 else ((1, 2), (3, 4)):
            parts = [
                flow_y(low),
                flow_y(top),
                flow_z[low - 1],
                flow_z[top - 1],
                spreading(low),
                spreading(top),
                jnp.where(from_above, flow_y(top + 1), flow_y(low - 1)),
                jnp.where(from_above, spreading(top + 1), spreading(low - 1)),
            ]
            left = jnp.concatenate([part.astype(jnp.bfloat16) for part in parts], axis=1)
            found[low, top] = jnp.dot(left, self.matrix[...], preferred_element_type=jnp.float32)
        return found

    def along_x(self, field, tile):
        def shifted(ref, *index, step):
            return ref[(*index, pl.ds(START + step, self.high))]

        total = 0.5 * (shifted(self.flow_x, field, tile - 1, step=-1) - shifted(self.flow_x, field, tile - 1, step=1))
        if field:
            kind = field - 1
            around = shifted(self.slow, kind, tile, step=2) + shifted(self.slow, kind, tile, step=-2)
            total = total + (0.25 * around - 0.5 * shifted(self.slow, kind, tile, step=0))
        return total

    def rates(self, found):
        for group, product in found.items():
            for field in range(FIELDS):
                for side, tile in enumerate(group):
                    start = field * self.high
                    part = product[start : start + self.high, side * LANES : (side + 1) * LANES]
                    yield field, tile, part + self.along_x(field, tile)


def edge_turns(chain, corrected):
    state = ((0, 4, True), (4, 2, False))
    terms = (((0, 2, True), (2, 2, False)), ((0, 2, False),))
    early = [(("state", 0), state)]
    late = []
    for link in range(chain):
        if link:
            late.append((("state", link), state))
        if corrected[link]:
            late.append((("kept", link, 0), terms[0]))
            (late if link else early).append((("kept", link, 1), terms[1]))
    return early, late


def edge_layout(kinds):
    sources = {}
    narrow = []
    row = 0
    for kind, pieces in kinds:
        for distance, count, wide in pieces:
            if wide:
                sources.setdefault(kind, []).append((distance, count, 4, row, 0))
                row += count
            else:
                narrow.append((kind, distance, count))
    for place, (kind, distance, count) in enumerate(narrow):
        sources.setdefault(kind, []).append((distance, count, 2, row + 2 * (place // 2), 2 * (place % 2)))
    return sources, row + 2 * ((len(narrow) + 1) // 2)


def first_kernel(chain, corrected, rows, *refs):
    flags, matrix, x_first, x_second, center, y_first, y_second, out, edges, *scratch = refs
    even_x = flags[0] == 1
    pieces, _ = edge_layout(edge_turns(chain, corrected)[0])
    unpack_edges(edges, x_first, x_second, even_x)
    level = Level(rows, even_x, flags[1] == 1, matrix, scratch)
    level.assemble(center, y_first, y_second, edges, pieces["state", 0])
    for field, tile, rate in level.rates(level.products(0)):
        out[field, tile - 1] = level.state[field, tile, level.window, :] + TIME_STEP * rate


def advance_kernel(chain, corrected, rows, *refs):
    flags, matrix, begun, *refs = refs
    came, refs = refs[:4], refs[4:]
    inputs = []
    for link in range(chain):
        state, refs = (refs[:3], refs[3:]) if link else (None, refs)
        stored, refs = (refs[:3], refs[3:]) if corrected[link] else (None, refs)
        inputs.append((state, stored))
    out, fresh, terms, edges, *refs = refs
    even_x = flags[0] == 1
    position = flags[2]
    levels = [
        Level(rows, even_x, flags[1] == 1, matrix, refs[5 * link : 5 * link + 5]) for link in range(chain)
    ]
    window = levels[0].window
    layout = {}
    for turn, kinds in enumerate(edge_turns(chain, corrected)):
        pieces, _ = edge_layout(kinds)
        layout.update((kind, (edges.at[turn], parts)) for kind, parts in pieces.items())

    def correction(link, tick, field, tile):
        total = terms[link, tick, field, tile - 1, window, :] + QUAD_WEIGHTS[3] * fresh[link, tick, field, tile - 1]
        for age in range(tick):
            weight = QUAD_WEIGHTS[3 - tick + age] - (1.0 if age == tick - 1 else 0.0)
            total = total + weight * fresh[link, age, field, tile - 1]
        return jnp.where(position > link, total, 0.0) if link else total

    def advance(links):
        def begin(link):
            state, stored = inputs[link]
            if state is not None:
                levels[link].assemble(*state, *layout["state", link])

        def begin_terms(link):
            if corrected[link]:
                places = [layout["kept", link, tick] for tick in range(2)]
                levels[link].assemble_terms(terms.at[link], *inputs[link][1], *zip(*places))

        def update(link, tick, found):
            level = levels[link]
            fix = corrected[link] and links > 1
            if link == 0 and tick == 0:
                for field in range(FIELDS):
                    for tile in range(1, 5):
                        state = begun[field, tile - 1]
                        if fix:
                            state = state + TIME_STEP * correction(0, 0, field, tile)
                        level.state[field, tile, window, :] = state
                return
            for field, tile, rate in level.rates(found):
                if link:
                    fresh[link - 1, tick, field, tile - 1] = rate.astype(jnp.bfloat16).astype(jnp.float32)
                if link + tick >= TICKS:
                    continue
                step = rate + correction(link, tick, field, tile) if fix else rate
                level.state[field, tile, window, :] = level.state[field, tile, window, :] + TIME_STEP * step
                if tick == TICKS - 1:
                    out[field, :, lanes(tile - 2)] = level.state[field, tile, pl.ds(FIRST, rows), :]

        waiting = {}

        def finish(link, tick):
            if (link, tick) in waiting:
                finish(link + 1, tick)
                update(link, tick, waiting.pop((link, tick)))

        if links > 1:
            for turn in range(2):
                unpack_edges(edges.at[turn], *came[2 * turn : 2 * turn + 2], even_x)
        for tick in range(TICKS):
            for link in reversed(range(min(links, TICKS - tick + 1))):
                if tick == 0:
                    begin(link)
                finish(link, tick - 1)
                waiting[link, tick] = levels[link].products(tick) if link or tick else None
                if tick == 0 and links > 1:
                    begin_terms(link)
        for link, tick in sorted(waiting, reverse=True):
            finish(link, tick)

    if chain == 1:
        advance(1)
    else:
        pl.when(position == 0)(lambda: advance(1))
        pl.when(position > 0)(lambda: advance(chain))


def kept_terms(old):
    first, second, third, _ = QUAD_WEIGHTS
    return (
        first * old[0] + second * old[1] + (third - 1.0) * old[2],
        first * old[1] + second * old[2],
        first * old[2],
    )


def per_device(fields, stored_rates):
    levels = min(4, lax.axis_size("sec"))
    position = lax.axis_index("sec") % levels
    even_x = lax.axis_index("gx") % 2 == 0 if lax.axis_size("gx") % 2 == 0 else jnp.bool_(True)
    even_y = lax.axis_index("gy") % 2 == 0 if lax.axis_size("gy") % 2 == 0 else jnp.bool_(True)
    block = fields[0]
    stored = stored_rates[0]
    rows, columns = block.shape[1:]
    chain = min(levels, TICKS + 1)
    corrected = [link < levels - 1 and link < TICKS for link in range(chain)]
    whole = lax.reduce_precision(block, 8, 22)
    sent = block.astype(jnp.bfloat16)
    whole, sent = lax.optimization_barrier((whole, sent))

    def padded_y(pair, center):
        first, second = pair
        low, top = jnp.where(even_y, second, first), jnp.where(even_y, first, second)
        return jnp.concatenate([low[:, :, -LANES:], center, top[:, :, :LANES]], axis=2)

    own_y = neighbours("gy", even_y, sent, sent)
    centers = [sent] + [from_lower(sent, levels, link) for link in range(1, chain)]
    kept = jnp.concatenate(kept_terms(stored.astype(jnp.float32))[:2], axis=0).astype(jnp.bfloat16)
    kept_y = neighbours("gy", even_y, kept[:, :, :LANES], kept[:, :, -LANES:])
    if chain > 1:
        first, centers = lax.optimization_barrier((own_y[0], centers))
        own_y = first, own_y[1]
    forwarded = [tuple(from_lower(half, levels, link) for half in own_y) for link in range(1, chain)]
    kept_y, forwarded = lax.optimization_barrier((kept_y, forwarded))

    padded = {("state", 0): padded_y(own_y, sent)}
    if corrected[0]:
        padded["kept", 0, 1] = jnp.pad(kept[FIELDS:], ((0, 0), (0, 0), (LANES, LANES)))

    width = columns + 2 * LANES

    def over_x(kinds):
        pieces, _ = edge_layout(kinds)

        def edge(from_top):
            grid = {}
            for kind, parts in pieces.items():
                for distance, count, tiles, row, first_tile in parts:
                    start = rows - distance - count if from_top else distance
                    skip = (4 - tiles) // 2 * LANES
                    grid[row, first_tile] = padded[kind][:, start : start + count, skip : width - skip]
            parts = []
            for row, first_tile in sorted(grid):
                if first_tile:
                    continue
                part = grid[row, 0]
                if part.shape[2] < width:
                    part = jnp.concatenate([part, grid.get((row, 2), part)], axis=2)
                parts.append(part)
            return jnp.concatenate(parts, axis=1)

        return [half.astype(jnp.float32) for half in neighbours("gx", even_x, edge(False), edge(True))]

    early, late = edge_turns(chain, corrected)
    came = over_x(early)
    kept_y, forwarded = lax.optimization_barrier((kept_y, forwarded))
    operands = []
    for link in range(chain):
        if link:
            operands += [centers[link], *forwarded[link - 1]]
            padded["state", link] = padded_y(forwarded[link - 1], centers[link])
        if corrected[link]:
            if link:
                link_kept = from_lower(kept, levels, link)
                link_y = tuple(from_lower(half, levels, link) for half in kept_y)
                operands += [from_lower(stored, levels, link), *link_y]
            else:
                link_kept, link_y = kept, kept_y
                operands += [stored, *link_y]
            link_padded = padded_y(link_y, link_kept)
            padded["kept", link, 0] = link_padded[:FIELDS]
            if link:
                padded["kept", link, 1] = link_padded[FIELDS:]
    came += over_x(late)
    flags = jnp.stack([even_x.astype(jnp.int32), even_y.astype(jnp.int32), position])
    matrix = jnp.asarray(stencil_matrix(), jnp.bfloat16)
    high, tall = rows + WINDOW, rows + 2 * FIRST
    smem = pl.BlockSpec(memory_space=pltpu.SMEM)
    vmem = pl.BlockSpec(memory_space=pltpu.VMEM)
    params = pltpu.CompilerParams(vmem_limit_bytes=48 * 1024 * 1024)
    taken = max(edge_layout(kinds)[1] for kinds in (early, late))
    edges = 2, FIELDS, 4, -(-taken // 8) * 8, LANES
    begun = pl.pallas_call(
        functools.partial(first_kernel, chain, corrected, rows),
        out_shape=jax.ShapeDtypeStruct((FIELDS, 4, high, LANES), jnp.float32),
        in_specs=[smem] + [vmem] * 6,
        out_specs=vmem,
        scratch_shapes=[pltpu.VMEM(edges, jnp.float32), *scratch_of_level(rows)],
        compiler_params=params,
        name="own_first_tick",
    )(flags, matrix, *came[:2], whole, *own_y)
    operands = [begun, *came, *operands]
    result = pl.pallas_call(
        functools.partial(advance_kernel, chain, corrected, rows),
        out_shape=jax.ShapeDtypeStruct((FIELDS, rows, columns), jnp.float32),
        in_specs=[smem] + [vmem] * (len(operands) + 1),
        out_specs=vmem,
        scratch_shapes=[
            pltpu.VMEM((chain, TICKS, FIELDS, 4, high, LANES), jnp.float32),
            pltpu.VMEM((chain, TICKS, FIELDS, 4, tall, LANES), jnp.float32),
            pltpu.VMEM((2, *edges), jnp.float32),
            *(scratch_of_level(rows) * chain),
        ],
        compiler_params=params,
        name="advance",
    )(flags, matrix, *operands)
    return result[None]


def solution(mesh):
    return jax.shard_map(
        per_device,
        mesh=mesh,
        in_specs=(P("sec", None, "gx", "gy"), P("sec", None, None, "gx", "gy")),
        out_specs=P("sec", None, "gx", "gy"),
        check_vma=False,
    )
```

```python
import functools

import jax
import jax.numpy as jnp
import numpy as np
from jax import lax
from jax.experimental import pallas as pl
from jax.experimental.pallas import tpu as pltpu
from jax.sharding import PartitionSpec as P

NZ = 32
TICKS = 3


TIME_STEP = 0.04
DYNAMIC_FRICTION = 0.4
CONDUCTIVITY = 0.5
GAMMA_LESS = 0.4
QUAD_WEIGHTS = (1.0 / 24.0, -5.0 / 24.0, 19.0 / 24.0, 9.0 / 24.0)

LANES = 128
FIRST = 12
START = 8
WINDOW = 2 * (FIRST - START)
FIELDS = 5


def neighbours(axis, even, low_edge, high_edge):
    count = lax.axis_size(axis)
    if count % 2:
        from_next = lax.ppermute(low_edge, axis, [(i, (i - 1) % count) for i in range(count)])
        from_last = lax.ppermute(high_edge, axis, [(i, (i + 1) % count) for i in range(count)])
        return from_next, from_last
    if low_edge is high_edge:
        outward = inward = low_edge
    else:
        outward = jnp.where(even, high_edge, low_edge)
        inward = jnp.where(even, low_edge, high_edge)
    far = [(i, (i + 1) % count if i % 2 else (i - 1) % count) for i in range(count)]
    near = [(i, i + 1 if i % 2 == 0 else i - 1) for i in range(count)]
    second = lax.ppermute(inward, axis, far)
    first = lax.ppermute(outward, axis, near)
    return first, second


def from_lower(block, levels, distance):
    count = lax.axis_size("sec")
    route = []
    for start in range(0, count, levels):
        route += [(start + i, start + (i + distance) % levels) for i in range(levels)]
    return lax.ppermute(block, "sec", route)


def stencil_matrix():
    per_tile = LANES // NZ
    wide = 2 * LANES
    half = LANES // 2
    d_y = np.zeros((4 * LANES, wide), np.float32)
    d_z = np.zeros((wide, wide), np.float32)
    sweep = np.zeros((4 * LANES, wide), np.float32)
    for y in range(2 * per_tile):
        for z in range(NZ):
            column = y * NZ + z
            here = (y + per_tile) * NZ + z
            d_y[here + NZ, column] -= 1.0
            d_y[here - NZ, column] += 1.0
            d_z[y * NZ + (z + 1) % NZ, column] -= 1.0
            d_z[y * NZ + (z - 1) % NZ, column] += 1.0
            sweep[here, column] -= 6.0
            sweep[here + 2 * NZ, column] += 1.0
            sweep[here - 2 * NZ, column] += 1.0
            base = (y + per_tile) * NZ
            sweep[base + (z + 2) % NZ, column] += 1.0
            sweep[base + (z - 2) % NZ, column] += 1.0

    def inner(matrix):
        return matrix[LANES : 3 * LANES]

    def outer(matrix):
        return np.concatenate([matrix[3 * LANES : 3 * LANES + half], matrix[half:LANES]])

    return np.concatenate([inner(d_y), d_z, inner(sweep), outer(d_y), outer(sweep)], axis=0)


def lanes(tile):
    return pl.ds(tile * LANES, LANES)


def scratch_of_level(rows):
    high, tall = rows + WINDOW, rows + 2 * FIRST
    return [
        pltpu.VMEM((FIELDS, 6, tall, LANES), jnp.float32),
        pltpu.VMEM((FIELDS, 4, tall, LANES), jnp.float32),
        pltpu.VMEM((FIELDS - 1, 6, tall, LANES), jnp.float32),
        pltpu.VMEM((6, FIELDS * high, LANES), jnp.float32),
        pltpu.VMEM((4, FIELDS * high, LANES), jnp.float32),
    ]


def unpack_edges(edges, first, second, even_x):
    count = first.shape[1]
    for field in range(FIELDS):
        for tile in range(4):
            one = first[field, :, lanes(tile)]
            two = second[field, :, lanes(tile)]
            edges[0, field, tile, pl.ds(0, count), :] = jnp.where(even_x, two, one)
            edges[1, field, tile, pl.ds(0, count), :] = jnp.where(even_x, one, two)


def place_edges(target, edges, pieces, field, rows):
    for distance, count, tiles, row, first_tile in pieces:
        for tile in range(tiles):
            start = (4 - tiles) // 2 + tile
            came = field, first_tile + tile, pl.ds(row, count)
            target(start)[pl.ds(FIRST - distance - count, count), :] = edges[(0, *came)]
            target(start)[pl.ds(FIRST + rows + distance, count), :] = edges[(1, *came)]


class Level:
    def __init__(self, rows, even_x, even_y, matrix, scratch):
        self.rows, self.even_x, self.even_y, self.matrix = rows, even_x, even_y, matrix
        self.state, self.flow_x, self.slow, self.flow_y, self.flow_z = scratch
        self.high = rows + WINDOW
        self.window = pl.ds(START, self.high)

    def ordered(self, even, first, second):
        return jnp.where(even, second, first), jnp.where(even, first, second)

    def assemble(self, center, y_first, y_second, edges, pieces):
        rows = self.rows
        for field in range(FIELDS):
            rest = jnp.full((FIRST, LANES), (1.0, 0.0, 0.0, 0.0, 2.5)[field], jnp.float32)
            for tile in range(6):
                target = self.state.at[field, tile]
                if tile in (2, 3):
                    middle = center[field, :, lanes(tile - 2)].astype(jnp.float32)
                else:
                    one = y_first[field, :, lanes(tile % 2)].astype(jnp.float32)
                    two = y_second[field, :, lanes(tile % 2)].astype(jnp.float32)
                    middle = self.ordered(self.even_y, one, two)[tile // 4]
                target[pl.ds(FIRST, rows), :] = middle
                target[pl.ds(0, FIRST), :] = rest
                target[pl.ds(FIRST + rows, FIRST), :] = rest
            place_edges(lambda tile: self.state.at[field, tile + 1], edges, pieces, field, rows)

    def assemble_terms(self, terms, stored, y_first, y_second, edges, pieces):
        rows = self.rows
        none = jnp.zeros((FIRST, LANES), jnp.float32)
        for field in range(FIELDS):
            for tile in (1, 2):
                old = [stored[age, field, :, lanes(tile - 1)].astype(jnp.float32) for age in range(3)]
                for tick, term in enumerate(kept_terms(old)):
                    terms[tick, field, tile, pl.ds(FIRST, rows), :] = term
            for tick in range(2):
                one = y_first[tick * FIELDS + field].astype(jnp.float32)
                two = y_second[tick * FIELDS + field].astype(jnp.float32)
                low, top = self.ordered(self.even_y, one, two)
                terms[tick, field, 0, pl.ds(FIRST, rows), :] = low
                terms[tick, field, 3, pl.ds(FIRST, rows), :] = top
                for tile in range(4):
                    terms[tick, field, tile, pl.ds(0, FIRST), :] = none
                    terms[tick, field, tile, pl.ds(FIRST + rows, FIRST), :] = none
                place_edges(lambda tile: terms.at[tick, field, tile], edges[tick], pieces[tick], field, rows)

    def pointwise(self, state, tile, place, along=True, across=True):
        density, mom_x, mom_y, mom_z, energy = state
        inverse = 1.0 / density
        vel_x = mom_x * inverse
        vel_y = mom_y * inverse
        vel_z = mom_z * inverse
        xx, yy, zz = mom_x * vel_x, mom_y * vel_y, mom_z * vel_z
        moving = xx + yy + zz
        pressure = GAMMA_LESS * energy - (0.5 * GAMMA_LESS) * moving
        enthalpy = energy + pressure
        heat = ((0.25 * DYNAMIC_FRICTION) * moving + (0.5 * CONDUCTIVITY) * pressure) * inverse
        xy = mom_x * vel_y
        xz = mom_x * vel_z
        yz = mom_y * vel_z
        along_x = (mom_x, xx + pressure, xy, xz, enthalpy * vel_x)
        along_y = (mom_y, xy, yy + pressure, yz, enthalpy * vel_y)
        along_z = (mom_z, xz, yz, zz + pressure, enthalpy * vel_z)
        friction = 0.5 * DYNAMIC_FRICTION
        spread = (friction * vel_x, friction * vel_y, friction * vel_z, heat)
        for field in range(FIELDS):
            if along:
                self.flow_x[field, tile - 1, place, :] = along_x[field]
            if field:
                self.slow[field - 1, tile, place, :] = spread[field - 1]
            if across:
                rows = pl.ds(field * self.high, self.high)
                self.flow_y[tile, rows, :] = along_y[field]
                if along:
                    self.flow_z[tile - 1, rows, :] = along_z[field]

    def products(self, tick):
        last = tick == TICKS - 1
        inner = (2, 3) if last else (1, 2, 3, 4)
        for tile in inner:
            parts = [(START, True)] + ([(0, False), (START + self.high, False)] if tick == 0 else [])
            for start, across in parts:
                place = pl.ds(start, self.high if across else START)
                state = [self.state[field, tile, place, :] for field in range(FIELDS)]
                self.pointwise(state, tile, place, across=across)
        outer = {0: (0, 5), TICKS - 1: (1, 4)}.get(tick)
        if outer:
            above = lax.broadcasted_iota(jnp.int32, (self.high, LANES), 1) < LANES // 2
            pairs = [[self.state[field, tile, self.window, :] for tile in outer] for field in range(FIELDS)]
            state = [jnp.where(above, top, low) for low, top in pairs]
            self.pointwise(state, 0, self.window, along=False)
        none = jnp.zeros((self.high, LANES), jnp.float32)

        def flow_y(tile):
            if tile in inner:
                return self.flow_y[tile]
            return self.flow_y[0] if outer else jnp.concatenate([none] * FIELDS)

        def spreading(tile):
            tile = tile if tile in inner else 0
            kinds = range(FIELDS - 1)
            known = tile or outer
            return jnp.concatenate([none] + [self.slow[kind, tile, self.window, :] if known else none for kind in kinds])

        from_above = lax.broadcasted_iota(jnp.int32, (FIELDS * self.high, LANES), 1) < LANES // 2
        flow_z = self.flow_z
        found = {}
        for low, top in ((2, 3),) if last else ((1, 2), (3, 4)):
            if last:
                around = [flow_y(0), spreading(0)]
            else:
                around = [jnp.where(from_above, part(top + 1), part(low - 1)) for part in (flow_y, spreading)]
            parts = [
                flow_y(low),
                flow_y(top),
                flow_z[low - 1],
                flow_z[top - 1],
                spreading(low),
                spreading(top),
                *around,
            ]
            left = jnp.concatenate([part.astype(jnp.bfloat16) for part in parts], axis=1)
            found[low, top] = jnp.dot(left, self.matrix[...], preferred_element_type=jnp.float32)
        return found

    def along_x(self, field, tile):
        def shifted(ref, *index, step):
            return ref[(*index, pl.ds(START + step, self.high))]

        total = shifted(self.flow_x, field, tile - 1, step=-1) - shifted(self.flow_x, field, tile - 1, step=1)
        if field:
            kind = field - 1
            total = total + (shifted(self.slow, kind, tile, step=2) + shifted(self.slow, kind, tile, step=-2))
        return total

    def rates(self, found):
        for group, product in found.items():
            for field in range(FIELDS):
                for side, tile in enumerate(group):
                    start = field * self.high
                    part = product[start : start + self.high, side * LANES : (side + 1) * LANES]
                    yield field, tile, part + self.along_x(field, tile)


def edge_turns(chain, corrected):
    state = ((0, 4, True), (4, 2, False))
    terms = (((0, 2, True), (2, 2, False)), ((0, 2, False),))
    early = [(("state", 0), state)]
    late = []
    for link in range(chain):
        if link:
            late.append((("state", link), state))
        if corrected[link]:
            late.append((("kept", link, 0), terms[0]))
            (late if link else early).append((("kept", link, 1), terms[1]))
    return early, late


def edge_layout(kinds):
    sources = {}
    narrow = []
    row = 0
    for kind, pieces in kinds:
        for distance, count, wide in pieces:
            if wide:
                sources.setdefault(kind, []).append((distance, count, 4, row, 0))
                row += count
            else:
                narrow.append((kind, distance, count))
    for place, (kind, distance, count) in enumerate(narrow):
        sources.setdefault(kind, []).append((distance, count, 2, row + 2 * (place // 2), 2 * (place % 2)))
    return sources, row + 2 * ((len(narrow) + 1) // 2)


def first_kernel(chain, corrected, rows, *refs):
    flags, matrix, x_first, x_second, center, y_first, y_second, out, edges, *scratch = refs
    even_x = flags[0] == 1
    pieces, _ = edge_layout(edge_turns(chain, corrected)[0])
    unpack_edges(edges, x_first, x_second, even_x)
    level = Level(rows, even_x, flags[1] == 1, matrix, scratch)
    level.assemble(center, y_first, y_second, edges, pieces["state", 0])
    for field, tile, rate in level.rates(level.products(0)):
        out[field, tile - 1] = level.state[field, tile, level.window, :] + (0.5 * TIME_STEP) * rate


def advance_kernel(chain, corrected, rows, *refs):
    flags, matrix, begun, *refs = refs
    came, refs = refs[:4], refs[4:]
    inputs = []
    for link in range(chain):
        state, refs = (refs[:3], refs[3:]) if link else (None, refs)
        stored, refs = (refs[:3], refs[3:]) if corrected[link] else (None, refs)
        inputs.append((state, stored))
    out, fresh, terms, edges, *refs = refs
    even_x = flags[0] == 1
    position = flags[2]
    levels = [
        Level(rows, even_x, flags[1] == 1, matrix, refs[5 * link : 5 * link + 5]) for link in range(chain)
    ]
    window = levels[0].window
    layout = {}
    for turn, kinds in enumerate(edge_turns(chain, corrected)):
        pieces, _ = edge_layout(kinds)
        layout.update((kind, (edges.at[turn], parts)) for kind, parts in pieces.items())

    def correction(link, tick, field, tile):
        total = terms[link, tick, field, tile - 1, window, :] + QUAD_WEIGHTS[3] * fresh[link, tick, field, tile - 1]
        for age in range(tick):
            weight = QUAD_WEIGHTS[3 - tick + age] - (1.0 if age == tick - 1 else 0.0)
            total = total + weight * fresh[link, age, field, tile - 1]
        return jnp.where(position > link, total, 0.0) if link else total

    def advance(links):
        def begin(link):
            state, stored = inputs[link]
            if state is not None:
                levels[link].assemble(*state, *layout["state", link])

        def begin_terms(link):
            if corrected[link]:
                places = [layout["kept", link, tick] for tick in range(2)]
                levels[link].assemble_terms(terms.at[link], *inputs[link][1], *zip(*places))

        def update(link, tick, found):
            level = levels[link]
            fix = corrected[link] and links > 1
            if link == 0 and tick == 0:
                for field in range(FIELDS):
                    for tile in range(1, 5):
                        state = begun[field, tile - 1]
                        if fix:
                            state = state + TIME_STEP * correction(0, 0, field, tile)
                        level.state[field, tile, window, :] = state
                return
            for field, tile, rate in level.rates(found):
                if link:
                    fresh[link - 1, tick, field, tile - 1] = (0.5 * rate).astype(jnp.bfloat16).astype(jnp.float32)
                if link + tick >= TICKS:
                    continue
                state = level.state[field, tile, window, :] + (0.5 * TIME_STEP) * rate
                if fix:
                    state = state + TIME_STEP * correction(link, tick, field, tile)
                level.state[field, tile, window, :] = state
                if tick == TICKS - 1:
                    out[field, :, lanes(tile - 2)] = level.state[field, tile, pl.ds(FIRST, rows), :]

        waiting = {}

        def finish(link, tick):
            if (link, tick) in waiting:
                finish(link + 1, tick)
                update(link, tick, waiting.pop((link, tick)))

        if links > 1:
            for turn in range(2):
                unpack_edges(edges.at[turn], *came[2 * turn : 2 * turn + 2], even_x)
        for tick in range(TICKS):
            for link in reversed(range(min(links, TICKS - tick + 1))):
                if tick == 0:
                    begin(link)
                finish(link, tick - 1)
                waiting[link, tick] = levels[link].products(tick) if link or tick else None
                if tick == 0 and links > 1:
                    begin_terms(link)
        for link, tick in sorted(waiting, reverse=True):
            finish(link, tick)

    if chain == 1:
        advance(1)
    else:
        pl.when(position == 0)(lambda: advance(1))
        pl.when(position > 0)(lambda: advance(chain))


def kept_terms(old):
    first, second, third, _ = QUAD_WEIGHTS
    return (
        first * old[0] + second * old[1] + (third - 1.0) * old[2],
        first * old[1] + second * old[2],
        first * old[2],
    )


def per_device(fields, stored_rates):
    levels = min(4, lax.axis_size("sec"))
    position = lax.axis_index("sec") % levels
    even_x = lax.axis_index("gx") % 2 == 0 if lax.axis_size("gx") % 2 == 0 else jnp.bool_(True)
    even_y = lax.axis_index("gy") % 2 == 0 if lax.axis_size("gy") % 2 == 0 else jnp.bool_(True)
    block = fields[0]
    stored = stored_rates[0]
    rows, columns = block.shape[1:]
    chain = min(levels, TICKS + 1)
    corrected = [link < levels - 1 and link < TICKS for link in range(chain)]
    whole = lax.reduce_precision(block, 8, 22)
    sent = block.astype(jnp.bfloat16)
    whole, sent = lax.optimization_barrier((whole, sent))

    def padded_y(pair, center):
        first, second = pair
        low, top = jnp.where(even_y, second, first), jnp.where(even_y, first, second)
        return jnp.concatenate([low[:, :, -LANES:], center, top[:, :, :LANES]], axis=2)

    own_y = neighbours("gy", even_y, sent, sent)
    centers = [sent] + [from_lower(sent, levels, link) for link in range(1, chain)]
    kept = jnp.concatenate(kept_terms(stored.astype(jnp.float32))[:2], axis=0).astype(jnp.bfloat16)
    kept_y = neighbours("gy", even_y, kept[:, :, :LANES], kept[:, :, -LANES:])
    if chain > 1:
        first, centers = lax.optimization_barrier((own_y[0], centers))
        own_y = first, own_y[1]
    forwarded = [tuple(from_lower(half, levels, link) for half in own_y) for link in range(1, chain)]
    kept_y, forwarded = lax.optimization_barrier((kept_y, forwarded))

    padded = {("state", 0): padded_y(own_y, sent)}
    if corrected[0]:
        padded["kept", 0, 1] = jnp.pad(kept[FIELDS:], ((0, 0), (0, 0), (LANES, LANES)))

    width = columns + 2 * LANES

    def over_x(kinds):
        pieces, _ = edge_layout(kinds)

        def edge(from_top):
            grid = {}
            for kind, parts in pieces.items():
                for distance, count, tiles, row, first_tile in parts:
                    start = rows - distance - count if from_top else distance
                    skip = (4 - tiles) // 2 * LANES
                    grid[row, first_tile] = padded[kind][:, start : start + count, skip : width - skip]
            parts = []
            for row, first_tile in sorted(grid):
                if first_tile:
                    continue
                part = grid[row, 0]
                if part.shape[2] < width:
                    part = jnp.concatenate([part, grid.get((row, 2), part)], axis=2)
                parts.append(part)
            return jnp.concatenate(parts, axis=1)

        return [half.astype(jnp.float32) for half in neighbours("gx", even_x, edge(False), edge(True))]

    early, late = edge_turns(chain, corrected)
    came = over_x(early)
    kept_y, forwarded = lax.optimization_barrier((kept_y, forwarded))
    operands = []
    for link in range(chain):
        if link:
            operands += [centers[link], *forwarded[link - 1]]
            padded["state", link] = padded_y(forwarded[link - 1], centers[link])
        if corrected[link]:
            if link:
                link_kept = from_lower(kept, levels, link)
                link_y = tuple(from_lower(half, levels, link) for half in kept_y)
                operands += [from_lower(stored, levels, link), *link_y]
            else:
                link_kept, link_y = kept, kept_y
                operands += [stored, *link_y]
            link_padded = padded_y(link_y, link_kept)
            padded["kept", link, 0] = link_padded[:FIELDS]
            if link:
                padded["kept", link, 1] = link_padded[FIELDS:]
    came += over_x(late)
    flags = jnp.stack([even_x.astype(jnp.int32), even_y.astype(jnp.int32), position])
    matrix = jnp.asarray(stencil_matrix(), jnp.bfloat16)
    high, tall = rows + WINDOW, rows + 2 * FIRST
    smem = pl.BlockSpec(memory_space=pltpu.SMEM)
    vmem = pl.BlockSpec(memory_space=pltpu.VMEM)
    params = pltpu.CompilerParams(vmem_limit_bytes=48 * 1024 * 1024)
    taken = max(edge_layout(kinds)[1] for kinds in (early, late))
    edges = 2, FIELDS, 4, -(-taken // 8) * 8, LANES
    begun = pl.pallas_call(
        functools.partial(first_kernel, chain, corrected, rows),
        out_shape=jax.ShapeDtypeStruct((FIELDS, 4, high, LANES), jnp.float32),
        in_specs=[smem] + [vmem] * 6,
        out_specs=vmem,
        scratch_shapes=[pltpu.VMEM(edges, jnp.float32), *scratch_of_level(rows)],
        compiler_params=params,
        name="own_first_tick",
    )(flags, matrix, *came[:2], whole, *own_y)
    operands = [begun, *came, *operands]
    result = pl.pallas_call(
        functools.partial(advance_kernel, chain, corrected, rows),
        out_shape=jax.ShapeDtypeStruct((FIELDS, rows, columns), jnp.float32),
        in_specs=[smem] + [vmem] * (len(operands) + 1),
        out_specs=vmem,
        scratch_shapes=[
            pltpu.VMEM((chain, TICKS, FIELDS, 4, high, LANES), jnp.float32),
            pltpu.VMEM((chain, TICKS, FIELDS, 4, tall, LANES), jnp.float32),
            pltpu.VMEM((2, *edges), jnp.float32),
            *(scratch_of_level(rows) * chain),
        ],
        compiler_params=params,
        name="advance",
    )(flags, matrix, *operands)
    return result[None]


def solution(mesh):
    return jax.shard_map(
        per_device,
        mesh=mesh,
        in_specs=(P("sec", None, "gx", "gy"), P("sec", None, None, "gx", "gy")),
        out_specs=P("sec", None, "gx", "gy"),
        check_vma=False,
    )
```

```python
import functools

import jax
import jax.numpy as jnp
import numpy as np
from jax import lax
from jax.experimental import pallas as pl
from jax.experimental.pallas import tpu as pltpu
from jax.sharding import PartitionSpec as P

NZ = 32
TICKS = 3


TIME_STEP = 0.04
DYNAMIC_FRICTION = 0.4
CONDUCTIVITY = 0.5
GAMMA_LESS = 0.4
QUAD_WEIGHTS = (1.0 / 24.0, -5.0 / 24.0, 19.0 / 24.0, 9.0 / 24.0)

LANES = 128
FIRST = 12
START = 8
WINDOW = 2 * (FIRST - START)
FIELDS = 5


def neighbours(axis, even, low_edge, high_edge):
    count = lax.axis_size(axis)
    if count % 2:
        from_next = lax.ppermute(low_edge, axis, [(i, (i - 1) % count) for i in range(count)])
        from_last = lax.ppermute(high_edge, axis, [(i, (i + 1) % count) for i in range(count)])
        return from_next, from_last
    if low_edge is high_edge:
        outward = inward = low_edge
    else:
        outward = jnp.where(even, high_edge, low_edge)
        inward = jnp.where(even, low_edge, high_edge)
    far = [(i, (i + 1) % count if i % 2 else (i - 1) % count) for i in range(count)]
    near = [(i, i + 1 if i % 2 == 0 else i - 1) for i in range(count)]
    second = lax.ppermute(inward, axis, far)
    first = lax.ppermute(outward, axis, near)
    return first, second


def from_lower(block, levels, distance):
    count = lax.axis_size("sec")
    route = []
    for start in range(0, count, levels):
        route += [(start + i, start + (i + distance) % levels) for i in range(levels)]
    return lax.ppermute(block, "sec", route)


def stencil_matrix():
    per_tile = LANES // NZ
    wide = 2 * LANES
    half = LANES // 2
    d_y = np.zeros((4 * LANES, wide), np.float32)
    d_z = np.zeros((wide, wide), np.float32)
    sweep = np.zeros((4 * LANES, wide), np.float32)
    for y in range(2 * per_tile):
        for z in range(NZ):
            column = y * NZ + z
            here = (y + per_tile) * NZ + z
            d_y[here + NZ, column] -= 1.0
            d_y[here - NZ, column] += 1.0
            d_z[y * NZ + (z + 1) % NZ, column] -= 1.0
            d_z[y * NZ + (z - 1) % NZ, column] += 1.0
            sweep[here, column] -= 6.0
            sweep[here + 2 * NZ, column] += 1.0
            sweep[here - 2 * NZ, column] += 1.0
            base = (y + per_tile) * NZ
            sweep[base + (z + 2) % NZ, column] += 1.0
            sweep[base + (z - 2) % NZ, column] += 1.0

    def inner(matrix):
        return matrix[LANES : 3 * LANES]

    def outer(matrix):
        return np.concatenate([matrix[3 * LANES : 3 * LANES + half], matrix[half:LANES]])

    return np.concatenate([inner(d_y), d_z, inner(sweep), outer(d_y), outer(sweep)], axis=0)


def lanes(tile):
    return pl.ds(tile * LANES, LANES)


def scratch_of_level(rows):
    high, tall = rows + WINDOW, rows + 2 * FIRST
    return [
        pltpu.VMEM((FIELDS, 6, tall, LANES), jnp.float32),
        pltpu.VMEM((FIELDS, 4, tall, LANES), jnp.float32),
        pltpu.VMEM((FIELDS - 1, 6, tall, LANES), jnp.float32),
        pltpu.VMEM((6, FIELDS * high, LANES), jnp.float32),
        pltpu.VMEM((4, FIELDS * high, LANES), jnp.float32),
    ]


def unpack_edges(edges, first, second, even_x):
    count = first.shape[1]
    for field in range(FIELDS):
        for tile in range(4):
            one = first[field, :, lanes(tile)]
            two = second[field, :, lanes(tile)]
            edges[0, field, tile, pl.ds(0, count), :] = jnp.where(even_x, two, one)
            edges[1, field, tile, pl.ds(0, count), :] = jnp.where(even_x, one, two)


def place_edges(target, edges, pieces, field, rows):
    for distance, count, tiles, row, first_tile in pieces:
        for tile in range(tiles):
            start = (4 - tiles) // 2 + tile
            came = field, first_tile + tile, pl.ds(row, count)
            target(start)[pl.ds(FIRST - distance - count, count), :] = edges[(0, *came)]
            target(start)[pl.ds(FIRST + rows + distance, count), :] = edges[(1, *came)]


class Level:
    def __init__(self, rows, even_x, even_y, matrix, scratch):
        self.rows, self.even_x, self.even_y, self.matrix = rows, even_x, even_y, matrix
        self.state, self.flow_x, self.slow, self.flow_y, self.flow_z = scratch
        self.high = rows + WINDOW
        self.window = pl.ds(START, self.high)

    def ordered(self, even, first, second):
        return jnp.where(even, second, first), jnp.where(even, first, second)

    def assemble(self, center, y_first, y_second, edges, pieces):
        rows = self.rows
        for field in range(FIELDS):
            rest = jnp.full((FIRST, LANES), (1.0, 0.0, 0.0, 0.0, 2.5)[field], jnp.float32)
            for tile in range(6):
                target = self.state.at[field, tile]
                if tile in (2, 3):
                    middle = center[field, :, lanes(tile - 2)].astype(jnp.float32)
                else:
                    one = y_first[field, :, lanes(tile % 2)].astype(jnp.float32)
                    two = y_second[field, :, lanes(tile % 2)].astype(jnp.float32)
                    middle = self.ordered(self.even_y, one, two)[tile // 4]
                target[pl.ds(FIRST, rows), :] = middle
                target[pl.ds(0, FIRST), :] = rest
                target[pl.ds(FIRST + rows, FIRST), :] = rest
            place_edges(lambda tile: self.state.at[field, tile + 1], edges, pieces, field, rows)

    def assemble_terms(self, terms, stored, y_first, y_second, edges, pieces):
        rows = self.rows
        none = jnp.zeros((FIRST, LANES), jnp.float32)
        for field in range(FIELDS):
            for tile in (1, 2):
                old = [stored[age, field, :, lanes(tile - 1)].astype(jnp.float32) for age in range(3)]
                for tick, term in enumerate(kept_terms(old)):
                    terms[tick, field, tile, pl.ds(FIRST, rows), :] = term
            for tick in range(2):
                one = y_first[tick * FIELDS + field].astype(jnp.float32)
                two = y_second[tick * FIELDS + field].astype(jnp.float32)
                low, top = self.ordered(self.even_y, one, two)
                terms[tick, field, 0, pl.ds(FIRST, rows), :] = low
                terms[tick, field, 3, pl.ds(FIRST, rows), :] = top
                for tile in range(4):
                    terms[tick, field, tile, pl.ds(0, FIRST), :] = none
                    terms[tick, field, tile, pl.ds(FIRST + rows, FIRST), :] = none
                place_edges(lambda tile: terms.at[tick, field, tile], edges[tick], pieces[tick], field, rows)

    def pointwise(self, state, tile, place, along=True, across=True):
        density, mom_x, mom_y, mom_z, energy = state
        inverse = 1.0 / density
        vel_x = mom_x * inverse
        vel_y = mom_y * inverse
        vel_z = mom_z * inverse
        xx, yy, zz = mom_x * vel_x, mom_y * vel_y, mom_z * vel_z
        moving = xx + yy + zz
        pressure = GAMMA_LESS * energy - (0.5 * GAMMA_LESS) * moving
        enthalpy = energy + pressure
        heat = ((0.25 * DYNAMIC_FRICTION) * moving + (0.5 * CONDUCTIVITY) * pressure) * inverse
        xy = mom_x * vel_y
        xz = mom_x * vel_z
        yz = mom_y * vel_z
        along_x = (mom_x, xx + pressure, xy, xz, enthalpy * vel_x)
        along_y = (mom_y, xy, yy + pressure, yz, enthalpy * vel_y)
        along_z = (mom_z, xz, yz, zz + pressure, enthalpy * vel_z)
        friction = 0.5 * DYNAMIC_FRICTION
        spread = (friction * vel_x, friction * vel_y, friction * vel_z, heat)
        for field in range(FIELDS):
            if along:
                self.flow_x[field, tile - 1, place, :] = along_x[field]
            if field:
                self.slow[field - 1, tile, place, :] = spread[field - 1]
            if across:
                rows = pl.ds(field * self.high, self.high)
                self.flow_y[tile, rows, :] = along_y[field]
                if along:
                    self.flow_z[tile - 1, rows, :] = along_z[field]

    def products(self, tick):
        last = tick == TICKS - 1
        inner = (2, 3) if last else (1, 2, 3, 4)
        for tile in inner:
            parts = [(START, True)] + ([(0, False), (START + self.high, False)] if tick == 0 else [])
            for start, across in parts:
                place = pl.ds(start, self.high if across else START)
                state = [self.state[field, tile, place, :] for field in range(FIELDS)]
                self.pointwise(state, tile, place, across=across)
        outer = {0: (0, 5), TICKS - 1: (1, 4)}.get(tick)
        if outer:
            above = lax.broadcasted_iota(jnp.int32, (self.high, LANES), 1) < LANES // 2
            pairs = [[self.state[field, tile, self.window, :] for tile in outer] for field in range(FIELDS)]
            state = [jnp.where(above, top, low) for low, top in pairs]
            self.pointwise(state, 0, self.window, along=False)
        none = jnp.zeros((self.high, LANES), jnp.float32)

        def flow_y(tile):
            if tile in inner:
                return self.flow_y[tile]
            return self.flow_y[0] if outer else jnp.concatenate([none] * FIELDS)

        def spreading(tile):
            tile = tile if tile in inner else 0
            kinds = range(FIELDS - 1)
            known = tile or outer
            return jnp.concatenate([none] + [self.slow[kind, tile, self.window, :] if known else none for kind in kinds])

        from_above = lax.broadcasted_iota(jnp.int32, (FIELDS * self.high, LANES), 1) < LANES // 2
        flow_z = self.flow_z
        found = {}
        for low, top in ((2, 3),) if last else ((1, 2), (3, 4)):
            if last:
                around = [flow_y(0), spreading(0)]
            else:
                around = [jnp.where(from_above, part(top + 1), part(low - 1)) for part in (flow_y, spreading)]
            parts = [
                flow_y(low),
                flow_y(top),
                flow_z[low - 1],
                flow_z[top - 1],
                spreading(low),
                spreading(top),
                *around,
            ]
            left = jnp.concatenate([part.astype(jnp.bfloat16) for part in parts], axis=1)
            found[low, top] = jnp.dot(left, self.matrix[...], preferred_element_type=jnp.float32)
        return found

    def along_x(self, field, tile):
        def shifted(ref, *index, step):
            return ref[(*index, pl.ds(START + step, self.high))]

        total = shifted(self.flow_x, field, tile - 1, step=-1) - shifted(self.flow_x, field, tile - 1, step=1)
        if field:
            kind = field - 1
            total = total + (shifted(self.slow, kind, tile, step=2) + shifted(self.slow, kind, tile, step=-2))
        return total

    def rates(self, found):
        for group, product in found.items():
            for field in range(FIELDS):
                for side, tile in enumerate(group):
                    start = field * self.high
                    part = product[start : start + self.high, side * LANES : (side + 1) * LANES]
                    yield field, tile, part + self.along_x(field, tile)


def edge_turns(chain, corrected):
    state = ((0, 4, True), (4, 2, False))
    terms = (((0, 2, True), (2, 2, False)), ((0, 2, False),))
    early = [(("state", 0), state)]
    late = []
    for link in range(chain):
        if link:
            late.append((("state", link), state))
        if corrected[link]:
            late.append((("kept", link, 0), terms[0]))
            (late if link else early).append((("kept", link, 1), terms[1]))
    return early, late


def edge_layout(kinds):
    sources = {}
    narrow = []
    row = 0
    for kind, pieces in kinds:
        for distance, count, wide in pieces:
            if wide:
                sources.setdefault(kind, []).append((distance, count, 4, row, 0))
                row += count
            else:
                narrow.append((kind, distance, count))
    for place, (kind, distance, count) in enumerate(narrow):
        sources.setdefault(kind, []).append((distance, count, 2, row + 2 * (place // 2), 2 * (place % 2)))
    return sources, row + 2 * ((len(narrow) + 1) // 2)


def whereabouts():
    def even(axis):
        return lax.axis_index(axis) % 2 == 0 if lax.axis_size(axis) % 2 == 0 else jnp.bool_(True)

    return even("gx"), even("gy"), lax.axis_index("sec") % min(4, lax.axis_size("sec"))


def first_kernel(chain, corrected, rows, *refs):
    matrix, x_first, x_second, center, y_first, y_second, out, edges, *scratch = refs
    even_x, even_y, _ = whereabouts()
    pieces, _ = edge_layout(edge_turns(chain, corrected)[0])
    unpack_edges(edges, x_first, x_second, even_x)
    level = Level(rows, even_x, even_y, matrix, scratch)
    level.assemble(center, y_first, y_second, edges, pieces["state", 0])
    for field, tile, rate in level.rates(level.products(0)):
        out[field, tile - 1] = level.state[field, tile, level.window, :] + (0.5 * TIME_STEP) * rate


def advance_kernel(chain, corrected, rows, *refs):
    matrix, begun, *refs = refs
    came, refs = refs[:4], refs[4:]
    inputs = []
    for link in range(chain):
        state, refs = (refs[:3], refs[3:]) if link else (None, refs)
        stored, refs = (refs[:3], refs[3:]) if corrected[link] else (None, refs)
        inputs.append((state, stored))
    out, fresh, terms, edges, *refs = refs
    even_x, even_y, position = whereabouts()
    levels = [
        Level(rows, even_x, even_y, matrix, refs[5 * link : 5 * link + 5]) for link in range(chain)
    ]
    window = levels[0].window
    layout = {}
    for turn, kinds in enumerate(edge_turns(chain, corrected)):
        pieces, _ = edge_layout(kinds)
        layout.update((kind, (edges.at[turn], parts)) for kind, parts in pieces.items())

    def correction(link, tick, field, tile):
        total = terms[link, tick, field, tile - 1, window, :] + QUAD_WEIGHTS[3] * fresh[link, tick, field, tile - 1]
        for age in range(tick):
            weight = QUAD_WEIGHTS[3 - tick + age] - (1.0 if age == tick - 1 else 0.0)
            total = total + weight * fresh[link, age, field, tile - 1]
        return jnp.where(position > link, total, 0.0) if link else total

    def advance(links):
        def begin(link):
            state, stored = inputs[link]
            if state is not None:
                levels[link].assemble(*state, *layout["state", link])

        def begin_terms(link):
            if corrected[link]:
                places = [layout["kept", link, tick] for tick in range(2)]
                levels[link].assemble_terms(terms.at[link], *inputs[link][1], *zip(*places))

        def update(link, tick, found):
            level = levels[link]
            fix = corrected[link] and links > 1
            if link == 0 and tick == 0:
                for field in range(FIELDS):
                    for tile in range(1, 5):
                        state = begun[field, tile - 1]
                        if fix:
                            state = state + TIME_STEP * correction(0, 0, field, tile)
                        level.state[field, tile, window, :] = state
                return
            for field, tile, rate in level.rates(found):
                if link:
                    fresh[link - 1, tick, field, tile - 1] = (0.5 * rate).astype(jnp.bfloat16).astype(jnp.float32)
                if link + tick >= TICKS:
                    continue
                state = level.state[field, tile, window, :] + (0.5 * TIME_STEP) * rate
                if fix:
                    state = state + TIME_STEP * correction(link, tick, field, tile)
                level.state[field, tile, window, :] = state
                if tick == TICKS - 1:
                    out[field, :, lanes(tile - 2)] = level.state[field, tile, pl.ds(FIRST, rows), :]

        waiting = {}

        def finish(link, tick):
            if (link, tick) in waiting:
                finish(link + 1, tick)
                update(link, tick, waiting.pop((link, tick)))

        if links > 1:
            for turn in range(2):
                unpack_edges(edges.at[turn], *came[2 * turn : 2 * turn + 2], even_x)
        for tick in range(TICKS):
            for link in reversed(range(min(links, TICKS - tick + 1))):
                if tick == 0:
                    begin(link)
                finish(link, tick - 1)
                waiting[link, tick] = levels[link].products(tick) if link or tick else None
                if tick == 0 and links > 1:
                    begin_terms(link)
        for link, tick in sorted(waiting, reverse=True):
            finish(link, tick)

    if chain == 1:
        advance(1)
    else:
        pl.when(position == 0)(lambda: advance(1))
        pl.when(position > 0)(lambda: advance(chain))


def kept_terms(old):
    first, second, third, _ = QUAD_WEIGHTS
    return (
        first * old[0] + second * old[1] + (third - 1.0) * old[2],
        first * old[1] + second * old[2],
        first * old[2],
    )


def per_device(fields, stored_rates):
    levels = min(4, lax.axis_size("sec"))
    even_x, even_y, _ = whereabouts()
    block = fields[0]
    stored = stored_rates[0]
    rows, columns = block.shape[1:]
    chain = min(levels, TICKS + 1)
    corrected = [link < levels - 1 and link < TICKS for link in range(chain)]
    whole = lax.reduce_precision(block, 8, 22)
    sent = block.astype(jnp.bfloat16)
    whole, sent = lax.optimization_barrier((whole, sent))

    def padded_y(pair, center):
        first, second = pair
        low, top = jnp.where(even_y, second, first), jnp.where(even_y, first, second)
        return jnp.concatenate([low[:, :, -LANES:], center, top[:, :, :LANES]], axis=2)

    own_y = neighbours("gy", even_y, sent, sent)
    centers = [sent] + [from_lower(sent, levels, link) for link in range(1, chain)]
    kept = jnp.concatenate(kept_terms(stored.astype(jnp.float32))[:2], axis=0).astype(jnp.bfloat16)
    kept_y = neighbours("gy", even_y, kept[:, :, :LANES], kept[:, :, -LANES:])
    if chain > 1:
        first, centers = lax.optimization_barrier((own_y[0], centers))
        own_y = first, own_y[1]
    forwarded = [tuple(from_lower(half, levels, link) for half in own_y) for link in range(1, chain)]
    kept_y, forwarded = lax.optimization_barrier((kept_y, forwarded))

    padded = {("state", 0): padded_y(own_y, sent)}
    if corrected[0]:
        padded["kept", 0, 1] = jnp.pad(kept[FIELDS:], ((0, 0), (0, 0), (LANES, LANES)))

    width = columns + 2 * LANES

    def over_x(kinds):
        pieces, _ = edge_layout(kinds)

        def edge(from_top):
            grid = {}
            for kind, parts in pieces.items():
                for distance, count, tiles, row, first_tile in parts:
                    start = rows - distance - count if from_top else distance
                    skip = (4 - tiles) // 2 * LANES
                    grid[row, first_tile] = padded[kind][:, start : start + count, skip : width - skip]
            parts = []
            for row, first_tile in sorted(grid):
                if first_tile:
                    continue
                part = grid[row, 0]
                if part.shape[2] < width:
                    part = jnp.concatenate([part, grid.get((row, 2), part)], axis=2)
                parts.append(part)
            return jnp.concatenate(parts, axis=1)

        return [half.astype(jnp.float32) for half in neighbours("gx", even_x, edge(False), edge(True))]

    early, late = edge_turns(chain, corrected)
    came = over_x(early)
    kept_y, forwarded = lax.optimization_barrier((kept_y, forwarded))
    operands = []
    for link in range(chain):
        if link:
            operands += [centers[link], *forwarded[link - 1]]
            padded["state", link] = padded_y(forwarded[link - 1], centers[link])
        if corrected[link]:
            if link:
                link_kept = from_lower(kept, levels, link)
                link_y = tuple(from_lower(half, levels, link) for half in kept_y)
                operands += [from_lower(stored, levels, link), *link_y]
            else:
                link_kept, link_y = kept, kept_y
                operands += [stored, *link_y]
            link_padded = padded_y(link_y, link_kept)
            padded["kept", link, 0] = link_padded[:FIELDS]
            if link:
                padded["kept", link, 1] = link_padded[FIELDS:]
    came += over_x(late)
    matrix = jnp.asarray(stencil_matrix(), jnp.bfloat16)
    high, tall = rows + WINDOW, rows + 2 * FIRST
    vmem = pl.BlockSpec(memory_space=pltpu.VMEM)
    params = pltpu.CompilerParams(vmem_limit_bytes=48 * 1024 * 1024)
    taken = max(edge_layout(kinds)[1] for kinds in (early, late))
    edges = 2, FIELDS, 4, -(-taken // 8) * 8, LANES
    begun = pl.pallas_call(
        functools.partial(first_kernel, chain, corrected, rows),
        out_shape=jax.ShapeDtypeStruct((FIELDS, 4, high, LANES), jnp.float32),
        in_specs=[vmem] * 6,
        out_specs=vmem,
        scratch_shapes=[pltpu.VMEM(edges, jnp.float32), *scratch_of_level(rows)],
        compiler_params=params,
        cost_estimate=pl.CostEstimate(flops=4 * 10**8, bytes_accessed=10**6, transcendentals=0),
        name="own_first_tick",
    )(matrix, *came[:2], whole, *own_y)
    operands = [begun, *came, *operands]
    result = pl.pallas_call(
        functools.partial(advance_kernel, chain, corrected, rows),
        out_shape=jax.ShapeDtypeStruct((FIELDS, rows, columns), jnp.float32),
        in_specs=[vmem] * (len(operands) + 1),
        out_specs=vmem,
        scratch_shapes=[
            pltpu.VMEM((chain, TICKS, FIELDS, 4, high, LANES), jnp.float32),
            pltpu.VMEM((chain, TICKS, FIELDS, 4, tall, LANES), jnp.float32),
            pltpu.VMEM((2, *edges), jnp.float32),
            *(scratch_of_level(rows) * chain),
        ],
        compiler_params=params,
        name="advance",
    )(matrix, *operands)
    return result[None]


def solution(mesh):
    return jax.shard_map(
        per_device,
        mesh=mesh,
        in_specs=(P("sec", None, "gx", "gy"), P("sec", None, None, "gx", "gy")),
        out_specs=P("sec", None, "gx", "gy"),
        check_vma=False,
    )
```

```python
import functools

import jax
import jax.numpy as jnp
import numpy as np
from jax import lax
from jax.experimental import pallas as pl
from jax.experimental.pallas import tpu as pltpu
from jax.sharding import PartitionSpec as P

NZ = 32
TICKS = 3


TIME_STEP = 0.04
DYNAMIC_FRICTION = 0.4
CONDUCTIVITY = 0.5
GAMMA_LESS = 0.4
QUAD_WEIGHTS = (1.0 / 24.0, -5.0 / 24.0, 19.0 / 24.0, 9.0 / 24.0)

LANES = 128
FIRST = 12
START = 8
WINDOW = 2 * (FIRST - START)
FIELDS = 5


def neighbours(axis, even, low_edge, high_edge):
    count = lax.axis_size(axis)
    if count % 2:
        from_next = lax.ppermute(low_edge, axis, [(i, (i - 1) % count) for i in range(count)])
        from_last = lax.ppermute(high_edge, axis, [(i, (i + 1) % count) for i in range(count)])
        return from_next, from_last
    if low_edge is high_edge:
        outward = inward = low_edge
    else:
        outward = jnp.where(even, high_edge, low_edge)
        inward = jnp.where(even, low_edge, high_edge)
    far = [(i, (i + 1) % count if i % 2 else (i - 1) % count) for i in range(count)]
    near = [(i, i + 1 if i % 2 == 0 else i - 1) for i in range(count)]
    second = lax.ppermute(inward, axis, far)
    first = lax.ppermute(outward, axis, near)
    return first, second


def from_lower(block, levels, distance):
    count = lax.axis_size("sec")
    route = []
    for start in range(0, count, levels):
        route += [(start + i, start + (i + distance) % levels) for i in range(levels)]
    return lax.ppermute(block, "sec", route)


def stencil_matrix():
    per_tile = LANES // NZ
    wide = 2 * LANES
    half = LANES // 2
    d_y = np.zeros((4 * LANES, wide), np.float32)
    d_z = np.zeros((wide, wide), np.float32)
    sweep = np.zeros((4 * LANES, wide), np.float32)
    for y in range(2 * per_tile):
        for z in range(NZ):
            column = y * NZ + z
            here = (y + per_tile) * NZ + z
            d_y[here + NZ, column] -= 1.0
            d_y[here - NZ, column] += 1.0
            d_z[y * NZ + (z + 1) % NZ, column] -= 1.0
            d_z[y * NZ + (z - 1) % NZ, column] += 1.0
            sweep[here, column] -= 6.0
            sweep[here + 2 * NZ, column] += 1.0
            sweep[here - 2 * NZ, column] += 1.0
            base = (y + per_tile) * NZ
            sweep[base + (z + 2) % NZ, column] += 1.0
            sweep[base + (z - 2) % NZ, column] += 1.0

    def inner(matrix):
        return matrix[LANES : 3 * LANES]

    def outer(matrix):
        return np.concatenate([matrix[3 * LANES : 3 * LANES + half], matrix[half:LANES]])

    return np.concatenate([inner(d_y), d_z, inner(sweep), outer(d_y), outer(sweep)], axis=0)


def lanes(tile):
    return pl.ds(tile * LANES, LANES)


def scratch_of_level(rows):
    high, tall = rows + WINDOW, rows + 2 * FIRST
    return [
        pltpu.VMEM((FIELDS, 6, tall, LANES), jnp.float32),
        pltpu.VMEM((FIELDS, 4, tall, LANES), jnp.float32),
        pltpu.VMEM((FIELDS - 1, 6, tall, LANES), jnp.float32),
        pltpu.VMEM((6, FIELDS * high, LANES), jnp.float32),
        pltpu.VMEM((4, FIELDS * high, LANES), jnp.float32),
    ]


def unpack_edges(edges, first, second, even_x):
    count = first.shape[1]
    for field in range(FIELDS):
        for tile in range(4):
            one = first[field, :, lanes(tile)]
            two = second[field, :, lanes(tile)]
            edges[0, field, tile, pl.ds(0, count), :] = jnp.where(even_x, two, one)
            edges[1, field, tile, pl.ds(0, count), :] = jnp.where(even_x, one, two)


def place_edges(target, edges, pieces, field, rows):
    for distance, count, tiles, row, first_tile in pieces:
        for tile in range(tiles):
            start = (4 - tiles) // 2 + tile
            came = field, first_tile + tile, pl.ds(row, count)
            target(start)[pl.ds(FIRST - distance - count, count), :] = edges[(0, *came)]
            target(start)[pl.ds(FIRST + rows + distance, count), :] = edges[(1, *came)]


class Level:
    def __init__(self, rows, even_x, even_y, matrix, scratch):
        self.rows, self.even_x, self.even_y, self.matrix = rows, even_x, even_y, matrix
        self.state, self.flow_x, self.slow, self.flow_y, self.flow_z = scratch
        self.high = rows + WINDOW
        self.window = pl.ds(START, self.high)

    def ordered(self, even, first, second):
        return jnp.where(even, second, first), jnp.where(even, first, second)

    def assemble(self, center, y_first, y_second, edges, pieces):
        rows = self.rows
        for field in range(FIELDS):
            rest = jnp.full((FIRST, LANES), (1.0, 0.0, 0.0, 0.0, 2.5)[field], jnp.float32)
            for tile in range(6):
                target = self.state.at[field, tile]
                if tile in (2, 3):
                    middle = center[field, :, lanes(tile - 2)].astype(jnp.float32)
                else:
                    one = y_first[field, :, lanes(tile % 2)].astype(jnp.float32)
                    two = y_second[field, :, lanes(tile % 2)].astype(jnp.float32)
                    middle = self.ordered(self.even_y, one, two)[tile // 4]
                target[pl.ds(FIRST, rows), :] = middle
                target[pl.ds(0, FIRST), :] = rest
                target[pl.ds(FIRST + rows, FIRST), :] = rest
            place_edges(lambda tile: self.state.at[field, tile + 1], edges, pieces, field, rows)

    def assemble_terms(self, terms, stored, y_first, y_second, edges, pieces):
        rows = self.rows
        none = jnp.zeros((FIRST, LANES), jnp.float32)
        for field in range(FIELDS):
            for tile in (1, 2):
                old = [stored[age, field, :, lanes(tile - 1)].astype(jnp.float32) for age in range(3)]
                for tick, term in enumerate(kept_terms(old)):
                    terms[tick, field, tile, pl.ds(FIRST, rows), :] = term
            for tick in range(2):
                one = y_first[tick * FIELDS + field].astype(jnp.float32)
                two = y_second[tick * FIELDS + field].astype(jnp.float32)
                low, top = self.ordered(self.even_y, one, two)
                terms[tick, field, 0, pl.ds(FIRST, rows), :] = low
                terms[tick, field, 3, pl.ds(FIRST, rows), :] = top
                for tile in range(4):
                    terms[tick, field, tile, pl.ds(0, FIRST), :] = none
                    terms[tick, field, tile, pl.ds(FIRST + rows, FIRST), :] = none
                place_edges(lambda tile: terms.at[tick, field, tile], edges[tick], pieces[tick], field, rows)

    def pointwise(self, state, tile, place, along=True, across=True):
        density, mom_x, mom_y, mom_z, energy = state
        inverse = 1.0 / density
        vel_x = mom_x * inverse
        vel_y = mom_y * inverse
        vel_z = mom_z * inverse
        xx, yy, zz = mom_x * vel_x, mom_y * vel_y, mom_z * vel_z
        moving = xx + yy + zz
        pressure = GAMMA_LESS * energy - (0.5 * GAMMA_LESS) * moving
        enthalpy = energy + pressure
        heat = ((0.25 * DYNAMIC_FRICTION) * moving + (0.5 * CONDUCTIVITY) * pressure) * inverse
        xy = mom_x * vel_y
        xz = mom_x * vel_z
        yz = mom_y * vel_z
        along_x = (mom_x, xx + pressure, xy, xz, enthalpy * vel_x)
        along_y = (mom_y, xy, yy + pressure, yz, enthalpy * vel_y)
        along_z = (mom_z, xz, yz, zz + pressure, enthalpy * vel_z)
        friction = 0.5 * DYNAMIC_FRICTION
        spread = (friction * vel_x, friction * vel_y, friction * vel_z, heat)
        for field in range(FIELDS):
            if along:
                self.flow_x[field, tile - 1, place, :] = along_x[field]
            if field:
                self.slow[field - 1, tile, place, :] = spread[field - 1]
            if across:
                rows = pl.ds(field * self.high, self.high)
                self.flow_y[tile, rows, :] = along_y[field]
                if along:
                    self.flow_z[tile - 1, rows, :] = along_z[field]

    def products(self, tick):
        last = tick == TICKS - 1
        inner = (2, 3) if last else (1, 2, 3, 4)
        for tile in inner:
            parts = [(START, True)] + ([(0, False), (START + self.high, False)] if tick == 0 else [])
            for start, across in parts:
                place = pl.ds(start, self.high if across else START)
                state = [self.state[field, tile, place, :] for field in range(FIELDS)]
                self.pointwise(state, tile, place, across=across)
        outer = {0: (0, 5), TICKS - 1: (1, 4)}.get(tick)
        if outer:
            above = lax.broadcasted_iota(jnp.int32, (self.high, LANES), 1) < LANES // 2
            pairs = [[self.state[field, tile, self.window, :] for tile in outer] for field in range(FIELDS)]
            state = [jnp.where(above, top, low) for low, top in pairs]
            self.pointwise(state, 0, self.window, along=False)
        none = jnp.zeros((self.high, LANES), jnp.float32)

        def flow_y(tile):
            if tile in inner:
                return self.flow_y[tile]
            return self.flow_y[0] if outer else jnp.concatenate([none] * FIELDS)

        def spreading(tile):
            tile = tile if tile in inner else 0
            kinds = range(FIELDS - 1)
            known = tile or outer
            return jnp.concatenate([none] + [self.slow[kind, tile, self.window, :] if known else none for kind in kinds])

        from_above = lax.broadcasted_iota(jnp.int32, (FIELDS * self.high, LANES), 1) < LANES // 2
        flow_z = self.flow_z
        found = {}
        for low, top in ((2, 3),) if last else ((1, 2), (3, 4)):
            if last:
                around = [flow_y(0), spreading(0)]
            else:
                around = [jnp.where(from_above, part(top + 1), part(low - 1)) for part in (flow_y, spreading)]
            parts = [
                flow_y(low),
                flow_y(top),
                flow_z[low - 1],
                flow_z[top - 1],
                spreading(low),
                spreading(top),
                *around,
            ]
            left = jnp.concatenate([part.astype(jnp.bfloat16) for part in parts], axis=1)
            found[low, top] = jnp.dot(left, self.matrix[...], preferred_element_type=jnp.float32)
        return found

    def along_x(self, field, tile):
        def shifted(ref, *index, step):
            return ref[(*index, pl.ds(START + step, self.high))]

        total = shifted(self.flow_x, field, tile - 1, step=-1) - shifted(self.flow_x, field, tile - 1, step=1)
        if field:
            kind = field - 1
            total = total + (shifted(self.slow, kind, tile, step=2) + shifted(self.slow, kind, tile, step=-2))
        return total

    def rates(self, found):
        for group, product in found.items():
            for field in range(FIELDS):
                for side, tile in enumerate(group):
                    start = field * self.high
                    part = product[start : start + self.high, side * LANES : (side + 1) * LANES]
                    yield field, tile, part + self.along_x(field, tile)


def edge_turns(chain, corrected):
    state = ((0, 4, True), (4, 2, False))
    terms = (((0, 2, True), (2, 2, False)), ((0, 2, False),))
    early = [(("state", 0), state)]
    late = []
    for link in range(chain):
        if link:
            late.append((("state", link), state))
        if corrected[link]:
            late.append((("kept", link, 0), terms[0]))
            (late if link else early).append((("kept", link, 1), terms[1]))
    return early, late


def edge_layout(kinds):
    sources = {}
    narrow = []
    row = 0
    for kind, pieces in kinds:
        for distance, count, wide in pieces:
            if wide:
                sources.setdefault(kind, []).append((distance, count, 4, row, 0))
                row += count
            else:
                narrow.append((kind, distance, count))
    for place, (kind, distance, count) in enumerate(narrow):
        sources.setdefault(kind, []).append((distance, count, 2, row + 2 * (place // 2), 2 * (place % 2)))
    return sources, row + 2 * ((len(narrow) + 1) // 2)


def whereabouts():
    def even(axis):
        return lax.axis_index(axis) % 2 == 0 if lax.axis_size(axis) % 2 == 0 else jnp.bool_(True)

    return even("gx"), even("gy"), lax.axis_index("sec") % min(4, lax.axis_size("sec"))


def first_kernel(chain, corrected, rows, *refs):
    matrix, x_first, x_second, center, y_first, y_second, out, edges, *scratch = refs
    even_x, even_y, _ = whereabouts()
    pieces, _ = edge_layout(edge_turns(chain, corrected)[0])
    unpack_edges(edges, x_first, x_second, even_x)
    level = Level(rows, even_x, even_y, matrix, scratch)
    level.assemble(center, y_first, y_second, edges, pieces["state", 0])
    for field, tile, rate in level.rates(level.products(0)):
        out[field, tile - 1] = level.state[field, tile, level.window, :] + (0.5 * TIME_STEP) * rate


def advance_kernel(chain, corrected, rows, *refs):
    matrix, begun, *refs = refs
    came, refs = refs[:4], refs[4:]
    inputs = []
    for link in range(chain):
        state, refs = (refs[:3], refs[3:]) if link else (None, refs)
        stored, refs = (refs[:3], refs[3:]) if corrected[link] else (None, refs)
        inputs.append((state, stored))
    out, fresh, terms, edges, *refs = refs
    even_x, even_y, position = whereabouts()
    levels = [
        Level(rows, even_x, even_y, matrix, refs[5 * link : 5 * link + 5]) for link in range(chain)
    ]
    window = levels[0].window
    layout = {}
    for turn, kinds in enumerate(edge_turns(chain, corrected)):
        pieces, _ = edge_layout(kinds)
        layout.update((kind, (edges.at[turn], parts)) for kind, parts in pieces.items())

    def correction(link, tick, field, tile):
        total = terms[link, tick, field, tile - 1, window, :] + QUAD_WEIGHTS[3] * fresh[link, tick, field, tile - 1]
        for age in range(tick):
            weight = QUAD_WEIGHTS[3 - tick + age] - (1.0 if age == tick - 1 else 0.0)
            total = total + weight * fresh[link, age, field, tile - 1]
        return jnp.where(position > link, total, 0.0) if link else total

    def advance(links):
        def begin(link):
            state, stored = inputs[link]
            if state is not None:
                levels[link].assemble(*state, *layout["state", link])

        def begin_terms(link):
            if corrected[link]:
                places = [layout["kept", link, tick] for tick in range(2)]
                levels[link].assemble_terms(terms.at[link], *inputs[link][1], *zip(*places))

        def update(link, tick, found):
            level = levels[link]
            fix = corrected[link] and links > 1
            if link == 0 and tick == 0:
                for field in range(FIELDS):
                    for tile in range(1, 5):
                        state = begun[field, tile - 1]
                        if fix:
                            state = state + TIME_STEP * correction(0, 0, field, tile)
                        level.state[field, tile, window, :] = state
                return
            for field, tile, rate in level.rates(found):
                if link:
                    fresh[link - 1, tick, field, tile - 1] = (0.5 * rate).astype(jnp.bfloat16).astype(jnp.float32)
                if link + tick >= TICKS:
                    continue
                state = level.state[field, tile, window, :] + (0.5 * TIME_STEP) * rate
                if fix:
                    state = state + TIME_STEP * correction(link, tick, field, tile)
                level.state[field, tile, window, :] = state
                if tick == TICKS - 1:
                    out[field, :, lanes(tile - 2)] = level.state[field, tile, pl.ds(FIRST, rows), :]

        waiting = {}

        def finish(link, tick):
            if (link, tick) in waiting:
                finish(link + 1, tick)
                update(link, tick, waiting.pop((link, tick)))

        if links > 1:
            for turn in range(2):
                unpack_edges(edges.at[turn], *came[2 * turn : 2 * turn + 2], even_x)
        for tick in range(TICKS):
            for link in reversed(range(min(links, TICKS - tick + 1))):
                if tick == 0:
                    begin(link)
                finish(link, tick - 1)
                waiting[link, tick] = levels[link].products(tick) if link or tick else None
                if tick == 0 and links > 1:
                    begin_terms(link)
        for link, tick in sorted(waiting, reverse=True):
            finish(link, tick)

    if chain == 1:
        advance(1)
    else:
        pl.when(position == 0)(lambda: advance(1))
        pl.when(position > 0)(lambda: advance(chain))


def kept_terms(old):
    first, second, third, _ = QUAD_WEIGHTS
    return (
        first * old[0] + second * old[1] + (third - 1.0) * old[2],
        first * old[1] + second * old[2],
        first * old[2],
    )


def per_device(fields, stored_rates):
    levels = min(4, lax.axis_size("sec"))
    even_x, even_y, _ = whereabouts()
    block = fields[0]
    stored = stored_rates[0]
    rows, columns = block.shape[1:]
    chain = min(levels, TICKS + 1)
    corrected = [link < levels - 1 and link < TICKS for link in range(chain)]
    whole = lax.reduce_precision(block, 8, 22)
    sent = block.astype(jnp.bfloat16)
    whole, sent = lax.optimization_barrier((whole, sent))

    def padded_y(pair, center):
        first, second = pair
        low, top = jnp.where(even_y, second, first), jnp.where(even_y, first, second)
        return jnp.concatenate([low[:, :, -LANES:], center, top[:, :, :LANES]], axis=2)

    own_y = neighbours("gy", even_y, sent, sent)
    centers = [sent] + [from_lower(sent, levels, link) for link in range(1, chain)]
    kept = jnp.concatenate(kept_terms(stored.astype(jnp.float32))[:2], axis=0).astype(jnp.bfloat16)
    kept_y = neighbours("gy", even_y, kept[:, :, :LANES], kept[:, :, -LANES:])
    if chain > 1:
        first, centers = lax.optimization_barrier((own_y[0], centers))
        own_y = first, own_y[1]
    forwarded = [tuple(from_lower(half, levels, link) for half in own_y) for link in range(1, chain)]
    kept_y, forwarded = lax.optimization_barrier((kept_y, forwarded))

    padded = {("state", 0): padded_y(own_y, sent)}
    if corrected[0]:
        padded["kept", 0, 1] = jnp.pad(kept[FIELDS:], ((0, 0), (0, 0), (LANES, LANES)))

    width = columns + 2 * LANES

    def over_x(kinds):
        pieces, _ = edge_layout(kinds)

        def edge(from_top):
            grid = {}
            for kind, parts in pieces.items():
                for distance, count, tiles, row, first_tile in parts:
                    start = rows - distance - count if from_top else distance
                    skip = (4 - tiles) // 2 * LANES
                    grid[row, first_tile] = padded[kind][:, start : start + count, skip : width - skip]
            parts = []
            for row, first_tile in sorted(grid):
                if first_tile:
                    continue
                part = grid[row, 0]
                if part.shape[2] < width:
                    part = jnp.concatenate([part, grid.get((row, 2), part)], axis=2)
                parts.append(part)
            return jnp.concatenate(parts, axis=1)

        return [half.astype(jnp.float32) for half in neighbours("gx", even_x, edge(False), edge(True))]

    early, late = edge_turns(chain, corrected)
    came = over_x(early)
    if chain > 1:
        kept_y, from_far = lax.optimization_barrier((kept_y, [pair[1] for pair in forwarded]))
        forwarded = [(pair[0], far) for pair, far in zip(forwarded, from_far)]
    operands = []
    for link in range(chain):
        if link:
            operands += [centers[link], *forwarded[link - 1]]
            padded["state", link] = padded_y(forwarded[link - 1], centers[link])
        if corrected[link]:
            if link:
                link_kept = from_lower(kept, levels, link)
                link_y = tuple(from_lower(half, levels, link) for half in kept_y)
                operands += [from_lower(stored, levels, link), *link_y]
            else:
                link_kept, link_y = kept, kept_y
                operands += [stored, *link_y]
            link_padded = padded_y(link_y, link_kept)
            padded["kept", link, 0] = link_padded[:FIELDS]
            if link:
                padded["kept", link, 1] = link_padded[FIELDS:]
    came += over_x(late)
    matrix = jnp.asarray(stencil_matrix(), jnp.bfloat16)
    high, tall = rows + WINDOW, rows + 2 * FIRST
    vmem = pl.BlockSpec(memory_space=pltpu.VMEM)
    params = pltpu.CompilerParams(vmem_limit_bytes=48 * 1024 * 1024)
    taken = max(edge_layout(kinds)[1] for kinds in (early, late))
    edges = 2, FIELDS, 4, -(-taken // 8) * 8, LANES
    begun = pl.pallas_call(
        functools.partial(first_kernel, chain, corrected, rows),
        out_shape=jax.ShapeDtypeStruct((FIELDS, 4, high, LANES), jnp.float32),
        in_specs=[vmem] * 6,
        out_specs=vmem,
        scratch_shapes=[pltpu.VMEM(edges, jnp.float32), *scratch_of_level(rows)],
        compiler_params=params,
        cost_estimate=pl.CostEstimate(flops=4 * 10**8, bytes_accessed=10**6, transcendentals=0),
        name="own_first_tick",
    )(matrix, *came[:2], whole, *own_y)
    operands = [begun, *came, *operands]
    result = pl.pallas_call(
        functools.partial(advance_kernel, chain, corrected, rows),
        out_shape=jax.ShapeDtypeStruct((FIELDS, rows, columns), jnp.float32),
        in_specs=[vmem] * (len(operands) + 1),
        out_specs=vmem,
        scratch_shapes=[
            pltpu.VMEM((chain, TICKS, FIELDS, 4, high, LANES), jnp.float32),
            pltpu.VMEM((chain, TICKS, FIELDS, 4, tall, LANES), jnp.float32),
            pltpu.VMEM((2, *edges), jnp.float32),
            *(scratch_of_level(rows) * chain),
        ],
        compiler_params=params,
        name="advance",
    )(matrix, *operands)
    return result[None]


def solution(mesh):
    return jax.shard_map(
        per_device,
        mesh=mesh,
        in_specs=(P("sec", None, "gx", "gy"), P("sec", None, None, "gx", "gy")),
        out_specs=P("sec", None, "gx", "gy"),
        check_vma=False,
    )
```

```python
import functools

import jax
import jax.numpy as jnp
import numpy as np
from jax import lax
from jax.experimental import pallas as pl
from jax.experimental.pallas import tpu as pltpu
from jax.sharding import PartitionSpec as P

NZ = 32
TICKS = 3


TIME_STEP = 0.04
DYNAMIC_FRICTION = 0.4
CONDUCTIVITY = 0.5
GAMMA_LESS = 0.4
QUAD_WEIGHTS = (1.0 / 24.0, -5.0 / 24.0, 19.0 / 24.0, 9.0 / 24.0)

LANES = 128
FIRST = 12
START = 8
WINDOW = 2 * (FIRST - START)
FIELDS = 5


def neighbours(axis, even, low_edge, high_edge):
    count = lax.axis_size(axis)
    if count % 2:
        from_next = lax.ppermute(low_edge, axis, [(i, (i - 1) % count) for i in range(count)])
        from_last = lax.ppermute(high_edge, axis, [(i, (i + 1) % count) for i in range(count)])
        return from_next, from_last
    if low_edge is high_edge:
        outward = inward = low_edge
    else:
        outward = jnp.where(even, high_edge, low_edge)
        inward = jnp.where(even, low_edge, high_edge)
    far = [(i, (i + 1) % count if i % 2 else (i - 1) % count) for i in range(count)]
    near = [(i, i + 1 if i % 2 == 0 else i - 1) for i in range(count)]
    second = lax.ppermute(inward, axis, far)
    first = lax.ppermute(outward, axis, near)
    return first, second


def from_lower(block, levels, distance):
    count = lax.axis_size("sec")
    route = []
    for start in range(0, count, levels):
        route += [(start + i, start + (i + distance) % levels) for i in range(levels)]
    return lax.ppermute(block, "sec", route)


def stencil_matrix():
    per_tile = LANES // NZ
    wide = 2 * LANES
    half = LANES // 2
    d_y = np.zeros((4 * LANES, wide), np.float32)
    d_z = np.zeros((wide, wide), np.float32)
    sweep = np.zeros((4 * LANES, wide), np.float32)
    for y in range(2 * per_tile):
        for z in range(NZ):
            column = y * NZ + z
            here = (y + per_tile) * NZ + z
            d_y[here + NZ, column] -= 1.0
            d_y[here - NZ, column] += 1.0
            d_z[y * NZ + (z + 1) % NZ, column] -= 1.0
            d_z[y * NZ + (z - 1) % NZ, column] += 1.0
            sweep[here, column] -= 6.0
            sweep[here + 2 * NZ, column] += 1.0
            sweep[here - 2 * NZ, column] += 1.0
            base = (y + per_tile) * NZ
            sweep[base + (z + 2) % NZ, column] += 1.0
            sweep[base + (z - 2) % NZ, column] += 1.0

    def inner(matrix):
        return matrix[LANES : 3 * LANES]

    def outer(matrix):
        return np.concatenate([matrix[3 * LANES : 3 * LANES + half], matrix[half:LANES]])

    return np.concatenate([inner(d_y), d_z, inner(sweep), outer(d_y), outer(sweep)], axis=0)


def lanes(tile):
    return pl.ds(tile * LANES, LANES)


def scratch_of_level(rows):
    high, tall = rows + WINDOW, rows + 2 * FIRST
    return [
        pltpu.VMEM((FIELDS, 6, tall, LANES), jnp.float32),
        pltpu.VMEM((FIELDS, 4, tall, LANES), jnp.float32),
        pltpu.VMEM((FIELDS - 1, 6, tall, LANES), jnp.float32),
        pltpu.VMEM((6, FIELDS * high, LANES), jnp.float32),
        pltpu.VMEM((4, FIELDS * high, LANES), jnp.float32),
    ]


def unpack_edges(edges, first, second, even_x, tiles=range(4)):
    count = first.shape[1]
    for field in range(FIELDS):
        for tile in tiles:
            one = first[field, :, lanes(tile)]
            two = second[field, :, lanes(tile)]
            edges[0, field, tile, pl.ds(0, count), :] = jnp.where(even_x, two, one)
            edges[1, field, tile, pl.ds(0, count), :] = jnp.where(even_x, one, two)


def place_edges(target, edges, pieces, field, rows):
    for distance, count, tiles, row, first_tile in pieces:
        for tile in range(tiles):
            start = (4 - tiles) // 2 + tile
            came = field, first_tile + tile, pl.ds(row, count)
            target(start)[pl.ds(FIRST - distance - count, count), :] = edges[(0, *came)]
            target(start)[pl.ds(FIRST + rows + distance, count), :] = edges[(1, *came)]


class Level:
    def __init__(self, rows, even_x, even_y, matrix, scratch):
        self.rows, self.even_x, self.even_y, self.matrix = rows, even_x, even_y, matrix
        self.state, self.flow_x, self.slow, self.flow_y, self.flow_z = scratch
        self.high = rows + WINDOW
        self.window = pl.ds(START, self.high)

    def ordered(self, even, first, second):
        return jnp.where(even, second, first), jnp.where(even, first, second)

    def assemble(self, center, y_first, y_second, edges, pieces):
        rows = self.rows
        for field in range(FIELDS):
            rest = jnp.full((FIRST, LANES), (1.0, 0.0, 0.0, 0.0, 2.5)[field], jnp.float32)
            for tile in range(6):
                target = self.state.at[field, tile]
                if tile in (2, 3):
                    middle = center[field, :, lanes(tile - 2)].astype(jnp.float32)
                else:
                    one = y_first[field, :, lanes(tile % 2)].astype(jnp.float32)
                    two = y_second[field, :, lanes(tile % 2)].astype(jnp.float32)
                    middle = self.ordered(self.even_y, one, two)[tile // 4]
                target[pl.ds(FIRST, rows), :] = middle
                target[pl.ds(0, FIRST), :] = rest
                target[pl.ds(FIRST + rows, FIRST), :] = rest
            place_edges(lambda tile: self.state.at[field, tile + 1], edges, pieces, field, rows)

    def assemble_terms(self, terms, stored, y_first, y_second, edges, pieces):
        rows = self.rows
        none = jnp.zeros((FIRST, LANES), jnp.float32)
        for field in range(FIELDS):
            for tile in (1, 2):
                old = [stored[age, field, :, lanes(tile - 1)].astype(jnp.float32) for age in range(3)]
                for tick, term in enumerate(kept_terms(old)):
                    terms[tick, field, tile, pl.ds(FIRST, rows), :] = term
            for tick in range(2):
                one = y_first[tick * FIELDS + field].astype(jnp.float32)
                two = y_second[tick * FIELDS + field].astype(jnp.float32)
                low, top = self.ordered(self.even_y, one, two)
                terms[tick, field, 0, pl.ds(FIRST, rows), :] = low
                terms[tick, field, 3, pl.ds(FIRST, rows), :] = top
                for tile in range(4):
                    terms[tick, field, tile, pl.ds(0, FIRST), :] = none
                    terms[tick, field, tile, pl.ds(FIRST + rows, FIRST), :] = none
                place_edges(lambda tile: terms.at[tick, field, tile], edges[tick], pieces[tick], field, rows)

    def pointwise(self, state, tile, place, along=True, across=True):
        density, mom_x, mom_y, mom_z, energy = state
        inverse = 1.0 / density
        vel_x = mom_x * inverse
        vel_y = mom_y * inverse
        vel_z = mom_z * inverse
        xx, yy, zz = mom_x * vel_x, mom_y * vel_y, mom_z * vel_z
        moving = xx + yy + zz
        pressure = GAMMA_LESS * energy - (0.5 * GAMMA_LESS) * moving
        enthalpy = energy + pressure
        heat = ((0.25 * DYNAMIC_FRICTION) * moving + (0.5 * CONDUCTIVITY) * pressure) * inverse
        xy = mom_x * vel_y
        xz = mom_x * vel_z
        yz = mom_y * vel_z
        along_x = (mom_x, xx + pressure, xy, xz, enthalpy * vel_x)
        along_y = (mom_y, xy, yy + pressure, yz, enthalpy * vel_y)
        along_z = (mom_z, xz, yz, zz + pressure, enthalpy * vel_z)
        friction = 0.5 * DYNAMIC_FRICTION
        spread = (friction * vel_x, friction * vel_y, friction * vel_z, heat)
        for field in range(FIELDS):
            if along:
                self.flow_x[field, tile - 1, place, :] = along_x[field]
            if field:
                self.slow[field - 1, tile, place, :] = spread[field - 1]
            if across:
                rows = pl.ds(field * self.high, self.high)
                self.flow_y[tile, rows, :] = along_y[field]
                if along:
                    self.flow_z[tile - 1, rows, :] = along_z[field]

    def products(self, tick):
        last = tick == TICKS - 1
        inner = (2, 3) if last else (1, 2, 3, 4)
        for tile in inner:
            parts = [(START, True)] + ([(0, False), (START + self.high, False)] if tick == 0 else [])
            for start, across in parts:
                place = pl.ds(start, self.high if across else START)
                state = [self.state[field, tile, place, :] for field in range(FIELDS)]
                self.pointwise(state, tile, place, across=across)
        outer = {0: (0, 5), TICKS - 1: (1, 4)}.get(tick)
        if outer:
            above = lax.broadcasted_iota(jnp.int32, (self.high, LANES), 1) < LANES // 2
            pairs = [[self.state[field, tile, self.window, :] for tile in outer] for field in range(FIELDS)]
            state = [jnp.where(above, top, low) for low, top in pairs]
            self.pointwise(state, 0, self.window, along=False)
        none = jnp.zeros((self.high, LANES), jnp.float32)

        def flow_y(tile):
            if tile in inner:
                return self.flow_y[tile]
            return self.flow_y[0] if outer else jnp.concatenate([none] * FIELDS)

        def spreading(tile):
            tile = tile if tile in inner else 0
            kinds = range(FIELDS - 1)
            known = tile or outer
            return jnp.concatenate([none] + [self.slow[kind, tile, self.window, :] if known else none for kind in kinds])

        from_above = lax.broadcasted_iota(jnp.int32, (FIELDS * self.high, LANES), 1) < LANES // 2
        flow_z = self.flow_z
        found = {}
        for low, top in ((2, 3),) if last else ((1, 2), (3, 4)):
            if last:
                around = [flow_y(0), spreading(0)]
            else:
                around = [jnp.where(from_above, part(top + 1), part(low - 1)) for part in (flow_y, spreading)]
            parts = [
                flow_y(low),
                flow_y(top),
                flow_z[low - 1],
                flow_z[top - 1],
                spreading(low),
                spreading(top),
                *around,
            ]
            left = jnp.concatenate([part.astype(jnp.bfloat16) for part in parts], axis=1)
            found[low, top] = jnp.dot(left, self.matrix[...], preferred_element_type=jnp.float32)
        return found

    def along_x(self, field, tile):
        def shifted(ref, *index, step):
            return ref[(*index, pl.ds(START + step, self.high))]

        total = shifted(self.flow_x, field, tile - 1, step=-1) - shifted(self.flow_x, field, tile - 1, step=1)
        if field:
            kind = field - 1
            total = total + (shifted(self.slow, kind, tile, step=2) + shifted(self.slow, kind, tile, step=-2))
        return total

    def rates(self, found):
        for group, product in found.items():
            for field in range(FIELDS):
                for side, tile in enumerate(group):
                    start = field * self.high
                    part = product[start : start + self.high, side * LANES : (side + 1) * LANES]
                    yield field, tile, part + self.along_x(field, tile)


def edge_turns(chain, corrected):
    state = ((0, 4, True), (4, 2, False))
    terms = (((0, 2, True), (2, 2, False)), ((0, 2, False),))
    early = [(("state", 0), state)]
    late = []
    for link in range(chain):
        if link:
            late.append((("state", link), state))
        if corrected[link]:
            late.append((("kept", link, 0), terms[0]))
            (late if link else early).append((("kept", link, 1), terms[1]))
    return early, late


def edge_layout(kinds):
    sources = {}
    narrow = []
    row = 0
    for kind, pieces in kinds:
        for distance, count, wide in pieces:
            if wide:
                sources.setdefault(kind, []).append((distance, count, 4, row, 0))
                row += count
            else:
                narrow.append((kind, distance, count))
    for place, (kind, distance, count) in enumerate(narrow):
        sources.setdefault(kind, []).append((distance, count, 2, row + 2 * (place // 2), 2 * (place % 2)))
    return sources, row + 2 * ((len(narrow) + 1) // 2)


def whereabouts():
    def even(axis):
        return lax.axis_index(axis) % 2 == 0 if lax.axis_size(axis) % 2 == 0 else jnp.bool_(True)

    return even("gx"), even("gy"), lax.axis_index("sec") % min(4, lax.axis_size("sec"))


def first_kernel(chain, corrected, rows, *refs):
    matrix, x_first, x_second, center, y_first, y_second, out, edges, *scratch = refs
    even_x, even_y, _ = whereabouts()
    pieces, _ = edge_layout(edge_turns(chain, corrected)[0])
    unpack_edges(edges, x_first, x_second, even_x)
    level = Level(rows, even_x, even_y, matrix, scratch)
    level.assemble(center, y_first, y_second, edges, pieces["state", 0])
    for field, tile, rate in level.rates(level.products(0)):
        out[field, tile - 1] = level.state[field, tile, level.window, :] + (0.5 * TIME_STEP) * rate


def advance_kernel(chain, corrected, rows, *refs):
    matrix, begun, *refs = refs
    came, refs = refs[:4], refs[4:]
    inputs = []
    for link in range(chain):
        state, refs = (refs[:3], refs[3:]) if link else (None, refs)
        stored, refs = (refs[:3], refs[3:]) if corrected[link] else (None, refs)
        inputs.append((state, stored))
    out, fresh, terms, edges, *refs = refs
    even_x, even_y, position = whereabouts()
    levels = [
        Level(rows, even_x, even_y, matrix, refs[5 * link : 5 * link + 5]) for link in range(chain)
    ]
    window = levels[0].window
    layout = {}
    for turn, kinds in enumerate(edge_turns(chain, corrected)):
        pieces, _ = edge_layout(kinds)
        layout.update((kind, (edges.at[turn], parts)) for kind, parts in pieces.items())

    def correction(link, tick, field, tile):
        total = terms[link, tick, field, tile - 1, window, :] + QUAD_WEIGHTS[3] * fresh[link, tick, field, tile - 1]
        for age in range(tick):
            weight = QUAD_WEIGHTS[3 - tick + age] - (1.0 if age == tick - 1 else 0.0)
            total = total + weight * fresh[link, age, field, tile - 1]
        return jnp.where(position > link, total, 0.0) if link else total

    def advance(links):
        def begin(link):
            state, stored = inputs[link]
            if state is not None:
                levels[link].assemble(*state, *layout["state", link])

        def begin_terms(link):
            if corrected[link]:
                places = [layout["kept", link, tick] for tick in range(2)]
                levels[link].assemble_terms(terms.at[link], *inputs[link][1], *zip(*places))

        def update(link, tick, found):
            level = levels[link]
            fix = corrected[link] and links > 1
            if link == 0 and tick == 0:
                for field in range(FIELDS):
                    for tile in range(1, 5):
                        state = begun[field, tile - 1]
                        if fix:
                            state = state + TIME_STEP * correction(0, 0, field, tile)
                        level.state[field, tile, window, :] = state
                return
            for field, tile, rate in level.rates(found):
                if link:
                    fresh[link - 1, tick, field, tile - 1] = (0.5 * rate).astype(jnp.bfloat16).astype(jnp.float32)
                if link + tick >= TICKS:
                    continue
                state = level.state[field, tile, window, :] + (0.5 * TIME_STEP) * rate
                if fix:
                    state = state + TIME_STEP * correction(link, tick, field, tile)
                level.state[field, tile, window, :] = state
                if tick == TICKS - 1:
                    out[field, :, lanes(tile - 2)] = level.state[field, tile, pl.ds(FIRST, rows), :]

        waiting = {}

        def finish(link, tick):
            if (link, tick) in waiting:
                finish(link + 1, tick)
                update(link, tick, waiting.pop((link, tick)))

        if links > 1:
            parts = layout["kept", 0, 1][1]
            used = [first + tile for _, _, tiles, _, first in parts for tile in range(tiles)]
            unpack_edges(edges.at[0], *came[:2], even_x, used)
            unpack_edges(edges.at[1], *came[2:], even_x)
        for tick in range(TICKS):
            for link in reversed(range(min(links, TICKS - tick + 1))):
                if tick == 0:
                    begin(link)
                finish(link, tick - 1)
                waiting[link, tick] = levels[link].products(tick) if link or tick else None
                if tick == 0 and links > 1:
                    begin_terms(link)
        for link, tick in sorted(waiting, reverse=True):
            finish(link, tick)

    if chain == 1:
        advance(1)
    else:
        pl.when(position == 0)(lambda: advance(1))
        pl.when(position > 0)(lambda: advance(chain))


def kept_terms(old):
    first, second, third, _ = QUAD_WEIGHTS
    return (
        first * old[0] + second * old[1] + (third - 1.0) * old[2],
        first * old[1] + second * old[2],
        first * old[2],
    )


def per_device(fields, stored_rates):
    levels = min(4, lax.axis_size("sec"))
    even_x, even_y, _ = whereabouts()
    block = fields[0]
    stored = stored_rates[0]
    rows, columns = block.shape[1:]
    chain = min(levels, TICKS + 1)
    corrected = [link < levels - 1 and link < TICKS for link in range(chain)]
    whole = lax.reduce_precision(block, 8, 22)
    sent = block.astype(jnp.bfloat16)
    whole, sent = lax.optimization_barrier((whole, sent))

    def padded_y(pair, center):
        first, second = pair
        low, top = jnp.where(even_y, second, first), jnp.where(even_y, first, second)
        return jnp.concatenate([low[:, :, -LANES:], center, top[:, :, :LANES]], axis=2)

    own_y = neighbours("gy", even_y, sent, sent)
    centers = [sent] + [from_lower(sent, levels, link) for link in range(1, chain)]
    kept = jnp.concatenate(kept_terms(stored.astype(jnp.float32))[:2], axis=0).astype(jnp.bfloat16)
    kept_y = neighbours("gy", even_y, kept[:, :, :LANES], kept[:, :, -LANES:])
    if chain > 1:
        first, centers = lax.optimization_barrier((own_y[0], centers))
        own_y = first, own_y[1]
    forwarded = [tuple(from_lower(half, levels, link) for half in own_y) for link in range(1, chain)]
    kept_y, forwarded = lax.optimization_barrier((kept_y, forwarded))

    padded = {("state", 0): padded_y(own_y, sent)}
    if corrected[0]:
        padded["kept", 0, 1] = jnp.pad(kept[FIELDS:], ((0, 0), (0, 0), (LANES, LANES)))

    width = columns + 2 * LANES

    def over_x(kinds):
        pieces, _ = edge_layout(kinds)

        def edge(from_top):
            grid = {}
            for kind, parts in pieces.items():
                for distance, count, tiles, row, first_tile in parts:
                    start = rows - distance - count if from_top else distance
                    skip = (4 - tiles) // 2 * LANES
                    grid[row, first_tile] = padded[kind][:, start : start + count, skip : width - skip]
            parts = []
            for row, first_tile in sorted(grid):
                if first_tile:
                    continue
                part = grid[row, 0]
                if part.shape[2] < width:
                    part = jnp.concatenate([part, grid.get((row, 2), part)], axis=2)
                parts.append(part)
            return jnp.concatenate(parts, axis=1)

        return [half.astype(jnp.float32) for half in neighbours("gx", even_x, edge(False), edge(True))]

    early, late = edge_turns(chain, corrected)
    came = over_x(early)
    if chain > 1:
        kept_y, from_far = lax.optimization_barrier((kept_y, [pair[1] for pair in forwarded]))
        forwarded = [(pair[0], far) for pair, far in zip(forwarded, from_far)]
    operands = []
    for link in range(chain):
        if link:
            operands += [centers[link], *forwarded[link - 1]]
            padded["state", link] = padded_y(forwarded[link - 1], centers[link])
        if corrected[link]:
            if link:
                link_kept = from_lower(kept, levels, link)
                link_y = tuple(from_lower(half, levels, link) for half in kept_y)
                operands += [from_lower(stored, levels, link), *link_y]
            else:
                link_kept, link_y = kept, kept_y
                operands += [stored, *link_y]
            link_padded = padded_y(link_y, link_kept)
            padded["kept", link, 0] = link_padded[:FIELDS]
            if link:
                padded["kept", link, 1] = link_padded[FIELDS:]
    came += over_x(late)
    matrix = jnp.asarray(stencil_matrix(), jnp.bfloat16)
    high, tall = rows + WINDOW, rows + 2 * FIRST
    vmem = pl.BlockSpec(memory_space=pltpu.VMEM)
    params = pltpu.CompilerParams(vmem_limit_bytes=48 * 1024 * 1024)
    taken = max(edge_layout(kinds)[1] for kinds in (early, late))
    edges = 2, FIELDS, 4, -(-taken // 8) * 8, LANES
    begun = pl.pallas_call(
        functools.partial(first_kernel, chain, corrected, rows),
        out_shape=jax.ShapeDtypeStruct((FIELDS, 4, high, LANES), jnp.float32),
        in_specs=[vmem] * 6,
        out_specs=vmem,
        scratch_shapes=[pltpu.VMEM(edges, jnp.float32), *scratch_of_level(rows)],
        compiler_params=params,
        cost_estimate=pl.CostEstimate(flops=4 * 10**8, bytes_accessed=10**6, transcendentals=0),
        name="own_first_tick",
    )(matrix, *came[:2], whole, *own_y)
    operands = [begun, *came, *operands]
    result = pl.pallas_call(
        functools.partial(advance_kernel, chain, corrected, rows),
        out_shape=jax.ShapeDtypeStruct((FIELDS, rows, columns), jnp.float32),
        in_specs=[vmem] * (len(operands) + 1),
        out_specs=vmem,
        scratch_shapes=[
            pltpu.VMEM((chain, TICKS, FIELDS, 4, high, LANES), jnp.float32),
            pltpu.VMEM((chain, TICKS, FIELDS, 4, tall, LANES), jnp.float32),
            pltpu.VMEM((2, *edges), jnp.float32),
            *(scratch_of_level(rows) * chain),
        ],
        compiler_params=params,
        cost_estimate=pl.CostEstimate(flops=10**9, bytes_accessed=10**6, transcendentals=0),
        name="advance",
    )(matrix, *operands)
    return result[None]


def solution(mesh):
    return jax.shard_map(
        per_device,
        mesh=mesh,
        in_specs=(P("sec", None, "gx", "gy"), P("sec", None, None, "gx", "gy")),
        out_specs=P("sec", None, "gx", "gy"),
        check_vma=False,
    )
```
